128 devices in a mesh: dp: 4 (over y), expert: 32 (over z, x, core).
Axes of the slice: x: 4, y: 4, z: 4, core: 2. Of those that a mesh axis runs over, the one named last changes fastest.
Arguments:
- inputs: bfloat16 [2, 32, 256, 768], P(None, 'expert', 'dp'), may hold values from -6 to 6
- wqkv: bfloat16 [768, 2304], P(('dp', 'expert')), may hold values from -0.21875 to 0.21875
- wo: bfloat16 [768, 768], P(('dp', 'expert')), may hold values from -0.625 to 0.625
- wr: bfloat16 [768, 64], P(('dp', 'expert')), may hold values from -0.15625 to 0.15625
- gain_one: bfloat16 [768], P(('dp', 'expert')), may hold values from 0.099609375 to 1.8984375
- gain_two: bfloat16 [768], P(('dp', 'expert')), may hold values from 0.099609375 to 1.8984375
- rel_bias: bfloat16 [384], P(('dp', 'expert')), may hold values from -4 to 4
- w_in: bfloat16 [64, 768, 3072], P('expert', None, 'dp'), may hold values from -0.21875 to 0.21875
- w_out: bfloat16 [64, 3072, 768], P('expert', 'dp'), may hold values from -0.109375 to 0.109375
- routes: int32 [2, 32, 256, 2], P(None, 'expert', 'dp'), may hold values from 0 to 63, all different within a row; in each aligned block of 64 rows (0 to 63, 64 to 127, ..., all dimensions but the last counted through in order) at most 3 rows name the same one
- lengths: int32 [2, 32, 3], P(None, 'expert'), may hold values from 1 to 224, 256 in all within a row
- cotangent: bfloat16 [2, 32, 256, 768], P(None, 'expert', 'dp'), may hold values from -6 to 6
Outputs:
- output: bfloat16 [2, 32, 256, 768], P(None, 'expert', 'dp')
- input_grad: float32 [2, 32, 256, 768], P(None, 'expert', 'dp')
- wqkv_grad: float32 [768, 2304], P(('dp', 'expert'))
- wo_grad: float32 [768, 768], P(('dp', 'expert'))
- wr_grad: float32 [768, 64], P(('dp', 'expert'))
- gain_one_grad: float32 [768], P(('dp', 'expert'))
- gain_two_grad: float32 [768], P(('dp', 'expert'))
- rel_bias_grad: float32 [384], P(('dp', 'expert'))
- w_in_grad: float32 [64, 768, 3072], P('expert', None, 'dp')
- w_out_grad: float32 [64, 3072, 768], P('expert', 'dp')
The draws below stay inside these ranges and needn't reach their ends.
Inputs may be any that keep to these rules, and one draw needn't show every extreme that they name: `routes`: each token names two different experts; in the 64 rows of one device in one micro-batch no expert is named more than 3 times, a bound that some block reaches. The 3 lengths of a pack add up to 256.
All inputs are finite; a program needn't handle non-finite values.
Results may differ from the reference program's by a relative error of at most 0.018.
Values may be sent and summed in bfloat16 or wider, within the bound.
No kernel may reach another device: no remote copies, remote signals or barrier semaphores. Data moves between devices by JAX's collectives and lax.ppermute only.
A program may use at most 192 MiB of HBM per device.

```python
import math
import jax
import jax.numpy as jnp
import numpy as np
from jax import lax

D = 768
HEADS = 12
HEAD_DIM = 64
FF = 3072
EXPERTS = 64
BUCKETS = 32
MB = 2
NSEQ = 3
TOK_MB = 64
CAP = 3
SEQ = 256
FAR_STEP = 6
PACKS = 32
N_DP = 4


def with_spikes(drawn, key, source, target, blocks, factor):
    def block_of(axis_at):
        return (jnp.arange(drawn.shape[axis_at]) // (drawn.shape[axis_at] // blocks)).reshape((-1,) + (1,) * (drawn.ndim - 1 - axis_at))

    first = jax.random.permutation(key, blocks)[block_of(target)]
    second = (block_of(target) + blocks // 2) % blocks
    return jnp.where((block_of(source) == first) | (block_of(source) == second), factor * drawn, drawn)


def level_of(key, shape, shards, smallest, top_value):
    level, own = 1.0, jax.random.fold_in(key, 6)
    for dim, shards_of in shards:
        draws = jnp.exp(jax.random.uniform(jax.random.fold_in(own, dim), (shards_of,), jnp.float32, smallest / len(shards), top_value / len(shards)))
        level = level * jnp.repeat(draws, shape[dim] // shards_of).reshape([-1 if axis == dim else 1 for axis in range(len(shape))])
    return level


def profile(amount, total, bound, lean):
    portions = [(1 << 20) // math.isqrt(standing ** lean) + 1 for standing in range(2, amount + 1)]
    surplus, counts = total - bound - (amount - 1), [1] * (amount - 1)
    while surplus > 0:
        free = [i for i in range(amount - 1) if counts[i] < bound]
        pool, budget = sum([portions[i] for i in free]), surplus
        for i in free:
            extra = min(bound - counts[i], max(1, budget * portions[i] // pool), surplus)
            counts[i] = counts[i] + extra
            surplus = surplus - extra
    return np.array([bound] + counts)


def ragged(key, number_of, total, reach, skew):
    if number_of == 2:
        one = jax.random.randint(key, (), max(1, total - reach), min(reach, total - 1) + 1)
        return jnp.stack([one, total - one])
    sizes = jnp.asarray(profile(number_of, total, reach, skew), jnp.int32)
    couples = (number_of - 1) // 2
    source_of, taker = sizes[1:1 + 2 * couples:2], sizes[2:2 + 2 * couples:2]
    slack = jnp.minimum(source_of - 1, reach - taker)
    shifted = jax.random.randint(jax.random.fold_in(key, 1), (couples,), 0, 1 << 20) % (slack + 1)
    sizes = sizes.at[1:1 + 2 * couples:2].set(source_of - shifted).at[2:2 + 2 * couples:2].set(taker + shifted)
    return sizes[jax.random.permutation(jax.random.fold_in(key, 2), number_of)]


def assign_block(stream_key, own, number, rows, number_of, top, limit, lean):
    sequence = jax.random.permutation(stream_key, number_of)
    crowded, common = portions_of(number_of, rows * top, limit, lean, True), portions_of(number_of, rows * top, limit, lean, False)
    places = jnp.arange(number_of)

    def named(tallies, turn):
        used = int((tallies > 0).sum())
        fixed = max(1, used // 4)
        shifted = fixed + (places - fixed + turn * (used - fixed)) % max(1, number_of - fixed)
        return jnp.zeros((number_of,), jnp.int32).at[sequence[jnp.where(places < fixed, places, shifted)]].set(jnp.asarray(tallies, jnp.int32))

    tallies = jnp.where(number % 4 == 0, named(crowded, number // 4), named(common, number - number // 4 - 1))
    mixed = jax.random.permutation(jax.random.fold_in(own, 3), number_of)
    source_of, taker = mixed[0:number_of // 2 * 2:2], mixed[1:number_of // 2 * 2:2]
    room = jnp.minimum(tallies[source_of] - 1, limit - tallies[taker]) // 2
    room = jnp.where((source_of == sequence[0]) | (taker == sequence[0]) | (tallies[taker] == 0), 0, jnp.maximum(room, 0))
    shifted = jax.random.randint(jax.random.fold_in(own, 4), (number_of // 2,), 0, 1 << 20) % (room + 1)
    tallies = tallies.at[source_of].add(-shifted).at[taker].add(shifted)
    labels = jnp.searchsorted(jnp.cumsum(tallies), jnp.arange(rows * top), side="right").astype(jnp.int32)
    listing = labels.reshape(top, rows).T
    listing = listing[jax.random.permutation(jax.random.fold_in(own, 1), rows)]
    turn = jax.random.randint(jax.random.fold_in(own, 2), (rows, 1), 0, top)
    return jnp.take_along_axis(listing, (jnp.arange(top)[None, :] + turn) % top, axis=1)


def portions_of(number_of, total, reach, lean, full):
    weights = [(1 << 20) // math.isqrt(standing ** lean) + 1 for standing in range(1, number_of + 1)]
    largest = reach if full else min(reach, max(-(-total // number_of), total * weights[0] // sum(weights)))
    least = 1 if total - largest >= number_of - 1 else 0
    given, rest = [largest] + [least] * (number_of - 1), total - largest - least * (number_of - 1)
    while rest > 0:
        free = [i for i in range(1, number_of) if given[i] < largest] or [i for i in range(1, number_of) if given[i] < reach]
        whole, left = sum([weights[i] for i in free]), rest
        for i in free:
            extra = min(reach - given[i], max(1, left * weights[i] // whole), rest)
            given[i] = given[i] + extra
            rest = rest - extra
    return np.array(given)


def normal_values(key, shape, scale, limit, cuts=(), held_as=jnp.bfloat16):
    entries = scale * jax.random.normal(key, shape, jnp.float32)
    if cuts:
        entries = entries * level_of(key, shape, cuts, -0.22, 0.18)
    return jnp.clip(entries, -limit, limit).astype(held_as)


def heavy_noise(key, extent, deviation, bound, cuts, heavy, kind=jnp.bfloat16):
    drawn = deviation * jax.random.normal(key, extent, jnp.float32)
    if cuts:
        drawn = drawn * level_of(key, extent, cuts, -0.22, 0.18)
    return jnp.clip(with_spikes(drawn, jax.random.fold_in(key, 3), *heavy), -bound, bound).astype(kind)


def setup_inputs(seed: int = 0) -> dict:
    seeds = jax.random.split(jax.random.key(seed), 13)
    inputs = heavy_noise(seeds[0], (MB, PACKS, SEQ, D), 1.0, 6.0, ((1, 32), (2, 4)), (1, 3, 32, 2.75))
    wqkv = normal_values(seeds[1], (D, 3 * D), D ** -0.5, 0.21875, ((0, 128),))
    wo = normal_values(seeds[2], (D, D), (D // 8) ** -0.5, 0.625, ((0, 128),))
    wr = normal_values(seeds[3], (D, EXPERTS), (2 * D) ** -0.5, 0.15625, ((0, 128),))
    gain_one = jnp.clip(1.0 + 0.18 * jax.random.normal(seeds[4], (D,), jnp.float32), 0.099609375, 1.8984375).astype(jnp.bfloat16)
    gain_two = jnp.clip(1.0 + 0.18 * jax.random.normal(seeds[5], (D,), jnp.float32), 0.099609375, 1.8984375).astype(jnp.bfloat16)
    rel_bias = normal_values(seeds[6], (HEADS * BUCKETS,), 1.0, 4.0, ((0, 128),))
    w_in = normal_values(seeds[7], (EXPERTS, D, FF), D ** -0.5, 0.21875, ((0, 32), (2, 4)))
    w_out = normal_values(seeds[8], (EXPERTS, FF, D), FF ** -0.5, 0.109375, ((0, 32), (1, 4)))
    routes_keys = jax.random.split(jax.random.fold_in(seeds[9], 1), MB * PACKS * SEQ // TOK_MB)
    routes_turns = jax.random.permutation(jax.random.fold_in(seeds[9], 3), MB * PACKS * SEQ // TOK_MB)
    routes = jax.vmap(lambda own, number: assign_block(jax.random.fold_in(seeds[9], 2), own, number, TOK_MB, EXPERTS, 2, CAP, 2))(routes_keys, routes_turns).reshape((MB, PACKS, SEQ, 2))
    lengths = jax.vmap(lambda own: ragged(own, NSEQ, SEQ, SEQ - TOK_MB // 2, 2))(jax.random.split(seeds[10], MB * PACKS)).reshape((MB, PACKS, NSEQ)).astype(jnp.int32)
    cotangent = normal_values(seeds[11], (MB, PACKS, SEQ, D), 1.0, 6.0, ((1, 32), (2, 4)))
    return dict(inputs=inputs, wqkv=wqkv, wo=wo, wr=wr, gain_one=gain_one, gain_two=gain_two, rel_bias=rel_bias, w_in=w_in, w_out=w_out, routes=routes, lengths=lengths, cotangent=cotangent)


exact_mode = lax.Precision.HIGHEST

@jax.custom_vjp
def low(v):
    return lax.optimization_barrier(v.astype(jnp.bfloat16)).astype(jnp.float32)

@jax.custom_vjp
def low_back(v):
    return v

def low_keep(v):
    return (low(v), None)

def low_pass(kept, grad):
    return (grad,)

def back_keep(v):
    return (v, None)

def back_low(kept, grad):
    return (low(grad),)
low.defvjp(low_keep, low_pass)
low_back.defvjp(back_keep, back_low)

def both_ways(value):
    return low(low_back(value))

def rms_scale(values):
    return lax.rsqrt(lax.optimization_barrier(jnp.mean(values * values, axis=-1, keepdims=True)) + 1e-06)

def softmax_last(scores):
    peak = lax.optimization_barrier(jnp.max(scores, axis=-1, keepdims=True))
    weights = jnp.exp(scores - peak)
    return weights / lax.optimization_barrier(jnp.sum(weights, axis=-1, keepdims=True))

def bucket_index(query_places, key_places):
    gap = jnp.maximum(query_places[:, None] - key_places[None, :], 0)
    halfway = BUCKETS // 2
    farther = jnp.minimum(BUCKETS - 1, halfway + (gap - halfway) // FAR_STEP)
    return jnp.where(gap < halfway, gap, farther)

def segment_of(lengths_row, places):
    bounds = jnp.cumsum(lengths_row)[:-1]
    return lax.optimization_barrier(jnp.sum((places[:, None] >= bounds[None, :]).astype(jnp.int32), axis=1))

def slot_numbers(routes_flat):
    marks = (routes_flat[:, None] == jnp.arange(EXPERTS, dtype=jnp.int32)[None, :]).astype(jnp.int32)
    before = jnp.cumsum(marks, axis=0) - marks
    return lax.optimization_barrier(jnp.sum(marks * before, axis=1))

def attend_pack(packed, table):
    queries, keys, values, segment = packed
    length = queries.shape[0]
    places = jnp.arange(length, dtype=jnp.int32)
    query_heads = queries.reshape(length, HEADS, HEAD_DIM)
    key_heads = keys.reshape(length, HEADS, HEAD_DIM)
    value_heads = values.reshape(length, HEADS, HEAD_DIM)
    raw = low_back(jnp.einsum('qhd,khd->hqk', query_heads, key_heads, precision=exact_mode))
    bias = table[:, bucket_index(places, places)]
    allowed = (segment[:, None] == segment[None, :]) & (places[:, None] >= places[None, :])
    scores = jnp.where(allowed[None], raw * (1.0 / math.sqrt(HEAD_DIM)) + bias, -1000000000.0)
    probs = softmax_last(scores)
    mixed = jnp.einsum('hqk,khd->qhd', low(probs), value_heads, precision=exact_mode)
    return mixed.reshape(length, HEADS * HEAD_DIM)

def expert_rows(packed):
    rows, first, second = packed
    raised = low_back(jnp.dot(rows, first, precision=exact_mode))
    active = low(jax.nn.gelu(raised))
    return both_ways(jnp.dot(active, second, precision=exact_mode))

def layer(inputs, wqkv, wo, wr, gain_one, gain_two, rel_bias, w_in, w_out, routes, lengths):
    packs, length, width = inputs.shape
    table = rel_bias.reshape(HEADS, BUCKETS)
    normed = low(inputs * rms_scale(inputs) * gain_one)
    qkv = both_ways(jnp.einsum('psd,de->pse', normed, wqkv, precision=exact_mode))
    queries = qkv[..., :width]
    keys = qkv[..., width:2 * width]
    values = qkv[..., 2 * width:]
    places = jnp.arange(length, dtype=jnp.int32)
    segments = jax.vmap(lambda lengths_row: segment_of(lengths_row, places))(lengths)
    mixed = lax.map(jax.checkpoint(lambda packed: attend_pack(packed, table)), (queries, keys, values, segments))
    mixed = both_ways(mixed)
    branch = low_back(jnp.einsum('psd,de->pse', mixed, wo, precision=exact_mode))
    middle = inputs + branch
    entering = low(middle * rms_scale(middle) * gain_two)
    logits = low_back(jnp.einsum('psd,de->pse', entering, wr, precision=exact_mode))
    picked = (routes[..., None] == jnp.arange(EXPERTS, dtype=jnp.int32)).astype(jnp.float32)
    chosen = jnp.einsum('pske,pse->psk', picked, logits, precision=exact_mode)
    gates = softmax_last(chosen)
    flat_routes = routes.reshape(packs, N_DP, 2 * TOK_MB)
    slots = jax.vmap(jax.vmap(slot_numbers))(flat_routes)
    sources = jnp.arange(N_DP, dtype=jnp.int32)[None, :] * packs + jnp.arange(packs, dtype=jnp.int32)[:, None]
    depth = N_DP * packs * CAP
    where_to = (flat_routes * depth + sources[:, :, None] * CAP + slots).reshape(-1)
    copies = jnp.repeat(entering.reshape(packs, N_DP, TOK_MB, width), 2, axis=2).reshape(-1, width)
    buffer = jnp.zeros((EXPERTS * depth, width), jnp.float32).at[where_to].set(copies)
    results = lax.map(jax.checkpoint(expert_rows), (buffer.reshape(EXPERTS, depth, width), w_in, w_out))
    returned = results.reshape(EXPERTS * depth, width)[where_to].reshape(packs, length, 2, width)
    mixture = jnp.einsum('psk,pskd->psd', gates, returned, precision=exact_mode)
    return middle + mixture

def reference(inputs, wqkv, wo, wr, gain_one, gain_two, rel_bias, w_in, w_out, routes, lengths, cotangent):
    params = (wqkv.astype(jnp.float32), wo.astype(jnp.float32), wr.astype(jnp.float32), gain_one.astype(jnp.float32), gain_two.astype(jnp.float32), rel_bias.astype(jnp.float32), w_in.astype(jnp.float32), w_out.astype(jnp.float32))
    totals = [jnp.zeros_like(param) for param in params]
    outputs = []
    input_grads = []
    for micro_index in range(MB):
        route_now = routes[micro_index]
        length_now = lengths[micro_index]

        def forward(values, qkv_weight, out_weight, router_weight, first_gain, second_gain, bias_table, expert_in, expert_out):
            return layer(values, qkv_weight, out_weight, router_weight, first_gain, second_gain, bias_table, expert_in, expert_out, route_now, length_now)
        result, pull = jax.vjp(forward, inputs[micro_index].astype(jnp.float32), params[0], params[1], params[2], params[3], params[4], params[5], params[6], params[7])
        grads = pull(cotangent[micro_index].astype(jnp.float32))
        outputs.append(result.astype(jnp.bfloat16))
        input_grads.append(grads[0])
        totals = [total + grad for total, grad in zip(totals, grads[1:])]
    return (jnp.stack(outputs), jnp.stack(input_grads), totals[0], totals[1], totals[2], totals[3], totals[4], totals[5], totals[6], totals[7])
```

```python
import math

import jax
import jax.numpy as jnp
from jax import lax
from jax.sharding import Mesh
from jax.sharding import PartitionSpec as P

HEADS = 12
HEAD_DIM = 64
BUCKETS = 32
CAP = 3
FAR_STEP = 6
WIDTH = 768
TOK = 64
MB = 2
NY = 4
NEX = 32
HG = HEADS // NY
EX = ("z", "x", "c")
F32 = jnp.float32
BF = jnp.bfloat16

UP = [(i, (i + 1) % NY) for i in range(NY)]
DOWN = [(i, (i - 1) % NY) for i in range(NY)]
ACROSS = [(i, (i + 2) % NY) for i in range(NY)]


def mm(a, b):
    return lax.dot_general(a, b, (((1,), (0,)), ((), ())), preferred_element_type=F32)


def mm_nt(a, b):
    return lax.dot_general(a, b, (((1,), (1,)), ((), ())), preferred_element_type=F32)


def mm_tn(a, b):
    return lax.dot_general(a, b, (((0,), (0,)), ((), ())), preferred_element_type=F32)


def gather_y(piece):
    below = lax.ppermute(piece, "y", UP)
    above = lax.ppermute(piece, "y", DOWN)
    half = piece.shape[0] // 2
    first = lax.ppermute(below[:half], "y", UP)
    second = lax.ppermute(above[half:], "y", DOWN)
    return piece, below, above, jnp.concatenate([first, second], axis=0)


def scatter_y(own, below, above, across):
    half = own.shape[0] // 2
    first = lax.ppermute(across[:half], "y", UP)
    second = lax.ppermute(across[half:], "y", DOWN)
    up = jnp.concatenate(
        [(above[:half].astype(F32) + first.astype(F32)).astype(BF), above[half:]], axis=0
    )
    down = jnp.concatenate(
        [below[:half], (below[half:].astype(F32) + second.astype(F32)).astype(BF)], axis=0
    )
    from_below = lax.ppermute(up, "y", UP)
    from_above = lax.ppermute(down, "y", DOWN)
    return own.astype(F32) + from_below.astype(F32) + from_above.astype(F32)


def gather_four(piece, axis):
    return [piece] + [lax.ppermute(piece, axis, way) for way in (UP, DOWN, ACROSS)]


def owner_at(step, axis):
    shift = jnp.where(step == 1, 3, jnp.where(step == 2, 1, jnp.where(step == 3, 2, 0)))
    return (lax.axis_index(axis) + shift) % 4


def natural(pieces, place):
    stacked = jnp.stack([pieces[0], pieces[2], pieces[3], pieces[1]])
    return jnp.roll(stacked, place, axis=0)


def relative(stacked, place):
    return tuple(
        lax.dynamic_index_in_dim(stacked, (place + step) % NY, 0, keepdims=False)
        for step in (0, 3, 1, 2)
    )


def rms_scale(values):
    return lax.rsqrt(jnp.mean(values * values, axis=-1, keepdims=True) + 1e-06)


def softmax_last(scores):
    peak = jnp.max(scores, axis=-1, keepdims=True)
    weights = jnp.exp(scores - peak)
    return weights / jnp.sum(weights, axis=-1, keepdims=True)


def body(
    inputs, wqkv, wo, wr, gain_one, gain_two, rel_bias, w_in, w_out, routes, lengths, cotangent
):
    place = lax.axis_index("y")
    span = TOK * NY
    tokens = MB * TOK
    x_own = inputs.reshape(tokens, WIDTH)
    dy_own = cotangent.reshape(tokens, WIDTH)
    cols = wqkv.reshape(6, 3, NY, 192).transpose(2, 0, 1, 3).reshape(NY, 6, 576)
    small = jnp.concatenate(
        [
            wr,
            gain_one[:, None],
            gain_two[:, None],
            jnp.pad(rel_bias, (0, 3))[:, None],
            jnp.zeros((6, 61), BF),
        ],
        axis=1,
    )
    to_y = jnp.concatenate([cols, jnp.broadcast_to(small[None], (NY, 6, 128))], axis=2)
    from_y = lax.all_to_all(to_y, "y", 0, 0).reshape(24, 704)
    pack = jnp.concatenate([from_y, wo.reshape(24, 192)], axis=1)
    packed = jnp.concatenate(gather_four(pack, "x"), axis=0)
    packed = jnp.concatenate(gather_four(packed, "z"), axis=0)
    packed = jnp.concatenate([packed, lax.ppermute(packed, "c", [(0, 1), (1, 0)])], axis=0)
    rows = jnp.arange(WIDTH, dtype=jnp.int32)
    step = rows // 24
    e_row = owner_at(step // 4 % 4, "z") * 8 + owner_at(step % 4, "x") * 2
    e_row = e_row + (lax.axis_index("c") + step // 16) % 2
    in_chunk = rows % 24
    natural_row = ((in_chunk // 6) * NEX + e_row) * 6 + in_chunk % 6
    perm = (rows[:, None] == natural_row[None, :]).astype(BF)
    weights = mm(perm, packed[:, :704]).astype(BF)
    w_heads = weights[:, :576]
    small_all = weights[:, 576:]
    full_router = small_all[:, :64]
    first_gain = small_all[:, 64].astype(F32)
    second_gain = small_all[:, 65].astype(F32)
    wo_row = e_row * 24 + in_chunk
    wo_perm = (rows[:, None] == wo_row[None, :]).astype(BF)
    wo_heads = mm(wo_perm, packed[:, 704:]).astype(BF).reshape(192, WIDTH)
    table = lax.dynamic_slice_in_dim(small_all[:, 66].reshape(NY, 32, 6), place, 1, 0)
    table = table[0, :, :3].reshape(HG, BUCKETS)
    shuffled = (rows // 6 % NEX) * 24 + (rows // (6 * NEX)) * 6 + rows % 6
    grad_perm = (shuffled[:, None] == rows[None, :]).astype(BF)
    route = routes.reshape(MB, 2 * TOK)
    flat = jnp.arange(2 * TOK, dtype=jnp.int32)
    same = (route[:, :, None] == route[:, None, :]) & (flat[:, None] > flat[None, :])[None]
    slot = jnp.sum(same.astype(jnp.int32), axis=2)
    slot = jnp.arange(MB, dtype=jnp.int32)[:, None] * CAP + slot
    slot = slot.reshape(tokens, 2)
    both = route.reshape(tokens, 2)
    side = both % 2
    dest = (both // 2) * 8
    buffer_rows = jnp.arange(256, dtype=jnp.int32)
    pick, spare, spare_low = [], [], []
    for n in range(2):
        here = [side[:, k : k + 1] == n for k in range(2)]
        for kept, at in ((pick, dest + slot), (spare, dest + 6), (spare_low, dest + 7)):
            kept.append(
                [
                    ((buffer_rows[None, :] == at[:, k : k + 1]) & here[k]).astype(BF)
                    for k in range(2)
                ]
            )
    lanes = jnp.arange(WIDTH, dtype=jnp.int32)
    lane_mark = [(lanes[None, :] == slot[:, k : k + 1]) for k in range(2)]
    slots = jnp.arange(192, dtype=jnp.int32)
    buffer_of = (slots // 6) * 8 + slots % 6
    compact = (buffer_of[:, None] == buffer_rows[None, :]).astype(BF)

    def to_experts(buffer):
        return lax.all_to_all(buffer.reshape(NEX, 8, WIDTH), EX, 0, 0).reshape(256, WIDTH)

    x_all = natural(gather_y(x_own), place).reshape(NY, MB, TOK, WIDTH)
    x_all = x_all.transpose(1, 0, 2, 3).reshape(MB * span, WIDTH).astype(F32)
    first_scale = rms_scale(x_all)
    normed = (x_all * first_scale * first_gain).astype(BF)
    qkv = mm(normed, w_heads).astype(BF)
    split = qkv.reshape(MB, span, 3, HG, HEAD_DIM)
    queries, keys, values = split[:, :, 0], split[:, :, 1], split[:, :, 2]
    places = jnp.arange(span, dtype=jnp.int32)
    gap = jnp.maximum(places[:, None] - places[None, :], 0)
    bucket = jnp.where(gap < 16, gap, jnp.minimum(BUCKETS - 1, 16 + (gap - 16) // FAR_STEP))
    marks = (
        bucket.reshape(1, span * span) == jnp.arange(BUCKETS, dtype=jnp.int32)[:, None]
    ).astype(BF)
    bias = mm(table, marks).reshape(1, HG, span, span)
    bounds = jnp.cumsum(lengths.reshape(MB, 3), axis=1)[:, :2]
    segment = jnp.sum((places[None, :, None] >= bounds[:, None, :]).astype(jnp.int32), axis=2)
    allowed = (segment[:, :, None] == segment[:, None, :]) & (
        places[:, None] >= places[None, :]
    )[None]
    scale = 1.0 / math.sqrt(HEAD_DIM)
    raw = jnp.einsum("mqhd,mkhd->mhqk", queries, keys, preferred_element_type=F32)
    scores = jnp.where(allowed[:, None], raw * scale + bias, -1000000000.0)
    probs = softmax_last(scores)
    probs_low = probs.astype(BF)
    mixed = jnp.einsum("mhqk,mkhd->mqhd", probs_low, values, preferred_element_type=F32)
    mixed = mixed.reshape(MB * span, 192).astype(BF)
    branch = mm(mixed, wo_heads).astype(BF)
    dy_later, branch = lax.optimization_barrier((dy_own, branch))
    dy_rows = []
    for n in range(2):
        sent = mm_tn(pick[n][0] + pick[n][1], dy_later).astype(BF)
        dy_rows.append(
            jnp.concatenate(gather_y(mm(compact, to_experts(sent)).astype(BF)), axis=0)
        )

    def by_owner(rows_all):
        ordered = rows_all.reshape(MB, NY, TOK, WIDTH).transpose(1, 0, 2, 3)
        return relative(ordered.reshape(NY, tokens, WIDTH), place)

    x = x_own.astype(F32)
    middle = x + scatter_y(*by_owner(branch))
    second_scale = rms_scale(middle)
    entering = (middle * second_scale * second_gain).astype(BF)
    logits = mm(entering, full_router)
    expert_ids = jnp.arange(64, dtype=jnp.int32)
    routed = [
        (route.reshape(tokens, 2)[:, k : k + 1] == expert_ids[None, :]).astype(F32)
        for k in range(2)
    ]
    chosen = jnp.stack([jnp.sum(mark * logits, axis=1) for mark in routed], axis=1)
    gates = softmax_last(chosen)
    gates_high = gates.astype(BF).astype(F32)
    gates_low = gates - gates_high
    arrived = []
    for n in range(2):
        buffer = mm_tn(pick[n][0] + pick[n][1], entering)
        for k in range(2):
            mark = lane_mark[k].astype(F32)
            high = (mark * gates_high[:, k : k + 1]).astype(BF)
            low = (mark * gates_low[:, k : k + 1]).astype(BF)
            buffer = buffer + mm_tn(spare[n][k], high) + mm_tn(spare_low[n][k], low)
        arrived.append(to_experts(buffer.astype(BF)))
    w_in_of = [w_in[n] for n in range(2)]
    w_out_of = [w_out[n] for n in range(2)]
    rows_all, actives, pulled_of, slopes, d_backs = [], [], [], [], []
    back_lane = (slots % 6)[:, None] == lanes[None, :]
    back_spare = ((slots // 6 * 8 + 6)[:, None] == buffer_rows[None, :]).astype(BF)
    back_spare_low = ((slots // 6 * 8 + 7)[:, None] == buffer_rows[None, :]).astype(BF)

    def home(rows_of):
        return scatter_y(*[rows_of[192 * n : 192 * n + 192] for n in range(4)])

    for n in range(2):
        rows_n = jnp.concatenate(gather_y(mm(compact, arrived[n]).astype(BF)), axis=0)
        pulled = mm_nt(dy_rows[n], w_out_of[n])
        raised = mm(rows_n, w_in_of[n])
        gelu_value, gelu_pull = jax.vjp(jax.nn.gelu, raised)
        active = gelu_value.astype(BF)
        slope = gelu_pull(jnp.ones_like(raised))[0]
        d_raised = slope * pulled
        d_arrived = mm_nt(d_raised.astype(BF), w_in_of[n]).astype(BF)
        d_gate = jnp.sum(active.astype(F32) * pulled, axis=1)
        d_gate_rows = d_gate[:192]
        for i, way in ((1, DOWN), (2, UP), (3, ACROSS)):
            d_gate_rows = d_gate_rows + lax.ppermute(
                d_gate[192 * i : 192 * i + 192], "y", way
            )
        d_gate_rows = d_gate_rows.reshape(192, 1)
        d_gate_high = d_gate_rows.astype(BF).astype(F32)
        d_gate_low = d_gate_rows - d_gate_high
        back = mm_tn(compact, home(d_arrived).astype(BF))
        back = back + mm_tn(back_spare, jnp.where(back_lane, d_gate_high, 0.0).astype(BF))
        back = back + mm_tn(back_spare_low, jnp.where(back_lane, d_gate_low, 0.0).astype(BF))
        d_backs.append(to_experts(back.astype(BF)))
        rows_all.append(rows_n)
        actives.append(active)
        slopes.append(d_raised)
    grads_in, grads_out, returned = [], [], []
    for n in range(2):
        gate_rows = arrived[n].reshape(NEX, 8, WIDTH)[:, 6:8, :6].astype(F32).sum(axis=1)
        gate_all = jnp.concatenate(gather_four(gate_rows.reshape(192), "y"), axis=0)[:, None]
        active_late, d_back_late = lax.optimization_barrier((actives[n], d_backs[1]))
        d_backs[1] = d_back_late
        result = mm(active_late, w_out_of[n]).astype(BF)
        returned.append(to_experts(mm_tn(compact, home(result).astype(BF)).astype(BF)))
        grads_in.append(mm_tn(rows_all[n], (slopes[n] * gate_all).astype(BF)))
        d_returned = (dy_rows[n].astype(F32) * gate_all).astype(BF)
        grads_out.append(mm_tn(actives[n], d_returned))
    grad_in = jnp.stack(grads_in)
    grad_out = jnp.stack(grads_out)
    mixture = sum(
        gates[:, k : k + 1] * (mm(pick[0][k], returned[0]) + mm(pick[1][k], returned[1]))
        for k in range(2)
    )
    output = (middle + mixture).astype(BF)
    d_gates = jnp.stack(
        [
            jnp.sum(
                jnp.where(
                    lane_mark[k],
                    sum(mm(spare[n][k] + spare_low[n][k], d_backs[n]) for n in range(2)),
                    0.0,
                ),
                axis=1,
            )
            for k in range(2)
        ],
        axis=1,
    )
    d_chosen = gates * (d_gates - jnp.sum(gates * d_gates, axis=1, keepdims=True))
    d_logits = sum(d_chosen[:, k : k + 1] * routed[k] for k in range(2)).astype(BF)
    d_entering = sum(
        gates[:, k : k + 1] * (mm(pick[0][k], d_backs[0]) + mm(pick[1][k], d_backs[1]))
        for k in range(2)
    )
    d_entering = d_entering + mm_nt(d_logits, full_router)
    grad_wr = mm_tn(entering, d_logits)
    grad_gain_two = jnp.sum(d_entering * middle * second_scale, axis=0)
    scaled = d_entering * second_gain
    inner = jnp.mean(scaled * middle, axis=1, keepdims=True)
    dy = dy_own.astype(F32)
    d_middle = dy + second_scale * scaled - middle * second_scale**3 * inner
    d_branch = natural(gather_y(d_middle.astype(BF)), place).reshape(NY, MB, TOK, WIDTH)
    d_branch = d_branch.transpose(1, 0, 2, 3).reshape(MB * span, WIDTH)
    grad_wo = mm_tn(mixed, d_branch)
    d_mixed = mm_nt(d_branch, wo_heads).astype(BF).reshape(MB, span, HG, HEAD_DIM)
    d_probs = jnp.einsum("mqhd,mkhd->mhqk", d_mixed, values, preferred_element_type=F32)
    d_values = jnp.einsum("mhqk,mqhd->mkhd", probs_low, d_mixed, preferred_element_type=F32)
    d_scores = probs * (d_probs - jnp.sum(probs * d_probs, axis=-1, keepdims=True))
    d_sum = jnp.sum(d_scores, axis=0).reshape(HG, span * span)
    d_sum_high = d_sum.astype(BF)
    d_sum_low = (d_sum - d_sum_high.astype(F32)).astype(BF)
    grad_table = mm_nt(d_sum_high, marks) + mm_nt(d_sum_low, marks)
    d_raw = (d_scores * scale).astype(BF)
    d_queries = jnp.einsum("mhqk,mkhd->mqhd", d_raw, keys, preferred_element_type=F32)
    d_keys = jnp.einsum("mhqk,mqhd->mkhd", d_raw, queries, preferred_element_type=F32)
    d_qkv = jnp.stack([d_queries, d_keys, d_values], axis=2).reshape(MB * span, 576).astype(BF)
    grad_heads = mm_tn(normed, d_qkv)
    d_normed = mm_nt(d_qkv, w_heads)
    grad_gain_one = jnp.sum(d_normed * x_all * first_scale, axis=0)
    d_normed_own = scatter_y(*by_owner(d_normed.astype(BF)))
    scale_own = rms_scale(x)
    scaled_one = d_normed_own * first_gain
    inner_one = jnp.mean(scaled_one * x, axis=1, keepdims=True)
    input_grad = d_middle + scale_own * scaled_one - x * scale_own**3 * inner_one
    table_column = jnp.pad(grad_table.reshape(1, 32, 3), ((0, 0), (0, 0), (0, 3)))
    table_column = (
        jnp.where((jnp.arange(NY) == place)[:, None, None], table_column, 0.0)
    ).reshape(WIDTH, 1)
    grad_small = jnp.concatenate(
        [
            grad_wr,
            grad_gain_one[:, None],
            grad_gain_two[:, None],
            table_column,
            jnp.zeros((WIDTH, 61), F32),
        ],
        axis=1,
    )
    grad_pack = mm_tn(grad_perm, jnp.concatenate([grad_heads, grad_small], axis=1).astype(BF))
    grad_pack = jnp.concatenate(
        [grad_pack.astype(BF), grad_wo.astype(BF).reshape(WIDTH, 192)], axis=1
    )
    terms = lax.all_to_all(grad_pack.reshape(NEX, 24, 896), EX, 0, 0)
    summed = jnp.sum(terms.astype(F32), axis=0)
    wo_out = summed[:, 704:].reshape(6, WIDTH)
    mine = lax.all_to_all(summed[:, :704].reshape(NY, 6, 704), "y", 0, 0)
    wqkv_out = mine[:, :, :576].reshape(NY, 6, 3, 192).transpose(1, 2, 0, 3).reshape(6, 2304)
    small_out = jnp.sum(mine[:, :, 576:], axis=0)
    return (
        output.reshape(MB, 1, TOK, WIDTH),
        input_grad.reshape(MB, 1, TOK, WIDTH),
        wqkv_out,
        wo_out,
        small_out[:, :64],
        small_out[:, 64],
        small_out[:, 65],
        small_out[:3, 66],
        grad_in,
        grad_out,
    )


def solution(mesh):
    grid = Mesh(mesh.devices.reshape(NY, 4, 4, 2), ("y", "z", "x", "c"))
    every = ("y",) + EX
    in_specs = (
        P(None, EX, "y", None),
        P(every, None),
        P(every, None),
        P(every, None),
        P(every),
        P(every),
        P(every),
        P(EX, None, "y"),
        P(EX, "y", None),
        P(None, EX, "y", None),
        P(None, EX, None),
        P(None, EX, "y", None),
    )
    out_specs = (
        P(None, EX, "y", None),
        P(None, EX, "y", None),
        P(every, None),
        P(every, None),
        P(every, None),
        P(every),
        P(every),
        P(every),
        P(EX, None, "y"),
        P(EX, "y", None),
    )
    return jax.shard_map(body, mesh=grid, in_specs=in_specs, out_specs=out_specs, check_vma=False)
```

```python
import math

import jax
import jax.numpy as jnp
from jax import lax
from jax.experimental import pallas as pl
from jax.experimental.pallas import tpu as pltpu
from jax.sharding import Mesh
from jax.sharding import PartitionSpec as P

HEADS = 12
HEAD_DIM = 64
BUCKETS = 32
CAP = 3
FAR_STEP = 6
WIDTH = 768
TOK = 64
MB = 2
NY = 4
NEX = 32
HG = HEADS // NY
SPAN = TOK * NY
SCORE_SCALE = 1.0 / math.sqrt(HEAD_DIM)
EX = ("z", "x", "c")
F32 = jnp.float32
BF = jnp.bfloat16
GELU_IN = math.sqrt(2.0 / math.pi)
GELU_CUBE = 0.044715

UP = [(i, (i + 1) % NY) for i in range(NY)]
DOWN = [(i, (i - 1) % NY) for i in range(NY)]
ACROSS = [(i, (i + 2) % NY) for i in range(NY)]


def dot(a, b, dims):
    return lax.dot_general(a, b, ((dims[:1], dims[1:]), ((), ())), preferred_element_type=F32)


def iota(shape, dim):
    return lax.broadcasted_iota(jnp.int32, shape, dim)


def bucket_of(gap):
    far = 16 + (jnp.maximum(gap - 16, 0) * 171) // 1024
    return jnp.where(gap < 16, gap, jnp.minimum(BUCKETS - 1, far))


def table_marks(place, head):
    shape = (WIDTH, SPAN)
    row = iota(shape, 0)
    owner = row // 6
    entry = 3 * (owner - NEX * place) + row - 6 * owner
    wanted = head * BUCKETS + bucket_of(iota(shape, 1))
    return jnp.where((row - 6 * owner < 3) & (entry == wanted), 1.0, 0.0).astype(BF)


def place_rows(pieces, place, target):
    for step, piece in zip((0, 3, 1, 2), pieces):
        start = lax.rem(place + step, NY) * TOK
        for m in range(MB):
            target[pl.ds(pl.multiple_of(m * SPAN + start, TOK), TOK), :] = piece[
                m * TOK : (m + 1) * TOK, :
            ]


def take_rows(pieces, place, source):
    for step, piece in zip((0, 3, 1, 2), pieces):
        start = lax.rem(place + step, NY) * TOK
        for m in range(MB):
            piece[m * TOK : (m + 1) * TOK, :] = source[
                pl.ds(pl.multiple_of(m * SPAN + start, TOK), TOK), :
            ].astype(piece.dtype)


def forward_kernel(
    scalars, nat_row, wo_row, x0, x1, x2, x3, packed,
    b0, b1, b2, b3, qkv, probs, mixed, weights, wo_heads, normed, x_all, rows, bias, branch,
):
    place = scalars[0]
    place_rows((x0, x1, x2, x3), place, x_all)
    row = iota((WIDTH, WIDTH), 0)
    perm = jnp.where(row == nat_row[0:1, :], 1.0, 0.0).astype(BF)
    weights[...] = dot(perm, packed[:, :704], (1, 0)).astype(BF)
    for part in range(4):
        choose = jnp.where(iota((192, WIDTH), 0) * 4 + part == wo_row[0:1, :], 1.0, 0.0).astype(BF)
        wo_heads[:, part * 192 : part * 192 + 192] = dot(
            choose, packed[:, 704:896], (1, 0)
        ).astype(BF)
    lane_of = jnp.where(iota((8, 128), 1) == iota((8, 128), 0) + 64, 1.0, 0.0).astype(BF)
    rows[...] = dot(lane_of, weights[:, 576:704], (1, 1))
    values = x_all[...].astype(F32)
    scale = lax.rsqrt(jnp.mean(values * values, axis=1, keepdims=True) + 1e-06)
    normed[...] = (values * scale * rows[0:1, :]).astype(BF)
    qkv[...] = dot(normed[...], weights[:, :576], (1, 0)).astype(BF)
    table = rows[...].astype(BF)
    for head in range(HG):
        mirrored = dot(table, table_marks(place, head), (1, 0))[2:3, :]
        flip = jnp.where(iota((SPAN, SPAN), 0) + iota((SPAN, SPAN), 1) == SPAN - 1, 1.0, 0.0)
        mirrored = dot(jnp.broadcast_to(mirrored, (8, SPAN)).astype(BF), flip.astype(BF), (1, 0))
        spread = jnp.broadcast_to(mirrored[0:1, :], (SPAN, SPAN))
        bias[head] = pltpu.roll(spread, 1, 1, stride=1, stride_axis=0)
    query = iota((SPAN, SPAN), 0)
    key = iota((SPAN, SPAN), 1)
    for m in range(MB):
        first = scalars[1 + 2 * m]
        second = scalars[2 + 2 * m]
        of_query = jnp.where(query >= first, 1, 0) + jnp.where(query >= second, 1, 0)
        of_key = jnp.where(key >= first, 1, 0) + jnp.where(key >= second, 1, 0)
        seen = (of_query == of_key) & (query >= key)
        part = slice(m * SPAN, (m + 1) * SPAN)
        for head in range(HG):
            at = head * HEAD_DIM
            raw = dot(
                qkv[part, at : at + HEAD_DIM], qkv[part, 192 + at : 192 + at + HEAD_DIM], (1, 1)
            )
            scores = jnp.where(seen, raw * SCORE_SCALE + bias[head], -1000000000.0)
            peak = jnp.max(scores, axis=1, keepdims=True)
            powers = jnp.exp(scores - peak)
            share = powers / jnp.sum(powers, axis=1, keepdims=True)
            probs[m * HG + head] = share
            mixed[part, at : at + HEAD_DIM] = dot(
                share.astype(BF), qkv[part, 384 + at : 384 + at + HEAD_DIM], (1, 0)
            ).astype(BF)
    branch[...] = dot(mixed[...], wo_heads[...], (1, 0))
    take_rows((b0, b1, b2, b3), place, branch)


def backward_kernel(
    scalars, d0, d1, d2, d3, qkv, probs, mixed, weights, wo_heads, normed, x_all, wr_grad, gain_two,
    n0, n1, n2, n3, grads, d_branch, d_mixed, d_qkv, d_normed, d_bias,
):
    place = scalars[0]
    place_rows((d0, d1, d2, d3), place, d_branch)
    grad_wo = dot(mixed[...], d_branch[...], (0, 0)).astype(BF)
    packed_wo = jnp.zeros((WIDTH, 192), F32)
    for part in range(4):
        choose = jnp.where(iota((WIDTH, 192), 1) * 4 + part == iota((WIDTH, 192), 0), 1.0, 0.0)
        packed_wo = packed_wo + dot(
            choose.astype(BF), grad_wo[:, part * 192 : part * 192 + 192], (1, 0)
        )
    grads[:, 704:896] = packed_wo.astype(BF)
    d_mixed[...] = dot(d_branch[...], wo_heads[...], (1, 1)).astype(BF)
    for m in range(MB):
        part = slice(m * SPAN, (m + 1) * SPAN)
        for head in range(HG):
            at = head * HEAD_DIM
            lanes = slice(at, at + HEAD_DIM)
            share = probs[m * HG + head]
            d_mixed_head = d_mixed[part, lanes]
            d_probs = dot(d_mixed_head, qkv[part, 384 + at : 384 + at + HEAD_DIM], (1, 1))
            d_qkv[part, 384 + at : 384 + at + HEAD_DIM] = dot(
                share.astype(BF), d_mixed_head, (0, 0)
            ).astype(BF)
            inner = jnp.sum(share * d_probs, axis=1, keepdims=True)
            d_scores = share * (d_probs - inner)
            if m == 0:
                d_bias[head] = d_scores
            else:
                d_bias[head] = d_bias[head] + d_scores
            d_raw = (d_scores * SCORE_SCALE).astype(BF)
            d_qkv[part, lanes] = dot(
                d_raw, qkv[part, 192 + at : 192 + at + HEAD_DIM], (1, 0)
            ).astype(BF)
            d_qkv[part, 192 + at : 192 + at + HEAD_DIM] = dot(
                d_raw, qkv[part, lanes], (0, 0)
            ).astype(BF)
    d_normed[...] = dot(d_qkv[...], weights[:, :576], (1, 1))
    take_rows((n0, n1, n2, n3), place, d_normed)
    values = x_all[...].astype(F32)
    scale = lax.rsqrt(jnp.mean(values * values, axis=1, keepdims=True) + 1e-06)
    gain_one = jnp.sum(d_normed[...] * values * scale, axis=0, keepdims=True)
    flip = jnp.where(iota((SPAN, SPAN), 0) + iota((SPAN, SPAN), 1) == SPAN - 1, 1.0, 0.0).astype(BF)
    table = jnp.zeros((8, WIDTH), F32)
    for head in range(HG):
        total = d_bias[head]
        high = total.astype(BF)
        low = (total - high.astype(F32)).astype(BF)
        turned = dot(flip, high, (1, 0)) + dot(flip, low, (1, 0))
        skewed = pltpu.roll(turned, 0, 1, stride=1, stride_axis=0)
        diagonal = jnp.broadcast_to(jnp.sum(skewed, axis=0, keepdims=True), (8, SPAN))
        high = diagonal.astype(BF)
        low = (diagonal - high.astype(F32)).astype(BF)
        by_gap = dot(high, flip, (1, 0)) + dot(low, flip, (1, 0))
        marks = table_marks(place, head)
        high = by_gap.astype(BF)
        low = (by_gap - high.astype(F32)).astype(BF)
        table = table + dot(high, marks, (1, 1)) + dot(low, marks, (1, 1))
    which = iota((8, WIDTH), 0)
    rows = jnp.where(
        which == 0, gain_one, jnp.where(which == 1, gain_two[0:1, :], jnp.where(which == 2, table, 0.0))
    )
    lane_of = jnp.where(iota((8, 128), 1) == iota((8, 128), 0) + 64, 1.0, 0.0).astype(BF)
    small = wr_grad[...] + dot(rows.astype(BF), lane_of, (0, 0))
    row = iota((WIDTH, WIDTH), 0)
    col = iota((WIDTH, WIDTH), 1)
    chunk = row // 24
    rest = row - 24 * chunk
    group = rest // 6
    wanted = (group * NEX + chunk) * 6 + rest - 6 * group
    perm = jnp.where(col == wanted, 1.0, 0.0).astype(BF)
    grad_heads = dot(normed[...], d_qkv[...], (0, 0)).astype(BF)
    grads[:, :576] = dot(perm, grad_heads, (1, 0)).astype(BF)
    grads[:, 576:704] = dot(perm, small.astype(BF), (1, 0)).astype(BF)


def vmem_call(kernel, outs, scratch, *args):
    full = pl.BlockSpec(memory_space=pltpu.VMEM)
    return pl.pallas_call(
        kernel,
        out_shape=[jax.ShapeDtypeStruct(shape, kind) for shape, kind in outs],
        in_specs=[pl.BlockSpec(memory_space=pltpu.SMEM)] + [full] * (len(args) - 1),
        out_specs=[full] * len(outs),
        scratch_shapes=[pltpu.VMEM(shape, kind) for shape, kind in scratch],
        compiler_params=pltpu.CompilerParams(vmem_limit_bytes=50 * 1024 * 1024),
    )(*args)


def attention_forward(scalars, nat_row, wo_row, x_pieces, packed):
    rows = MB * SPAN
    outs = [((128, WIDTH), BF)] * 4 + [
        ((rows, 576), BF),
        ((MB * HG, SPAN, SPAN), F32),
        ((rows, 192), BF),
        ((WIDTH, 704), BF),
        ((192, WIDTH), BF),
        ((rows, WIDTH), BF),
        ((rows, WIDTH), BF),
        ((8, WIDTH), F32),
    ]
    scratch = [((HG, SPAN, SPAN), F32), ((rows, WIDTH), F32)]
    return vmem_call(forward_kernel, outs, scratch, scalars, nat_row, wo_row, *x_pieces, packed)


def attention_backward(scalars, d_pieces, kept, wr_grad, gain_two):
    rows = MB * SPAN
    outs = [((128, WIDTH), BF)] * 4 + [((WIDTH, 896), BF)]
    scratch = [
        ((rows, WIDTH), BF),
        ((rows, 192), BF),
        ((rows, 576), BF),
        ((rows, WIDTH), F32),
        ((HG, SPAN, SPAN), F32),
    ]
    return vmem_call(backward_kernel, outs, scratch, scalars, *d_pieces, *kept, wr_grad, gain_two)


def middle_kernel(
    scalars, b0, b1, b2, b3, x_own, rows, weights, info, middle, entering, gates, buffer
):
    values = x_own[...].astype(F32) + (
        (b0[...].astype(F32) + b1[...].astype(F32)) + (b2[...].astype(F32) + b3[...].astype(F32))
    )
    middle[...] = values
    scale = lax.rsqrt(jnp.mean(values * values, axis=1, keepdims=True) + 1e-06)
    low = (values * scale * rows[1:2, :]).astype(BF)
    entering[...] = low
    logits = dot(low, weights[:, 576:704], (1, 0))
    lane = iota((128, 128), 1)
    chosen = [
        jnp.sum(jnp.where(lane == info[:, 6 + k : 7 + k], logits, 0.0), axis=1, keepdims=True)
        for k in range(2)
    ]
    peak = jnp.maximum(chosen[0], chosen[1])
    powers = [jnp.exp(value - peak) for value in chosen]
    total = powers[0] + powers[1]
    share = [power / total for power in powers]
    gates[...] = jnp.where(lane == 0, share[0], jnp.where(lane == 1, share[1], 0.0))
    place = iota((128, 512), 1)
    wide = iota((128, WIDTH), 1)
    pick = jnp.where(
        (place == info[:, 0:1]) | (place == info[:, 1:2]), 1.0, 0.0
    ).astype(BF)
    sent = dot(pick, low, (0, 0))
    for k in range(2):
        mark = wide == info[:, 4 + k : 5 + k]
        high = share[k].astype(BF).astype(F32)
        rest = share[k] - high
        for at, value in ((0, high), (1, rest)):
            spot = jnp.where(place == info[:, 2 + k : 3 + k] + at, 1.0, 0.0).astype(BF)
            sent = sent + dot(spot, jnp.where(mark, value, 0.0).astype(BF), (0, 0))
    buffer[...] = sent.astype(BF)


def return_kernel(
    scalars, back, info, gates, entering, middle, rows, weights, dy_own,
    d_middle, d_branch, wr_grad, gain_two,
):
    place = iota((128, 512), 1)
    wide = iota((128, WIDTH), 1)
    lane = iota((128, 128), 1)
    share = [gates[:, k : k + 1] for k in range(2)]
    d_entering = jnp.zeros((128, WIDTH), F32)
    d_gates = []
    for k in range(2):
        pick = jnp.where(place == info[:, k : k + 1], 1.0, 0.0).astype(BF)
        d_entering = d_entering + share[k] * dot(pick, back[...], (1, 0))
        at = info[:, 2 + k : 3 + k]
        spot = jnp.where((place == at) | (place == at + 1), 1.0, 0.0).astype(BF)
        d_gates.append(
            jnp.sum(
                jnp.where(wide == info[:, 4 + k : 5 + k], dot(spot, back[...], (1, 0)), 0.0),
                axis=1,
                keepdims=True,
            )
        )
    inner = share[0] * d_gates[0] + share[1] * d_gates[1]
    d_logits = jnp.zeros((128, 128), F32)
    for k in range(2):
        d_logits = d_logits + jnp.where(
            lane == info[:, 6 + k : 7 + k], share[k] * (d_gates[k] - inner), 0.0
        )
    d_logits = d_logits.astype(BF)
    d_entering = d_entering + dot(d_logits, weights[:, 576:704], (1, 1))
    wr_grad[...] = dot(entering[...], d_logits, (0, 0))
    values = middle[...]
    scale = lax.rsqrt(jnp.mean(values * values, axis=1, keepdims=True) + 1e-06)
    gain_two[...] = jnp.broadcast_to(
        jnp.sum(d_entering * values * scale, axis=0, keepdims=True), (8, WIDTH)
    )
    scaled = d_entering * rows[1:2, :]
    mean = jnp.mean(scaled * values, axis=1, keepdims=True)
    total = dy_own[...].astype(F32) + scale * scaled - values * scale * scale * scale * mean
    d_middle[...] = total
    d_branch[...] = total.astype(BF)


def gelu_parts(value):
    inner = GELU_IN * (value + GELU_CUBE * value * value * value)
    bend = jnp.tanh(inner)
    half = 0.5 * (1.0 + bend)
    slope = half + 0.5 * value * (1.0 - bend * bend) * GELU_IN * (
        1.0 + 3.0 * GELU_CUBE * value * value
    )
    return value * half, slope


def expert_kernel(
    scalars, p0, p1, p2, p3a, p3b, dy_rows, w_in, w_out,
    o0, o1, o2, o3, rows_all, active_all, d_raised_all, d_returned_all,
):
    place = scalars[0]
    tall = NEX * 6
    ones = jnp.ones((8, WIDTH), BF)
    extra_row = iota((16, tall), 0)
    eye = iota((tall, tall), 0) == iota((tall, tall), 1)
    for step, out in zip((0, 3, 1, 2), (o0, o1, o2, o3)):
        spot = (0, 3, 1, 2).index(step)
        owner = lax.rem(place + step, NY)
        out[384:400, 384:WIDTH] = jnp.zeros((16, WIDTH - 384), BF)
        for n in range(2):
            if step == 2:
                rows = p3a[0:tall, :] if n == 0 else jnp.concatenate(
                    [p3a[tall : tall + 16, :], p3b[0 : tall - 16, :]], axis=0
                )
                gate = p3b[tall - 16 : tall, n * tall : n * tall + tall]
            else:
                source = {0: p0, 3: p1, 1: p2}[step]
                rows = source[n * tall : n * tall + tall, :]
                gate = source[384:400, n * tall : n * tall + tall]
            here = slice(spot * tall, spot * tall + tall)
            gate_row = gate.astype(F32)[0:1, :]
            gate_low = gate.astype(F32)[1:2, :]
            wide_ones = jnp.ones((tall, 128), BF)
            gate_col = dot(jnp.where(eye, gate_row, 0.0).astype(BF), wide_ones, (1, 0)) + dot(
                jnp.where(eye, gate_low, 0.0).astype(BF), wide_ones, (1, 0)
            )
            gate_col = gate_col[:, 0:1]
            dy = dy_rows[owner, n * tall : n * tall + tall, :]
            rows_all[n, here, :] = rows
            raised = dot(rows, w_in[n], (1, 0))
            pulled = dot(dy, w_out[n], (1, 1))
            active, slope = gelu_parts(raised)
            active = active.astype(BF)
            active_all[n, here, :] = active
            d_raised = slope * pulled
            out[n * tall : n * tall + tall, :] = dot(d_raised.astype(BF), w_in[n], (1, 1)).astype(BF)
            product = active.astype(F32) * pulled
            high = product.astype(BF)
            low = (product - high.astype(F32)).astype(BF)
            d_gate = dot(ones, high, (1, 1)) + dot(ones, low, (1, 1))
            out[384:400, n * tall : n * tall + tall] = jnp.where(
                extra_row == 0, d_gate[0:1, :], 0.0
            ).astype(BF)
            d_raised_all[n, here, :] = (d_raised * gate_col).astype(BF)
            d_returned_all[n, here, :] = (dy.astype(F32) * gate_col).astype(BF)


def expert_rows(scalars, pieces, dy_rows, w_in, w_out):
    square = ((2, WIDTH, WIDTH), BF)
    outs = [((400, WIDTH), BF)] * 4 + [square] * 4
    return vmem_call(expert_kernel, outs, [], scalars, *pieces, dy_rows, w_in, w_out)


def middle_step(scalars, pieces, x_own, rows, weights, info):
    outs = [((128, WIDTH), F32), ((128, WIDTH), BF), ((128, 128), F32), ((512, WIDTH), BF)]
    return vmem_call(middle_kernel, outs, [], scalars, *pieces, x_own, rows, weights, info)


def return_step(scalars, back, info, gates, entering, middle, rows, weights, dy_own):
    outs = [((128, WIDTH), F32), ((128, WIDTH), BF), ((WIDTH, 128), F32), ((8, WIDTH), F32)]
    return vmem_call(
        return_kernel, outs, [], scalars, back, info, gates, entering, middle, rows, weights, dy_own
    )


def gather_four(piece, axis):
    return [piece] + [lax.ppermute(piece, axis, way) for way in (UP, DOWN, ACROSS)]


def owner_at(step, axis):
    shift = jnp.where(step == 1, 3, jnp.where(step == 2, 1, jnp.where(step == 3, 2, 0)))
    return (lax.axis_index(axis) + shift) % 4


def exchange_y(pieces):
    ways = (DOWN, UP, ACROSS)
    return [pieces[0]] + [lax.ppermute(piece, "y", way) for piece, way in zip(pieces[1:], ways)]


def ring_gather(piece, cut):
    below = lax.ppermute(piece, "y", UP)
    above = lax.ppermute(piece, "y", DOWN)
    first = lax.ppermute(below[:cut], "y", UP)
    second = lax.ppermute(above[cut:], "y", DOWN)
    return piece, below, above, first, second


def ring_scatter(pieces, cut):
    own, below, above, across = pieces
    first = lax.ppermute(across[:cut], "y", UP)
    second = lax.ppermute(across[cut:], "y", DOWN)
    up = jnp.concatenate(
        [(above[:cut].astype(F32) + first.astype(F32)).astype(BF), above[cut:]], axis=0
    )
    down = jnp.concatenate(
        [below[:cut], (below[cut:].astype(F32) + second.astype(F32)).astype(BF)], axis=0
    )
    from_below = lax.ppermute(up, "y", UP)
    from_above = lax.ppermute(down, "y", DOWN)
    return own.astype(F32) + from_below.astype(F32) + from_above.astype(F32)


def mm(a, b):
    return lax.dot_general(a, b, (((1,), (0,)), ((), ())), preferred_element_type=F32)


def mm_tn(a, b):
    return lax.dot_general(a, b, (((0,), (0,)), ((), ())), preferred_element_type=F32)


def body(
    inputs, wqkv, wo, wr, gain_one, gain_two, rel_bias, w_in, w_out, routes, lengths, cotangent
):
    place = lax.axis_index("y")
    tokens = MB * TOK
    x_own = inputs.reshape(tokens, WIDTH)
    dy_own = cotangent.reshape(tokens, WIDTH)
    cols = wqkv.reshape(6, 3, NY, 192).transpose(2, 0, 1, 3).reshape(NY, 6, 576)
    small = jnp.concatenate(
        [
            wr,
            gain_one[:, None],
            gain_two[:, None],
            jnp.pad(rel_bias, (0, 3))[:, None],
            jnp.zeros((6, 61), BF),
        ],
        axis=1,
    )
    to_y = jnp.concatenate([cols, jnp.broadcast_to(small[None], (NY, 6, 128))], axis=2)
    from_y = lax.all_to_all(to_y, "y", 0, 0).reshape(24, 704)
    pack = jnp.concatenate([from_y, wo.reshape(24, 192)], axis=1)
    packed = jnp.concatenate(gather_four(pack, "x"), axis=0)
    packed = jnp.concatenate(gather_four(packed, "z"), axis=0)
    packed = jnp.concatenate([packed, lax.ppermute(packed, "c", [(0, 1), (1, 0)])], axis=0)
    x_pieces = gather_four(x_own, "y")
    rows = jnp.arange(WIDTH, dtype=jnp.int32)
    step = rows // 24
    owner = owner_at(step // 4 % 4, "z") * 8 + owner_at(step % 4, "x") * 2
    owner = owner + (lax.axis_index("c") + step // 16) % 2
    in_chunk = rows % 24
    nat_row = jnp.broadcast_to((((in_chunk // 6) * NEX + owner) * 6 + in_chunk % 6)[None], (8, WIDTH))
    wo_row = jnp.broadcast_to((owner * 24 + in_chunk)[None], (8, WIDTH))
    bounds = jnp.cumsum(lengths.reshape(MB, 3), axis=1)[:, :2].reshape(4)
    scalars = jnp.concatenate([place[None].astype(jnp.int32), bounds])
    route = routes.reshape(MB, 2 * TOK)
    flat = jnp.arange(2 * TOK, dtype=jnp.int32)
    same = (route[:, :, None] == route[:, None, :]) & (flat[:, None] > flat[None, :])[None]
    slot = jnp.sum(same.astype(jnp.int32), axis=2)
    slot = (slot + jnp.arange(MB, dtype=jnp.int32)[:, None] * CAP).reshape(tokens, 2)
    route = route.reshape(tokens, 2)
    side = route % 2
    dest = (route // 2) * 16
    me = lax.axis_index(EX)
    info = jnp.concatenate(
        [dest + side * 6 + slot, dest + 12, side * 192 + me * 6 + slot, route], axis=1
    )
    buffer_rows = jnp.arange(512, dtype=jnp.int32)
    pick = [(buffer_rows[None, :] == info[:, k : k + 1]).astype(BF) for k in range(2)]
    slots = jnp.arange(400, dtype=jnp.int32)
    buffer_of = (slots // 6 % NEX) * 16 + (slots // 192) * 6 + slots % 6
    compact = jnp.where(
        slots[:, None] < 384,
        buffer_of[:, None] == buffer_rows[None, :],
        (buffer_rows % 16)[None, :] == 12 + slots[:, None] - 384,
    )
    compact = (compact & (slots < 386)[:, None]).astype(BF)

    def to_experts(buffer):
        return lax.all_to_all(buffer.reshape(NEX, 16, WIDTH), EX, 0, 0).reshape(512, WIDTH)

    kept = attention_forward(scalars, nat_row, wo_row, x_pieces, packed)
    branch, saved, gain_rows = kept[:4], kept[4:11], kept[11]
    weights = saved[3]
    dy_later, branch_own = lax.optimization_barrier((dy_own, branch[0]))
    dy_rows = mm(compact[:384], to_experts(mm_tn(pick[0] + pick[1], dy_later).astype(BF)))
    dy_rows = lax.all_gather(dy_rows.astype(BF), "y")
    middle, entering, gates, buffer = middle_step(
        scalars, exchange_y([branch_own] + list(branch[1:])), x_own, gain_rows, weights, info
    )
    arrived = mm(compact, to_experts(buffer)).astype(BF)
    results = expert_rows(scalars, ring_gather(arrived, 208), dy_rows, w_in, w_out)
    d_arrived, (rows_all, active, d_raised, d_returned) = results[:4], results[4:]
    d_home = ring_scatter(d_arrived, 208)
    d_home_high = d_home.astype(BF)
    d_home_low = (d_home[384:385] - d_home_high[384:385].astype(F32)).astype(BF)
    d_home = jnp.where(
        (slots == 385)[:, None], d_home_low, d_home_high
    )
    back = to_experts(mm_tn(compact, d_home).astype(BF))
    result = jnp.einsum("erf,efd->erd", active, w_out, preferred_element_type=F32).astype(BF)
    result = result.reshape(2, NY, 192, WIDTH)
    order = (0, 2, 3, 1)
    result = jnp.roll(jnp.stack([result[:, n] for n in order]), place, axis=0)
    result = lax.psum_scatter(result.reshape(NY, 384, WIDTH), "y", scatter_dimension=0)
    d_middle, d_branch, wr_grad, gain_two_grad = return_step(
        scalars, back, info, gates, entering, middle, gain_rows, weights, dy_own
    )
    result, d_branch = lax.optimization_barrier((result, d_branch))
    returned = to_experts(mm_tn(compact[:384], result).astype(BF))
    grad_in = jnp.einsum("erd,erf->edf", rows_all, d_raised, preferred_element_type=F32)
    grad_out = jnp.einsum("erf,erd->efd", active, d_returned, preferred_element_type=F32)
    mixture = sum(gates[:, k : k + 1] * mm(pick[k], returned) for k in range(2))
    output = (middle + mixture).astype(BF)
    ended = attention_backward(
        scalars, gather_four(d_branch, "y"), saved, wr_grad, gain_two_grad
    )
    terms = lax.all_to_all(ended[4].reshape(NEX, 24, 896), EX, 0, 0)
    d_normed = sum(piece.astype(F32) for piece in exchange_y(ended[:4]))
    x = x_own.astype(F32)
    scale = lax.rsqrt(jnp.mean(x * x, axis=1, keepdims=True) + 1e-06)
    scaled = d_normed * gain_rows[0:1]
    inner = jnp.mean(scaled * x, axis=1, keepdims=True)
    input_grad = d_middle + scale * scaled - x * scale**3 * inner
    summed = jnp.sum(terms.astype(F32), axis=0)
    wo_out = summed[:, 704:].reshape(6, WIDTH)
    mine = lax.all_to_all(summed[:, :704].reshape(NY, 6, 704), "y", 0, 0)
    wqkv_out = mine[:, :, :576].reshape(NY, 6, 3, 192).transpose(1, 2, 0, 3).reshape(6, 2304)
    small_out = jnp.sum(mine[:, :, 576:], axis=0)
    return (
        output.reshape(MB, 1, TOK, WIDTH),
        input_grad.reshape(MB, 1, TOK, WIDTH),
        wqkv_out,
        wo_out,
        small_out[:, :64],
        small_out[:, 64],
        small_out[:, 65],
        small_out[:3, 66],
        grad_in,
        grad_out,
    )


def solution(mesh):
    grid = Mesh(mesh.devices.reshape(NY, 4, 4, 2), ("y", "z", "x", "c"))
    every = ("y",) + EX
    in_specs = (
        P(None, EX, "y", None),
        P(every, None),
        P(every, None),
        P(every, None),
        P(every),
        P(every),
        P(every),
        P(EX, None, "y"),
        P(EX, "y", None),
        P(None, EX, "y", None),
        P(None, EX, None),
        P(None, EX, "y", None),
    )
    out_specs = (
        P(None, EX, "y", None),
        P(None, EX, "y", None),
        P(every, None),
        P(every, None),
        P(every, None),
        P(every),
        P(every),
        P(every),
        P(EX, None, "y"),
        P(EX, "y", None),
    )
    return jax.shard_map(body, mesh=grid, in_specs=in_specs, out_specs=out_specs, check_vma=False)
```

```python
import math

import jax
import jax.numpy as jnp
from jax import lax
from jax.experimental import pallas as pl
from jax.experimental.pallas import tpu as pltpu
from jax.sharding import Mesh
from jax.sharding import PartitionSpec as P

HEADS = 12
HEAD_DIM = 64
BUCKETS = 32
CAP = 3
FAR_STEP = 6
WIDTH = 768
TOK = 64
MB = 2
NY = 4
NEX = 32
HG = HEADS // NY
SPAN = TOK * NY
SCORE_SCALE = 1.0 / math.sqrt(HEAD_DIM)
EX = ("z", "x", "c")
F32 = jnp.float32
BF = jnp.bfloat16
GELU_IN = math.sqrt(2.0 / math.pi)
GELU_CUBE = 0.044715

UP = [(i, (i + 1) % NY) for i in range(NY)]
DOWN = [(i, (i - 1) % NY) for i in range(NY)]
ACROSS = [(i, (i + 2) % NY) for i in range(NY)]


def dot(a, b, dims):
    return lax.dot_general(a, b, ((dims[:1], dims[1:]), ((), ())), preferred_element_type=F32)


def iota(shape, dim):
    return lax.broadcasted_iota(jnp.int32, shape, dim)


def bucket_of(gap):
    far = 16 + (jnp.maximum(gap - 16, 0) * 171) // 1024
    return jnp.where(gap < 16, gap, jnp.minimum(BUCKETS - 1, far))


def table_marks(place, head):
    shape = (WIDTH, SPAN)
    row = iota(shape, 0)
    owner = row // 6
    entry = 3 * (owner - NEX * place) + row - 6 * owner
    wanted = head * BUCKETS + bucket_of(iota(shape, 1))
    return jnp.where((row - 6 * owner < 3) & (entry == wanted), 1.0, 0.0).astype(BF)


def place_rows(pieces, place, target):
    for step, piece in zip((0, 3, 1, 2), pieces):
        start = lax.rem(place + step, NY) * TOK
        for m in range(MB):
            target[pl.ds(pl.multiple_of(m * SPAN + start, TOK), TOK), :] = piece[
                m * TOK : (m + 1) * TOK, :
            ]


def take_rows(pieces, place, source):
    for step, piece in zip((0, 3, 1, 2), pieces):
        start = lax.rem(place + step, NY) * TOK
        for m in range(MB):
            piece[m * TOK : (m + 1) * TOK, :] = source[
                pl.ds(pl.multiple_of(m * SPAN + start, TOK), TOK), :
            ].astype(piece.dtype)


def forward_kernel(
    scalars, nat_row, wo_row, x0, x1, x2, x3, packed,
    b0, b1, b2, b3, qkv, probs, mixed, weights, wo_heads, normed, x_all, rows, bias, branch,
):
    place = scalars[0]
    place_rows((x0, x1, x2, x3), place, x_all)
    row = iota((WIDTH, WIDTH), 0)
    perm = jnp.where(row == nat_row[0:1, :], 1.0, 0.0).astype(BF)
    weights[...] = dot(perm, packed[:, :704], (1, 0)).astype(BF)
    for part in range(4):
        choose = jnp.where(iota((192, WIDTH), 0) * 4 + part == wo_row[0:1, :], 1.0, 0.0).astype(BF)
        wo_heads[:, part * 192 : part * 192 + 192] = dot(
            choose, packed[:, 704:896], (1, 0)
        ).astype(BF)
    lane_of = jnp.where(iota((8, 128), 1) == iota((8, 128), 0) + 64, 1.0, 0.0).astype(BF)
    rows[...] = dot(lane_of, weights[:, 576:704], (1, 1))
    values = x_all[...].astype(F32)
    scale = lax.rsqrt(jnp.mean(values * values, axis=1, keepdims=True) + 1e-06)
    normed[...] = (values * scale * rows[0:1, :]).astype(BF)
    qkv[...] = dot(normed[...], weights[:, :576], (1, 0)).astype(BF)
    table = rows[...].astype(BF)
    for head in range(HG):
        mirrored = dot(table, table_marks(place, head), (1, 0))[2:3, :]
        flip = jnp.where(iota((SPAN, SPAN), 0) + iota((SPAN, SPAN), 1) == SPAN - 1, 1.0, 0.0)
        mirrored = dot(jnp.broadcast_to(mirrored, (8, SPAN)).astype(BF), flip.astype(BF), (1, 0))
        spread = jnp.broadcast_to(mirrored[0:1, :], (SPAN, SPAN))
        bias[head] = pltpu.roll(spread, 1, 1, stride=1, stride_axis=0)
    query = iota((SPAN, SPAN), 0)
    key = iota((SPAN, SPAN), 1)
    for m in range(MB):
        first = scalars[1 + 2 * m]
        second = scalars[2 + 2 * m]
        of_query = jnp.where(query >= first, 1, 0) + jnp.where(query >= second, 1, 0)
        of_key = jnp.where(key >= first, 1, 0) + jnp.where(key >= second, 1, 0)
        seen = (of_query == of_key) & (query >= key)
        part = slice(m * SPAN, (m + 1) * SPAN)
        for head in range(HG):
            at = head * HEAD_DIM
            raw = dot(
                qkv[part, at : at + HEAD_DIM], qkv[part, 192 + at : 192 + at + HEAD_DIM], (1, 1)
            )
            scores = jnp.where(seen, raw * SCORE_SCALE + bias[head], -1000000000.0)
            peak = jnp.max(scores, axis=1, keepdims=True)
            powers = jnp.exp(scores - peak)
            share = powers / jnp.sum(powers, axis=1, keepdims=True)
            probs[m * HG + head] = share
            mixed[part, at : at + HEAD_DIM] = dot(
                share.astype(BF), qkv[part, 384 + at : 384 + at + HEAD_DIM], (1, 0)
            ).astype(BF)
    branch[...] = dot(mixed[...], wo_heads[...], (1, 0))
    take_rows((b0, b1, b2, b3), place, branch)


def backward_kernel(
    scalars, d0, d1, d2, d3, qkv, probs, mixed, weights, wo_heads, normed, x_all, wr_grad, gain_two,
    n0, n1, n2, n3, grads, d_branch, d_mixed, d_qkv, d_normed, d_bias,
):
    place = scalars[0]
    place_rows((d0, d1, d2, d3), place, d_branch)
    grad_wo = dot(mixed[...], d_branch[...], (0, 0)).astype(BF)
    packed_wo = jnp.zeros((WIDTH, 192), F32)
    for part in range(4):
        choose = jnp.where(iota((WIDTH, 192), 1) * 4 + part == iota((WIDTH, 192), 0), 1.0, 0.0)
        packed_wo = packed_wo + dot(
            choose.astype(BF), grad_wo[:, part * 192 : part * 192 + 192], (1, 0)
        )
    grads[:, 704:896] = packed_wo.astype(BF)
    d_mixed[...] = dot(d_branch[...], wo_heads[...], (1, 1)).astype(BF)
    for m in range(MB):
        part = slice(m * SPAN, (m + 1) * SPAN)
        for head in range(HG):
            at = head * HEAD_DIM
            lanes = slice(at, at + HEAD_DIM)
            share = probs[m * HG + head]
            d_mixed_head = d_mixed[part, lanes]
            d_probs = dot(d_mixed_head, qkv[part, 384 + at : 384 + at + HEAD_DIM], (1, 1))
            d_qkv[part, 384 + at : 384 + at + HEAD_DIM] = dot(
                share.astype(BF), d_mixed_head, (0, 0)
            ).astype(BF)
            inner = jnp.sum(share * d_probs, axis=1, keepdims=True)
            d_scores = share * (d_probs - inner)
            if m == 0:
                d_bias[head] = d_scores
            else:
                d_bias[head] = d_bias[head] + d_scores
            d_raw = (d_scores * SCORE_SCALE).astype(BF)
            d_qkv[part, lanes] = dot(
                d_raw, qkv[part, 192 + at : 192 + at + HEAD_DIM], (1, 0)
            ).astype(BF)
            d_qkv[part, 192 + at : 192 + at + HEAD_DIM] = dot(
                d_raw, qkv[part, lanes], (0, 0)
            ).astype(BF)
    d_normed[...] = dot(d_qkv[...], weights[:, :576], (1, 1))
    take_rows((n0, n1, n2, n3), place, d_normed)
    values = x_all[...].astype(F32)
    scale = lax.rsqrt(jnp.mean(values * values, axis=1, keepdims=True) + 1e-06)
    gain_one = jnp.sum(d_normed[...] * values * scale, axis=0, keepdims=True)
    flip = jnp.where(iota((SPAN, SPAN), 0) + iota((SPAN, SPAN), 1) == SPAN - 1, 1.0, 0.0).astype(BF)
    table = jnp.zeros((8, WIDTH), F32)
    for head in range(HG):
        total = d_bias[head]
        high = total.astype(BF)
        low = (total - high.astype(F32)).astype(BF)
        turned = dot(flip, high, (1, 0)) + dot(flip, low, (1, 0))
        skewed = pltpu.roll(turned, 0, 1, stride=1, stride_axis=0)
        diagonal = jnp.broadcast_to(jnp.sum(skewed, axis=0, keepdims=True), (8, SPAN))
        high = diagonal.astype(BF)
        low = (diagonal - high.astype(F32)).astype(BF)
        by_gap = dot(high, flip, (1, 0)) + dot(low, flip, (1, 0))
        marks = table_marks(place, head)
        high = by_gap.astype(BF)
        low = (by_gap - high.astype(F32)).astype(BF)
        table = table + dot(high, marks, (1, 1)) + dot(low, marks, (1, 1))
    which = iota((8, WIDTH), 0)
    rows = jnp.where(
        which == 0, gain_one, jnp.where(which == 1, gain_two[0:1, :], jnp.where(which == 2, table, 0.0))
    )
    lane_of = jnp.where(iota((8, 128), 1) == iota((8, 128), 0) + 64, 1.0, 0.0).astype(BF)
    small = wr_grad[...] + dot(rows.astype(BF), lane_of, (0, 0))
    row = iota((WIDTH, WIDTH), 0)
    col = iota((WIDTH, WIDTH), 1)
    chunk = row // 24
    rest = row - 24 * chunk
    group = rest // 6
    wanted = (group * NEX + chunk) * 6 + rest - 6 * group
    perm = jnp.where(col == wanted, 1.0, 0.0).astype(BF)
    grad_heads = dot(normed[...], d_qkv[...], (0, 0)).astype(BF)
    grads[:, :576] = dot(perm, grad_heads, (1, 0)).astype(BF)
    grads[:, 576:704] = dot(perm, small.astype(BF), (1, 0)).astype(BF)


def vmem_call(kernel, outs, scratch, *args):
    full = pl.BlockSpec()
    return pl.pallas_call(
        kernel,
        out_shape=[jax.ShapeDtypeStruct(shape, kind) for shape, kind in outs],
        in_specs=[pl.BlockSpec(memory_space=pltpu.SMEM)] + [full] * (len(args) - 1),
        out_specs=[full] * len(outs),
        scratch_shapes=[pltpu.VMEM(shape, kind) for shape, kind in scratch],
        compiler_params=pltpu.CompilerParams(vmem_limit_bytes=60 * 1024 * 1024),
    )(*args)


def attention_forward(scalars, nat_row, wo_row, x_pieces, packed):
    rows = MB * SPAN
    outs = [((128, WIDTH), BF)] * 4 + [
        ((rows, 576), BF),
        ((MB * HG, SPAN, SPAN), F32),
        ((rows, 192), BF),
        ((WIDTH, 704), BF),
        ((192, WIDTH), BF),
        ((rows, WIDTH), BF),
        ((rows, WIDTH), BF),
        ((8, WIDTH), F32),
    ]
    scratch = [((HG, SPAN, SPAN), F32), ((rows, WIDTH), F32)]
    return vmem_call(forward_kernel, outs, scratch, scalars, nat_row, wo_row, *x_pieces, packed)


def attention_backward(scalars, d_pieces, kept, wr_grad, gain_two):
    rows = MB * SPAN
    outs = [((128, WIDTH), BF)] * 4 + [((WIDTH, 896), BF)]
    scratch = [
        ((rows, WIDTH), BF),
        ((rows, 192), BF),
        ((rows, 576), BF),
        ((rows, WIDTH), F32),
        ((HG, SPAN, SPAN), F32),
    ]
    return vmem_call(backward_kernel, outs, scratch, scalars, *d_pieces, *kept, wr_grad, gain_two)


def middle_kernel(
    scalars, b0, b1, b2, b3, x_own, rows, weights, info, middle, entering, gates, buffer
):
    values = x_own[...].astype(F32) + (
        (b0[...].astype(F32) + b1[...].astype(F32)) + (b2[...].astype(F32) + b3[...].astype(F32))
    )
    middle[...] = values
    scale = lax.rsqrt(jnp.mean(values * values, axis=1, keepdims=True) + 1e-06)
    low = (values * scale * rows[1:2, :]).astype(BF)
    entering[...] = low
    logits = dot(low, weights[:, 576:704], (1, 0))
    lane = iota((128, 128), 1)
    chosen = [
        jnp.sum(jnp.where(lane == info[:, 6 + k : 7 + k], logits, 0.0), axis=1, keepdims=True)
        for k in range(2)
    ]
    peak = jnp.maximum(chosen[0], chosen[1])
    powers = [jnp.exp(value - peak) for value in chosen]
    total = powers[0] + powers[1]
    share = [power / total for power in powers]
    gates[...] = jnp.where(lane == 0, share[0], jnp.where(lane == 1, share[1], 0.0))
    place = iota((128, 512), 1)
    wide = iota((128, WIDTH), 1)
    pick = jnp.where(
        (place == info[:, 0:1]) | (place == info[:, 1:2]), 1.0, 0.0
    ).astype(BF)
    sent = dot(pick, low, (0, 0))
    for k in range(2):
        mark = wide == info[:, 4 + k : 5 + k]
        high = share[k].astype(BF).astype(F32)
        rest = share[k] - high
        for at, value in ((0, high), (1, rest)):
            spot = jnp.where(place == info[:, 2 + k : 3 + k] + at, 1.0, 0.0).astype(BF)
            sent = sent + dot(spot, jnp.where(mark, value, 0.0).astype(BF), (0, 0))
    buffer[...] = sent.astype(BF)


def return_kernel(
    scalars, back, info, gates, entering, middle, rows, weights, dy_own,
    d_middle, d_branch, wr_grad, gain_two,
):
    place = iota((128, 512), 1)
    wide = iota((128, WIDTH), 1)
    lane = iota((128, 128), 1)
    share = [gates[:, k : k + 1] for k in range(2)]
    d_entering = jnp.zeros((128, WIDTH), F32)
    d_gates = []
    for k in range(2):
        pick = jnp.where(place == info[:, k : k + 1], 1.0, 0.0).astype(BF)
        d_entering = d_entering + share[k] * dot(pick, back[...], (1, 0))
        at = info[:, 2 + k : 3 + k]
        spot = jnp.where((place == at) | (place == at + 1), 1.0, 0.0).astype(BF)
        d_gates.append(
            jnp.sum(
                jnp.where(wide == info[:, 4 + k : 5 + k], dot(spot, back[...], (1, 0)), 0.0),
                axis=1,
                keepdims=True,
            )
        )
    inner = share[0] * d_gates[0] + share[1] * d_gates[1]
    d_logits = jnp.zeros((128, 128), F32)
    for k in range(2):
        d_logits = d_logits + jnp.where(
            lane == info[:, 6 + k : 7 + k], share[k] * (d_gates[k] - inner), 0.0
        )
    d_logits = d_logits.astype(BF)
    d_entering = d_entering + dot(d_logits, weights[:, 576:704], (1, 1))
    wr_grad[...] = dot(entering[...], d_logits, (0, 0))
    values = middle[...]
    scale = lax.rsqrt(jnp.mean(values * values, axis=1, keepdims=True) + 1e-06)
    gain_two[...] = jnp.broadcast_to(
        jnp.sum(d_entering * values * scale, axis=0, keepdims=True), (8, WIDTH)
    )
    scaled = d_entering * rows[1:2, :]
    mean = jnp.mean(scaled * values, axis=1, keepdims=True)
    total = dy_own[...].astype(F32) + scale * scaled - values * scale * scale * scale * mean
    d_middle[...] = total
    d_branch[...] = total.astype(BF)


def gelu_parts(value):
    inner = GELU_IN * (value + GELU_CUBE * value * value * value)
    bend = jnp.tanh(inner)
    half = 0.5 * (1.0 + bend)
    slope = half + 0.5 * value * (1.0 - bend * bend) * GELU_IN * (
        1.0 + 3.0 * GELU_CUBE * value * value
    )
    return value * half, slope


def expert_kernel(
    scalars, p0, p1, p2, p3a, p3b, dy_rows, w_in, w_out,
    o0, o1, o2, o3a, o3b, rows_all, active_all, d_raised_all, d_returned_all,
    dy_here, raised, pulled, d_raised,
):
    place = scalars[0]
    tall = NEX * 6
    ones = jnp.ones((8, WIDTH), BF)
    wide_ones = jnp.ones((tall, 128), BF)
    extra_row = iota((16, tall), 0)
    eye = iota((tall, tall), 0) == iota((tall, tall), 1)
    for n in range(2):
        part = slice(n * tall, n * tall + tall)
        for spot, step in enumerate((0, 3, 1, 2)):
            here = slice(spot * tall, spot * tall + tall)
            owner = lax.rem(place + step, NY)
            dy_here[here, :] = dy_rows[owner, part, :]
            if step != 2:
                rows_all[n, here, :] = (p0, p1, p2)[spot][part, :]
            elif n == 0:
                rows_all[n, here, :] = p3a[0:tall, :]
            else:
                rows_all[n, spot * tall : spot * tall + 16, :] = p3a[tall : tall + 16, :]
                rows_all[n, spot * tall + 16 : spot * tall + tall, :] = p3b[0 : tall - 16, :]
        raised[...] = dot(rows_all[n], w_in[n], (1, 0))
        pulled[...] = dot(dy_here[...], w_out[n], (1, 1))
        for spot, step in enumerate((0, 3, 1, 2)):
            here = slice(spot * tall, spot * tall + tall)
            gate = p3b[tall - 16 : tall, part] if step == 2 else (p0, p1, p2)[spot][384:400, part]
            gate = gate.astype(F32)
            gate_col = dot(jnp.where(eye, gate[0:1, :], 0.0).astype(BF), wide_ones, (1, 0))
            gate_col = gate_col + dot(
                jnp.where(eye, gate[1:2, :], 0.0).astype(BF), wide_ones, (1, 0)
            )
            gate_col = gate_col[:, 0:1]
            active, slope = gelu_parts(raised[here, :])
            active = active.astype(BF)
            active_all[n, here, :] = active
            pull = pulled[here, :]
            product = active.astype(F32) * pull
            change = slope * pull
            d_raised[here, :] = change.astype(BF)
            d_raised_all[n, here, :] = (change * gate_col).astype(BF)
            d_returned_all[n, here, :] = (dy_here[here, :].astype(F32) * gate_col).astype(BF)
            high = product.astype(BF)
            low = (product - high.astype(F32)).astype(BF)
            d_gate = dot(ones, high, (1, 1)) + dot(ones, low, (1, 1))
            tail = (o0, o1, o2, o3b)[spot]
            last = tail.shape[0] - 16
            if n == 0:
                tail[last:, 384:WIDTH] = jnp.zeros((16, WIDTH - 384), BF)
            tail[last:, part] = jnp.where(extra_row == 0, d_gate[0:1, :], 0.0).astype(BF)
        raised[...] = dot(d_raised[...], w_in[n], (1, 1))
        for spot in range(3):
            (o0, o1, o2)[spot][part, :] = raised[spot * tall : spot * tall + tall, :].astype(BF)
        last = raised[3 * tall : 4 * tall, :].astype(BF)
        if n == 0:
            o3a[0:tall, :] = last
        else:
            o3a[tall : tall + 16, :] = last[0:16, :]
            o3b[0 : tall - 16, :] = last[16:tall, :]


def expert_rows(scalars, pieces, dy_rows, w_in, w_out):
    square = ((2, WIDTH, WIDTH), BF)
    outs = [((400, WIDTH), BF)] * 3 + [((208, WIDTH), BF), ((192, WIDTH), BF)] + [square] * 4
    whole = (WIDTH, WIDTH)
    scratch = [(whole, BF), (whole, F32), (whole, F32), (whole, BF)]
    return vmem_call(expert_kernel, outs, scratch, scalars, *pieces, dy_rows, w_in, w_out)


def middle_step(scalars, pieces, x_own, rows, weights, info):
    outs = [((128, WIDTH), F32), ((128, WIDTH), BF), ((128, 128), F32), ((512, WIDTH), BF)]
    return vmem_call(middle_kernel, outs, [], scalars, *pieces, x_own, rows, weights, info)


def return_step(scalars, back, info, gates, entering, middle, rows, weights, dy_own):
    outs = [((128, WIDTH), F32), ((128, WIDTH), BF), ((WIDTH, 128), F32), ((8, WIDTH), F32)]
    return vmem_call(
        return_kernel, outs, [], scalars, back, info, gates, entering, middle, rows, weights, dy_own
    )


def gather_four(piece, axis):
    return [piece] + [lax.ppermute(piece, axis, way) for way in (UP, DOWN, ACROSS)]


def owner_at(step, axis):
    shift = jnp.where(step == 1, 3, jnp.where(step == 2, 1, jnp.where(step == 3, 2, 0)))
    return (lax.axis_index(axis) + shift) % 4


def exchange_y(pieces):
    ways = (DOWN, UP, ACROSS)
    return [pieces[0]] + [lax.ppermute(piece, "y", way) for piece, way in zip(pieces[1:], ways)]


def ring_gather(piece, cut):
    below = lax.ppermute(piece, "y", UP)
    above = lax.ppermute(piece, "y", DOWN)
    first = lax.ppermute(below[:cut], "y", UP)
    second = lax.ppermute(above[cut:], "y", DOWN)
    return piece, below, above, first, second


def ring_scatter(pieces, cut):
    own, below, above, across_first, across_second = pieces
    first = lax.ppermute(across_first, "y", UP)
    second = lax.ppermute(across_second, "y", DOWN)
    up = jnp.concatenate(
        [(above[:cut].astype(F32) + first.astype(F32)).astype(BF), above[cut:]], axis=0
    )
    down = jnp.concatenate(
        [below[:cut], (below[cut:].astype(F32) + second.astype(F32)).astype(BF)], axis=0
    )
    from_below = lax.ppermute(up, "y", UP)
    from_above = lax.ppermute(down, "y", DOWN)
    total = own.astype(F32) + from_below.astype(F32) + from_above.astype(F32)
    return total, up


def mm(a, b):
    return lax.dot_general(a, b, (((1,), (0,)), ((), ())), preferred_element_type=F32)


def mm_tn(a, b):
    return lax.dot_general(a, b, (((0,), (0,)), ((), ())), preferred_element_type=F32)


def body(
    inputs, wqkv, wo, wr, gain_one, gain_two, rel_bias, w_in, w_out, routes, lengths, cotangent
):
    place = lax.axis_index("y")
    tokens = MB * TOK
    x_own = inputs.reshape(tokens, WIDTH)
    dy_own = cotangent.reshape(tokens, WIDTH)
    cols = wqkv.reshape(6, 3, NY, 192).transpose(2, 0, 1, 3).reshape(NY, 6, 576)
    small = jnp.concatenate(
        [
            wr,
            gain_one[:, None],
            gain_two[:, None],
            jnp.pad(rel_bias, (0, 3))[:, None],
            jnp.zeros((6, 61), BF),
        ],
        axis=1,
    )
    to_y = jnp.concatenate([cols, jnp.broadcast_to(small[None], (NY, 6, 128))], axis=2)
    from_y = lax.all_to_all(to_y, "y", 0, 0).reshape(24, 704)
    pack = jnp.concatenate([from_y, wo.reshape(24, 192)], axis=1)
    x_pieces = gather_four(x_own, "y")
    packed = jnp.concatenate(gather_four(pack, "x"), axis=0)
    packed = jnp.concatenate(gather_four(packed, "z"), axis=0)
    dy_later, x_pieces[1] = lax.optimization_barrier((dy_own, x_pieces[1]))
    packed = jnp.concatenate([packed, lax.ppermute(packed, "c", [(0, 1), (1, 0)])], axis=0)
    rows = jnp.arange(WIDTH, dtype=jnp.int32)
    step = rows // 24
    owner = owner_at(step // 4 % 4, "z") * 8 + owner_at(step % 4, "x") * 2
    owner = owner + (lax.axis_index("c") + step // 16) % 2
    in_chunk = rows % 24
    nat_row = jnp.broadcast_to((((in_chunk // 6) * NEX + owner) * 6 + in_chunk % 6)[None], (8, WIDTH))
    wo_row = jnp.broadcast_to((owner * 24 + in_chunk)[None], (8, WIDTH))
    bounds = jnp.cumsum(lengths.reshape(MB, 3), axis=1)[:, :2].reshape(4)
    scalars = jnp.concatenate([place[None].astype(jnp.int32), bounds])
    route = routes.reshape(MB, 2 * TOK)
    flat = jnp.arange(2 * TOK, dtype=jnp.int32)
    same = (route[:, :, None] == route[:, None, :]) & (flat[:, None] > flat[None, :])[None]
    slot = jnp.sum(same.astype(jnp.int32), axis=2)
    slot = (slot + jnp.arange(MB, dtype=jnp.int32)[:, None] * CAP).reshape(tokens, 2)
    route = route.reshape(tokens, 2)
    side = route % 2
    dest = (route // 2) * 16
    me = lax.axis_index(EX)
    info = jnp.concatenate(
        [dest + side * 6 + slot, dest + 12, side * 192 + me * 6 + slot, route], axis=1
    )
    buffer_rows = jnp.arange(512, dtype=jnp.int32)
    pick = [(buffer_rows[None, :] == info[:, k : k + 1]).astype(BF) for k in range(2)]
    slots = jnp.arange(400, dtype=jnp.int32)
    buffer_of = (slots // 6 % NEX) * 16 + (slots // 192) * 6 + slots % 6
    compact = jnp.where(
        slots[:, None] < 384,
        buffer_of[:, None] == buffer_rows[None, :],
        (buffer_rows % 16)[None, :] == 12 + slots[:, None] - 384,
    )
    compact = (compact & (slots < 386)[:, None]).astype(BF)

    def to_experts(buffer):
        return lax.all_to_all(buffer.reshape(NEX, 16, WIDTH), EX, 0, 0).reshape(512, WIDTH)

    dy_rows = mm(compact[:384], to_experts(mm_tn(pick[0] + pick[1], dy_later).astype(BF)))
    kept = attention_forward(scalars, nat_row, wo_row, x_pieces, packed)
    branch, saved, gain_rows = kept[:4], kept[4:11], kept[11]
    weights = saved[3]
    branch = exchange_y(branch)
    dy_rows, *branch = lax.optimization_barrier((dy_rows.astype(BF), *branch))
    dy_rows = lax.all_gather(dy_rows, "y")
    middle, entering, gates, buffer = middle_step(
        scalars, branch, x_own, gain_rows, weights, info
    )
    arrived = mm(compact, to_experts(buffer)).astype(BF)
    results = expert_rows(scalars, ring_gather(arrived, 208), dy_rows, w_in, w_out)
    d_arrived, (rows_all, active, d_raised, d_returned) = results[:5], results[5:]
    d_home, in_flight = ring_scatter(d_arrived, 208)
    d_home_high = d_home.astype(BF)
    d_home_low = (d_home[384:385] - d_home_high[384:385].astype(F32)).astype(BF)
    d_home = jnp.where(
        (slots == 385)[:, None], d_home_low, d_home_high
    )
    back = to_experts(mm_tn(compact, d_home).astype(BF))
    active, _ = lax.optimization_barrier((active, in_flight))
    result = jnp.einsum("erf,efd->erd", active, w_out, preferred_element_type=F32).astype(BF)
    result = result.reshape(2, NY, 192, WIDTH)
    order = (0, 2, 3, 1)
    result = jnp.roll(jnp.stack([result[:, n] for n in order]), place, axis=0)
    result, _ = lax.optimization_barrier((result, d_home))
    result = lax.psum_scatter(result.reshape(NY, 384, WIDTH), "y", scatter_dimension=0)
    grad_in = jnp.einsum("erd,erf->edf", rows_all, d_raised, preferred_element_type=F32)
    grad_out = jnp.einsum("erf,erd->efd", active, d_returned, preferred_element_type=F32)
    back, grad_in, grad_out = lax.optimization_barrier((back, grad_in, grad_out))
    d_middle, d_branch, wr_grad, gain_two_grad = return_step(
        scalars, back, info, gates, entering, middle, gain_rows, weights, dy_own
    )
    d_pieces = gather_four(d_branch, "y")
    back_result = mm_tn(compact[:384], result).astype(BF)
    back_result, *d_pieces = lax.optimization_barrier((back_result, *d_pieces))
    returned = to_experts(back_result)
    mixture = sum(gates[:, k : k + 1] * mm(pick[k], returned) for k in range(2))
    output = (middle + mixture).astype(BF)
    ended = attention_backward(
        scalars, d_pieces, saved, wr_grad, gain_two_grad
    )
    terms = lax.all_to_all(ended[4].reshape(NEX, 24, 896), EX, 0, 0)
    d_normed = sum(piece.astype(F32) for piece in exchange_y(ended[:4]))
    x = x_own.astype(F32)
    scale = lax.rsqrt(jnp.mean(x * x, axis=1, keepdims=True) + 1e-06)
    scaled = d_normed * gain_rows[0:1]
    inner = jnp.mean(scaled * x, axis=1, keepdims=True)
    input_grad = d_middle + scale * scaled - x * scale**3 * inner
    summed = jnp.sum(terms.astype(F32), axis=0)
    wo_out = summed[:, 704:].reshape(6, WIDTH)
    mine = lax.all_to_all(summed[:, :704].reshape(NY, 6, 704), "y", 0, 0)
    wqkv_out = mine[:, :, :576].reshape(NY, 6, 3, 192).transpose(1, 2, 0, 3).reshape(6, 2304)
    small_out = jnp.sum(mine[:, :, 576:], axis=0)
    return (
        output.reshape(MB, 1, TOK, WIDTH),
        input_grad.reshape(MB, 1, TOK, WIDTH),
        wqkv_out,
        wo_out,
        small_out[:, :64],
        small_out[:, 64],
        small_out[:, 65],
        small_out[:3, 66],
        grad_in,
        grad_out,
    )


def solution(mesh):
    grid = Mesh(mesh.devices.reshape(NY, 4, 4, 2), ("y", "z", "x", "c"))
    every = ("y",) + EX
    in_specs = (
        P(None, EX, "y", None),
        P(every, None),
        P(every, None),
        P(every, None),
        P(every),
        P(every),
        P(every),
        P(EX, None, "y"),
        P(EX, "y", None),
        P(None, EX, "y", None),
        P(None, EX, None),
        P(None, EX, "y", None),
    )
    out_specs = (
        P(None, EX, "y", None),
        P(None, EX, "y", None),
        P(every, None),
        P(every, None),
        P(every, None),
        P(every),
        P(every),
        P(every),
        P(EX, None, "y"),
        P(EX, "y", None),
    )
    return jax.shard_map(body, mesh=grid, in_specs=in_specs, out_specs=out_specs, check_vma=False)
```

```python
import math

import jax
import jax.numpy as jnp
from jax import lax
from jax.experimental import pallas as pl
from jax.experimental.pallas import tpu as pltpu
from jax.sharding import Mesh
from jax.sharding import PartitionSpec as P

HEADS = 12
HEAD_DIM = 64
BUCKETS = 32
CAP = 3
FAR_STEP = 6
WIDTH = 768
TOK = 64
MB = 2
NY = 4
NEX = 32
HG = HEADS // NY
SPAN = TOK * NY
SCORE_SCALE = 1.0 / math.sqrt(HEAD_DIM)
EX = ("z", "x", "c")
F32 = jnp.float32
BF = jnp.bfloat16
GELU_IN = math.sqrt(2.0 / math.pi)
GELU_CUBE = 0.044715

UP = [(i, (i + 1) % NY) for i in range(NY)]
DOWN = [(i, (i - 1) % NY) for i in range(NY)]
ACROSS = [(i, (i + 2) % NY) for i in range(NY)]


def dot(a, b, dims):
    return lax.dot_general(a, b, ((dims[:1], dims[1:]), ((), ())), preferred_element_type=F32)


def iota(shape, dim):
    return lax.broadcasted_iota(jnp.int32, shape, dim)


def bucket_of(gap):
    far = 16 + (jnp.maximum(gap - 16, 0) * 171) // 1024
    return jnp.where(gap < 16, gap, jnp.minimum(BUCKETS - 1, far))


def table_marks(place, head):
    shape = (WIDTH, SPAN)
    row = iota(shape, 0)
    owner = row // 6
    entry = 3 * (owner - NEX * place) + row - 6 * owner
    wanted = head * BUCKETS + bucket_of(iota(shape, 1))
    return jnp.where((row - 6 * owner < 3) & (entry == wanted), 1.0, 0.0).astype(BF)


def place_rows(pieces, place, target):
    for step, piece in zip((0, 3, 1, 2), pieces):
        start = lax.rem(place + step, NY) * TOK
        for m in range(MB):
            target[pl.ds(pl.multiple_of(m * SPAN + start, TOK), TOK), :] = piece[
                m * TOK : (m + 1) * TOK, :
            ]


def take_rows(pieces, place, source):
    for step, piece in zip((0, 3, 1, 2), pieces):
        start = lax.rem(place + step, NY) * TOK
        for m in range(MB):
            piece[m * TOK : (m + 1) * TOK, :] = source[
                pl.ds(pl.multiple_of(m * SPAN + start, TOK), TOK), :
            ].astype(piece.dtype)


def forward_kernel(
    scalars, nat_row, wo_row, x0, x1, x2, x3, q0, q1, q2, q3, q4, q5, q6, q7,
    b0, b1, b2, b3, qkv, probs, mixed, weights, wo_heads, normed, router, rows,
    x_all, bias, branch, packed,
):
    place = scalars[0]
    place_rows((x0, x1, x2, x3), place, x_all)
    for spot, piece in enumerate((q0, q1, q2, q3, q4, q5, q6, q7)):
        packed[spot * 96 : spot * 96 + 96, :] = piece[...]
    row = iota((WIDTH, WIDTH), 0)
    perm = jnp.where(row == nat_row[0:1, :], 1.0, 0.0).astype(BF)
    weights[...] = dot(perm, packed[:, :704], (1, 0)).astype(BF)
    router[...] = weights[:, 576:704]
    for part in range(4):
        choose = jnp.where(iota((192, WIDTH), 0) * 4 + part == wo_row[0:1, :], 1.0, 0.0).astype(BF)
        wo_heads[:, part * 192 : part * 192 + 192] = dot(
            choose, packed[:, 704:896], (1, 0)
        ).astype(BF)
    lane_of = jnp.where(iota((8, 128), 1) == iota((8, 128), 0) + 64, 1.0, 0.0).astype(BF)
    rows[...] = dot(lane_of, weights[:, 576:704], (1, 1))
    values = x_all[...].astype(F32)
    scale = lax.rsqrt(jnp.mean(values * values, axis=1, keepdims=True) + 1e-06)
    normed[...] = (values * scale * rows[0:1, :]).astype(BF)
    qkv[...] = dot(normed[...], weights[:, :576], (1, 0)).astype(BF)
    table = rows[...].astype(BF)
    for head in range(HG):
        mirrored = dot(table, table_marks(place, head), (1, 0))[2:3, :]
        flip = jnp.where(iota((SPAN, SPAN), 0) + iota((SPAN, SPAN), 1) == SPAN - 1, 1.0, 0.0)
        mirrored = dot(jnp.broadcast_to(mirrored, (8, SPAN)).astype(BF), flip.astype(BF), (1, 0))
        spread = jnp.broadcast_to(mirrored[0:1, :], (SPAN, SPAN))
        bias[head] = pltpu.roll(spread, 1, 1, stride=1, stride_axis=0)
    query = iota((SPAN, SPAN), 0)
    key = iota((SPAN, SPAN), 1)
    for m in range(MB):
        first = scalars[1 + 2 * m]
        second = scalars[2 + 2 * m]
        of_query = jnp.where(query >= first, 1, 0) + jnp.where(query >= second, 1, 0)
        of_key = jnp.where(key >= first, 1, 0) + jnp.where(key >= second, 1, 0)
        seen = (of_query == of_key) & (query >= key)
        part = slice(m * SPAN, (m + 1) * SPAN)
        for head in range(HG):
            at = head * HEAD_DIM
            raw = dot(
                qkv[part, at : at + HEAD_DIM], qkv[part, 192 + at : 192 + at + HEAD_DIM], (1, 1)
            )
            scores = jnp.where(seen, raw * SCORE_SCALE + bias[head], -1000000000.0)
            peak = jnp.max(scores, axis=1, keepdims=True)
            powers = jnp.exp(scores - peak)
            share = powers / jnp.sum(powers, axis=1, keepdims=True)
            probs[m * HG + head] = share
            mixed[part, at : at + HEAD_DIM] = dot(
                share.astype(BF), qkv[part, 384 + at : 384 + at + HEAD_DIM], (1, 0)
            ).astype(BF)
    branch[...] = dot(mixed[...], wo_heads[...], (1, 0))
    take_rows((b0, b1, b2, b3), place, branch)


def backward_kernel(
    scalars, d0, d1, d2, d3, qkv, probs, mixed, weights, wo_heads, normed, wr_grad, gain_two,
    grads, d_qkv, d_branch, d_mixed, d_bias,
):
    place = scalars[0]
    place_rows((d0, d1, d2, d3), place, d_branch)
    grad_wo = dot(mixed[...], d_branch[...], (0, 0)).astype(BF)
    packed_wo = jnp.zeros((WIDTH, 192), F32)
    for part in range(4):
        choose = jnp.where(iota((WIDTH, 192), 1) * 4 + part == iota((WIDTH, 192), 0), 1.0, 0.0)
        packed_wo = packed_wo + dot(
            choose.astype(BF), grad_wo[:, part * 192 : part * 192 + 192], (1, 0)
        )
    grads[:, 704:896] = packed_wo.astype(BF)
    d_mixed[...] = dot(d_branch[...], wo_heads[...], (1, 1)).astype(BF)
    for m in range(MB):
        part = slice(m * SPAN, (m + 1) * SPAN)
        for head in range(HG):
            at = head * HEAD_DIM
            lanes = slice(at, at + HEAD_DIM)
            share = probs[m * HG + head]
            d_mixed_head = d_mixed[part, lanes]
            d_probs = dot(d_mixed_head, qkv[part, 384 + at : 384 + at + HEAD_DIM], (1, 1))
            d_qkv[part, 384 + at : 384 + at + HEAD_DIM] = dot(
                share.astype(BF), d_mixed_head, (0, 0)
            ).astype(BF)
            inner = jnp.sum(share * d_probs, axis=1, keepdims=True)
            d_scores = share * (d_probs - inner)
            if m == 0:
                d_bias[head] = d_scores
            else:
                d_bias[head] = d_bias[head] + d_scores
            d_raw = (d_scores * SCORE_SCALE).astype(BF)
            d_qkv[part, lanes] = dot(
                d_raw, qkv[part, 192 + at : 192 + at + HEAD_DIM], (1, 0)
            ).astype(BF)
            d_qkv[part, 192 + at : 192 + at + HEAD_DIM] = dot(
                d_raw, qkv[part, lanes], (0, 0)
            ).astype(BF)
    flip = jnp.where(iota((SPAN, SPAN), 0) + iota((SPAN, SPAN), 1) == SPAN - 1, 1.0, 0.0).astype(BF)
    table = jnp.zeros((8, WIDTH), F32)
    for head in range(HG):
        total = d_bias[head]
        high = total.astype(BF)
        low = (total - high.astype(F32)).astype(BF)
        turned = dot(flip, high, (1, 0)) + dot(flip, low, (1, 0))
        skewed = pltpu.roll(turned, 0, 1, stride=1, stride_axis=0)
        diagonal = jnp.broadcast_to(jnp.sum(skewed, axis=0, keepdims=True), (8, SPAN))
        high = diagonal.astype(BF)
        low = (diagonal - high.astype(F32)).astype(BF)
        by_gap = dot(high, flip, (1, 0)) + dot(low, flip, (1, 0))
        marks = table_marks(place, head)
        high = by_gap.astype(BF)
        low = (by_gap - high.astype(F32)).astype(BF)
        table = table + dot(high, marks, (1, 1)) + dot(low, marks, (1, 1))
    which = iota((8, WIDTH), 0)
    rows = jnp.where(which == 1, gain_two[0:1, :], jnp.where(which == 2, table, 0.0))
    lane_of = jnp.where(iota((8, 128), 1) == iota((8, 128), 0) + 64, 1.0, 0.0).astype(BF)
    grad_heads = dot(normed[...], d_qkv[...], (0, 0))
    gain_one = jnp.sum(grad_heads * weights[:, :576].astype(F32), axis=1, keepdims=True)
    gain_one = gain_one / weights[:, 640:641].astype(F32)
    small = wr_grad[...] + dot(rows.astype(BF), lane_of, (0, 0))
    small = small + jnp.where(iota((WIDTH, 128), 1) == 64, gain_one, 0.0)
    row = iota((WIDTH, WIDTH), 0)
    col = iota((WIDTH, WIDTH), 1)
    chunk = row // 24
    rest = row - 24 * chunk
    group = rest // 6
    wanted = (group * NEX + chunk) * 6 + rest - 6 * group
    perm = jnp.where(col == wanted, 1.0, 0.0).astype(BF)
    grads[:, :576] = dot(perm, grad_heads.astype(BF), (1, 0)).astype(BF)
    grads[:, 576:704] = dot(perm, small.astype(BF), (1, 0)).astype(BF)


def normed_kernel(scalars, d_qkv, weights, n0, n1, n2, n3, d_normed):
    d_normed[...] = dot(d_qkv[...], weights[:, :576], (1, 1))
    take_rows((n0, n1, n2, n3), scalars[0], d_normed)


def vmem_call(kernel, outs, scratch, *args):
    full = pl.BlockSpec()
    return pl.pallas_call(
        kernel,
        out_shape=[jax.ShapeDtypeStruct(shape, kind) for shape, kind in outs],
        in_specs=[pl.BlockSpec(memory_space=pltpu.SMEM)] + [full] * (len(args) - 1),
        out_specs=[full] * len(outs),
        scratch_shapes=[pltpu.VMEM(shape, kind) for shape, kind in scratch],
        compiler_params=pltpu.CompilerParams(vmem_limit_bytes=60 * 1024 * 1024),
    )(*args)


def attention_forward(scalars, nat_row, wo_row, x_pieces, packed):
    rows = MB * SPAN
    outs = [((128, WIDTH), BF)] * 4 + [
        ((rows, 576), BF),
        ((MB * HG, SPAN, SPAN), F32),
        ((rows, 192), BF),
        ((WIDTH, 704), BF),
        ((192, WIDTH), BF),
        ((rows, WIDTH), BF),
        ((WIDTH, 128), BF),
        ((8, WIDTH), F32),
    ]
    scratch = [((rows, WIDTH), BF), ((HG, SPAN, SPAN), F32), ((rows, WIDTH), F32), ((WIDTH, 896), BF)]
    return vmem_call(forward_kernel, outs, scratch, scalars, nat_row, wo_row, *x_pieces, *packed)


def attention_backward(scalars, d_pieces, kept, wr_grad, gain_two):
    rows = MB * SPAN
    outs = [((WIDTH, 896), BF), ((rows, 576), BF)]
    scratch = [((rows, WIDTH), BF), ((rows, 192), BF), ((HG, SPAN, SPAN), F32)]
    return vmem_call(backward_kernel, outs, scratch, scalars, *d_pieces, *kept, wr_grad, gain_two)


def middle_kernel(
    scalars, b0, b1, b2, b3, x_own, rows, router, info, middle, entering, gates, buffer
):
    values = x_own[...].astype(F32) + (
        (b0[...].astype(F32) + b1[...].astype(F32)) + (b2[...].astype(F32) + b3[...].astype(F32))
    )
    middle[...] = values
    scale = lax.rsqrt(jnp.mean(values * values, axis=1, keepdims=True) + 1e-06)
    low = (values * scale * rows[1:2, :]).astype(BF)
    entering[...] = low
    logits = dot(low, router[...], (1, 0))
    lane = iota((128, 128), 1)
    chosen = [
        jnp.sum(jnp.where(lane == info[:, 6 + k : 7 + k], logits, 0.0), axis=1, keepdims=True)
        for k in range(2)
    ]
    peak = jnp.maximum(chosen[0], chosen[1])
    powers = [jnp.exp(value - peak) for value in chosen]
    total = powers[0] + powers[1]
    share = [power / total for power in powers]
    gates[...] = jnp.where(lane == 0, share[0], jnp.where(lane == 1, share[1], 0.0))
    place = iota((128, 512), 1)
    wide = iota((128, WIDTH), 1)
    pick = jnp.where(
        (place == info[:, 0:1]) | (place == info[:, 1:2]), 1.0, 0.0
    ).astype(BF)
    sent = dot(pick, low, (0, 0))
    for k in range(2):
        mark = wide == info[:, 4 + k : 5 + k]
        high = share[k].astype(BF).astype(F32)
        rest = share[k] - high
        for at, value in ((0, high), (1, rest)):
            spot = jnp.where(place == info[:, 2 + k : 3 + k] + at, 1.0, 0.0).astype(BF)
            sent = sent + dot(spot, jnp.where(mark, value, 0.0).astype(BF), (0, 0))
    buffer[...] = sent.astype(BF)


def return_kernel(
    scalars, back, info, gates, entering, middle, rows, router, dy_own,
    d_middle, d_branch, wr_grad, gain_two,
):
    place = iota((128, 512), 1)
    wide = iota((128, WIDTH), 1)
    lane = iota((128, 128), 1)
    share = [gates[:, k : k + 1] for k in range(2)]
    d_entering = jnp.zeros((128, WIDTH), F32)
    d_gates = []
    for k in range(2):
        pick = jnp.where(place == info[:, k : k + 1], 1.0, 0.0).astype(BF)
        d_entering = d_entering + share[k] * dot(pick, back[...], (1, 0))
        at = info[:, 2 + k : 3 + k]
        spot = jnp.where((place == at) | (place == at + 1), 1.0, 0.0).astype(BF)
        d_gates.append(
            jnp.sum(
                jnp.where(wide == info[:, 4 + k : 5 + k], dot(spot, back[...], (1, 0)), 0.0),
                axis=1,
                keepdims=True,
            )
        )
    inner = share[0] * d_gates[0] + share[1] * d_gates[1]
    d_logits = jnp.zeros((128, 128), F32)
    for k in range(2):
        d_logits = d_logits + jnp.where(
            lane == info[:, 6 + k : 7 + k], share[k] * (d_gates[k] - inner), 0.0
        )
    d_logits = d_logits.astype(BF)
    d_entering = d_entering + dot(d_logits, router[...], (1, 1))
    wr_grad[...] = dot(entering[...], d_logits, (0, 0))
    values = middle[...]
    scale = lax.rsqrt(jnp.mean(values * values, axis=1, keepdims=True) + 1e-06)
    gain_two[...] = jnp.broadcast_to(
        jnp.sum(d_entering * values * scale, axis=0, keepdims=True), (8, WIDTH)
    )
    scaled = d_entering * rows[1:2, :]
    mean = jnp.mean(scaled * values, axis=1, keepdims=True)
    total = dy_own[...].astype(F32) + scale * scaled - values * scale * scale * scale * mean
    d_middle[...] = total
    d_branch[...] = total.astype(BF)


def gelu_parts(value):
    square = value * value
    bend = jnp.tanh(value * (GELU_IN + (GELU_IN * GELU_CUBE) * square))
    half = 0.5 + 0.5 * bend
    rise = value * (0.5 * GELU_IN + (1.5 * GELU_IN * GELU_CUBE) * square)
    return value * half, half + rise * (1.0 - bend * bend)


def pull_kernel(scalars, dy_rows, w_out, pulled, dy_all):
    tall = NEX * 6
    for n in range(2):
        for owner in range(NY):
            dy_all[n, owner * tall : owner * tall + tall, :] = dy_rows[
                owner, n * tall : n * tall + tall, :
            ]
        pulled[n] = dot(dy_all[n], w_out[n], (1, 1))


def expert_kernel(
    scalars, p0, p1, p2, p3a, p3b, pulled, w_in,
    o0, o1, o2, o3a, o3b, rows_all, active_all, d_raised_all, gate_all,
    rows, raised, d_raised,
):
    place = scalars[0]
    tall = NEX * 6
    wide_ones = jnp.ones((tall, 128), BF)
    extra_row = iota((16, tall), 0)
    eye = iota((tall, tall), 0) == iota((tall, tall), 1)
    starts = [
        pl.multiple_of(lax.rem(place + step, NY) * tall, tall) for step in (0, 3, 1, 2)
    ]
    for n in range(2):
        part = slice(n * tall, n * tall + tall)
        for spot in range(4):
            here = slice(spot * tall, spot * tall + tall)
            if spot < 3:
                rows[here, :] = (p0, p1, p2)[spot][part, :]
            elif n == 0:
                rows[here, :] = p3a[0:tall, :]
            else:
                rows[spot * tall : spot * tall + 16, :] = p3a[tall : tall + 16, :]
                rows[spot * tall + 16 : spot * tall + tall, :] = p3b[0 : tall - 16, :]
            rows_all[n, pl.ds(starts[spot], tall), :] = rows[here, :]
        raised[...] = dot(rows[...], w_in[n], (1, 0))
        for spot in range(4):
            here = slice(spot * tall, spot * tall + tall)
            there = pl.ds(starts[spot], tall)
            gate = p3b[tall - 16 : tall, part] if spot == 3 else (p0, p1, p2)[spot][384:400, part]
            gate = gate.astype(F32)
            gate_col = dot(jnp.where(eye, gate[0:1, :], 0.0).astype(BF), wide_ones, (1, 0))
            gate_col = gate_col + dot(
                jnp.where(eye, gate[1:2, :], 0.0).astype(BF), wide_ones, (1, 0)
            )
            gate_all[n, there, :] = gate_col
            active, slope = gelu_parts(raised[here, :])
            active = active.astype(BF)
            active_all[n, there, :] = active
            pull = pulled[n, there, :]
            product = active.astype(F32) * pull
            change = slope * pull
            d_raised[here, :] = change.astype(BF)
            d_raised_all[n, there, :] = (change * gate_col[:, 0:1]).astype(BF)
            d_gate = jnp.sum(product, axis=1, keepdims=True)
            d_gate = jnp.sum(jnp.where(eye, d_gate, 0.0), axis=0, keepdims=True)
            tail = (o0, o1, o2, o3b)[spot]
            last = tail.shape[0] - 16
            if n == 0:
                tail[last:, 384:WIDTH] = jnp.zeros((16, WIDTH - 384), BF)
            tail[last:, part] = jnp.where(extra_row == 0, d_gate, 0.0).astype(BF)
        raised[...] = dot(d_raised[...], w_in[n], (1, 1))
        for spot in range(3):
            (o0, o1, o2)[spot][part, :] = raised[spot * tall : spot * tall + tall, :].astype(BF)
        final = raised[3 * tall : 4 * tall, :].astype(BF)
        if n == 0:
            o3a[0:tall, :] = final
        else:
            o3a[tall : tall + 16, :] = final[0:16, :]
            o3b[0 : tall - 16, :] = final[16:tall, :]


def expert_rows(scalars, pieces, pulled, w_in):
    square = ((2, WIDTH, WIDTH), BF)
    outs = [((400, WIDTH), BF)] * 3 + [((208, WIDTH), BF), ((192, WIDTH), BF)]
    outs = outs + [square] * 3 + [((2, WIDTH, 128), F32)]
    whole = (WIDTH, WIDTH)
    scratch = [(whole, BF), (whole, F32), (whole, BF)]
    return vmem_call(expert_kernel, outs, scratch, scalars, *pieces, pulled, w_in)


def prepare_kernel(scalars, wqkv, wr, gain_one, gain_two, rel_bias, o0, o1, o2, o3):
    place = scalars[0]
    lane = iota((6, 128), 1)
    own = iota((6, 6), 0) == iota((6, 6), 1)
    one = jnp.sum(jnp.where(own, gain_one[...].astype(F32), 0.0), axis=1, keepdims=True)
    two = jnp.sum(jnp.where(own, gain_two[...].astype(F32), 0.0), axis=1, keepdims=True)
    bias = jnp.sum(jnp.where(own, rel_bias[...].astype(F32), 0.0), axis=1, keepdims=True)
    small = jnp.concatenate([wr[...].astype(F32), jnp.zeros((6, 64), F32)], axis=1)
    small = jnp.where(
        lane == 64, one, jnp.where(lane == 65, two, jnp.where(lane == 66, bias, small))
    ).astype(BF)
    values = wqkv[...].astype(F32)
    for step, out in zip((0, 3, 1, 2), (o0, o1, o2, o3)):
        owner = lax.rem(place + step, NY)
        out[:, 576:704] = small
        for part in range(3):
            taken = jnp.zeros((6, 192), F32)
            for group in range(NY):
                at = part * WIDTH + group * 192
                taken = taken + jnp.where(owner == group, 1.0, 0.0) * values[:, at : at + 192]
            out[:, part * 192 : part * 192 + 192] = taken.astype(BF)


def pack_kernel(scalars, p0, p1, p2, p3, wo, out):
    row = iota((24, 6), 0)
    col = iota((24, 6), 1)
    total = jnp.zeros((24, 704), F32)
    for spot, piece in enumerate((p0, p1, p2, p3)):
        total = total + dot(jnp.where(row == spot * 6 + col, 1.0, 0.0).astype(BF), piece[...], (1, 0))
    out[:, :704] = total.astype(BF)
    total = jnp.zeros((24, 192), F32)
    for part in range(4):
        spot = jnp.where(row == col * 4 + part, 1.0, 0.0).astype(BF)
        total = total + dot(spot, wo[:, part * 192 : part * 192 + 192], (1, 0))
    out[:, 704:896] = total.astype(BF)


def sum_kernel(scalars, terms, wo_out, o0, o1, o2, o3):
    place = scalars[0]
    total = jnp.sum(terms[...].astype(F32), axis=0)
    for part in range(4):
        spot = jnp.where(iota((6, 24), 1) == iota((6, 24), 0) * 4 + part, 1.0, 0.0)
        wo_out[:, part * 192 : part * 192 + 192] = lax.dot_general(
            spot,
            total[:, 704:896],
            (((1,), (0,)), ((), ())),
            precision=lax.Precision.HIGHEST,
            preferred_element_type=F32,
        )
    for step, out in zip((0, 3, 1, 2), (o0, o1, o2, o3)):
        owner = lax.rem(place + step, NY)
        taken = jnp.zeros((6, 704), F32)
        for group in range(NY):
            taken = taken + jnp.where(owner == group, 1.0, 0.0) * total[
                group * 6 : group * 6 + 6, :704
            ]
        out[...] = taken


def finish_kernel(scalars, p0, p1, p2, p3, wqkv_out, wr_out, one_out, two_out, bias_out):
    place = scalars[0]
    pieces = (p0, p1, p2, p3)
    for part in range(3):
        for group in range(NY):
            taken = jnp.zeros((6, 192), F32)
            for step, piece in zip((0, 1, 3, 2), pieces):
                owner = lax.rem(place + step, NY)
                taken = taken + jnp.where(owner == group, 1.0, 0.0) * piece[
                    :, part * 192 : part * 192 + 192
                ]
            at = part * WIDTH + group * 192
            wqkv_out[:, at : at + 192] = taken
    small = p0[:, 576:704] + p1[:, 576:704] + p2[:, 576:704] + p3[:, 576:704]
    wr_out[...] = small[:, :64]
    for lane, out in ((64, one_out), (65, two_out), (66, bias_out)):
        shape = (6, out.shape[1])
        mark = iota(shape, 0) == iota(shape, 1)
        out[...] = jnp.sum(
            jnp.where(mark, small[:, lane : lane + 1], 0.0), axis=0, keepdims=True
        )


def middle_step(scalars, pieces, x_own, rows, weights, info):
    outs = [((128, WIDTH), F32), ((128, WIDTH), BF), ((128, 128), F32), ((512, WIDTH), BF)]
    return vmem_call(middle_kernel, outs, [], scalars, *pieces, x_own, rows, weights, info)


def return_step(scalars, back, info, gates, entering, middle, rows, weights, dy_own):
    outs = [((128, WIDTH), F32), ((128, WIDTH), BF), ((WIDTH, 128), F32), ((8, WIDTH), F32)]
    return vmem_call(
        return_kernel, outs, [], scalars, back, info, gates, entering, middle, rows, weights, dy_own
    )


def gather_four(piece, axis):
    return [piece] + [lax.ppermute(piece, axis, way) for way in (UP, DOWN, ACROSS)]


def owner_at(step, axis):
    shift = jnp.where(step == 1, 3, jnp.where(step == 2, 1, jnp.where(step == 3, 2, 0)))
    return (lax.axis_index(axis) + shift) % 4


def exchange_y(pieces):
    ways = (DOWN, UP, ACROSS)
    return [pieces[0]] + [lax.ppermute(piece, "y", way) for piece, way in zip(pieces[1:], ways)]


def ring_gather(piece, cut):
    below = lax.ppermute(piece, "y", UP)
    above = lax.ppermute(piece, "y", DOWN)
    first = lax.ppermute(below[:cut], "y", UP)
    second = lax.ppermute(above[cut:], "y", DOWN)
    return piece, below, above, first, second


def ring_scatter(pieces, cut):
    own, below, above, across_first, across_second = pieces
    first = lax.ppermute(across_first, "y", UP)
    second = lax.ppermute(across_second, "y", DOWN)
    up = jnp.concatenate(
        [(above[:cut].astype(F32) + first.astype(F32)).astype(BF), above[cut:]], axis=0
    )
    down = jnp.concatenate(
        [below[:cut], (below[cut:].astype(F32) + second.astype(F32)).astype(BF)], axis=0
    )
    from_below = lax.ppermute(up, "y", UP)
    from_above = lax.ppermute(down, "y", DOWN)
    total = own.astype(F32) + from_below.astype(F32) + from_above.astype(F32)
    return total, up


def mm(a, b):
    return lax.dot_general(a, b, (((1,), (0,)), ((), ())), preferred_element_type=F32)


def mm_tn(a, b):
    return lax.dot_general(a, b, (((0,), (0,)), ((), ())), preferred_element_type=F32)


def body(
    inputs, wqkv, wo, wr, gain_one, gain_two, rel_bias, w_in, w_out, routes, lengths, cotangent
):
    place = lax.axis_index("y")
    tokens = MB * TOK
    x_own = inputs.reshape(tokens, WIDTH)
    dy_own = cotangent.reshape(tokens, WIDTH)
    here = place[None].astype(jnp.int32)
    bounds = jnp.cumsum(lengths.reshape(MB, 3), axis=1)[:, :2].reshape(4)
    scalars = jnp.concatenate([here, bounds])
    x_pieces = gather_four(x_own, "y")
    bias_row = jnp.pad(rel_bias, (0, 3))[None]
    sides = vmem_call(
        prepare_kernel,
        [((6, 704), BF)] * 4,
        [],
        *(here, wqkv, wr, gain_one[None], gain_two[None], bias_row),
    )
    (pack,) = vmem_call(pack_kernel, [((24, 896), BF)], [], here, *exchange_y(sides), wo)
    packed = gather_four(jnp.concatenate(gather_four(pack, "x"), axis=0), "z")
    packed = packed + [lax.ppermute(piece, "c", [(0, 1), (1, 0)]) for piece in packed]
    dy_later, *packed = lax.optimization_barrier((dy_own, *packed))
    rows = jnp.arange(WIDTH, dtype=jnp.int32)
    step = rows // 24
    owner = owner_at(step // 4 % 4, "z") * 8 + owner_at(step % 4, "x") * 2
    owner = owner + (lax.axis_index("c") + step // 16) % 2
    in_chunk = rows % 24
    source = in_chunk // 6
    source = (place + jnp.where(source == 2, 3, jnp.where(source == 3, 2, source))) % NY
    nat_row = jnp.broadcast_to(((source * NEX + owner) * 6 + in_chunk % 6)[None], (8, WIDTH))
    wo_row = jnp.broadcast_to((owner * 24 + in_chunk)[None], (8, WIDTH))
    route = routes.reshape(MB, 2 * TOK)
    flat = jnp.arange(2 * TOK, dtype=jnp.int32)
    same = (route[:, :, None] == route[:, None, :]) & (flat[:, None] > flat[None, :])[None]
    slot = jnp.sum(same.astype(jnp.int32), axis=2)
    slot = (slot + jnp.arange(MB, dtype=jnp.int32)[:, None] * CAP).reshape(tokens, 2)
    route = route.reshape(tokens, 2)
    side = route % 2
    dest = (route // 2) * 16
    me = lax.axis_index(EX)
    info = jnp.concatenate(
        [dest + side * 6 + slot, dest + 12, side * 192 + me * 6 + slot, route], axis=1
    )
    buffer_rows = jnp.arange(512, dtype=jnp.int32)
    pick = [(buffer_rows[None, :] == info[:, k : k + 1]).astype(BF) for k in range(2)]
    slots = jnp.arange(400, dtype=jnp.int32)
    buffer_of = (slots // 6 % NEX) * 16 + (slots // 192) * 6 + slots % 6
    compact = jnp.where(
        slots[:, None] < 384,
        buffer_of[:, None] == buffer_rows[None, :],
        (buffer_rows % 16)[None, :] == 12 + slots[:, None] - 384,
    )
    compact = (compact & (slots < 386)[:, None]).astype(BF)

    def to_experts(buffer):
        return lax.all_to_all(buffer.reshape(NEX, 16, WIDTH), EX, 0, 0).reshape(512, WIDTH)

    dy_rows = mm(compact[:384], to_experts(mm_tn(pick[0] + pick[1], dy_later).astype(BF)))
    kept = attention_forward(scalars, nat_row, wo_row, x_pieces, packed)
    branch, saved, router, gain_rows = kept[:4], kept[4:10], kept[10], kept[11]
    weights = saved[3]
    branch = exchange_y(branch)
    dy_rows, *branch = lax.optimization_barrier((dy_rows.astype(BF), *branch))
    dy_rows = lax.all_gather(dy_rows, "y")
    middle, entering, gates, buffer = middle_step(
        scalars, branch, x_own, gain_rows, router, info
    )
    arrived = mm(compact, to_experts(buffer)).astype(BF)
    pulled, dy_all = vmem_call(
        pull_kernel, [((2, WIDTH, WIDTH), F32), ((2, WIDTH, WIDTH), BF)], [], here, dy_rows, w_out
    )
    results = expert_rows(scalars, ring_gather(arrived, 208), pulled, w_in)
    d_arrived, (rows_all, active, d_raised, gate_all) = results[:5], results[5:]
    d_home, in_flight = ring_scatter(d_arrived, 208)
    d_home_high = d_home.astype(BF)
    d_home_low = (d_home[384:385] - d_home_high[384:385].astype(F32)).astype(BF)
    d_home = jnp.where(
        (slots == 385)[:, None], d_home_low, d_home_high
    )
    back = to_experts(mm_tn(compact, d_home).astype(BF))
    active, _ = lax.optimization_barrier((active, in_flight))
    result = jnp.einsum("erf,efd->erd", active, w_out, preferred_element_type=F32).astype(BF)
    result = result.reshape(2, NY, 192, WIDTH).transpose(1, 0, 2, 3).reshape(NY, 384, WIDTH)
    result, _ = lax.optimization_barrier((result, d_home))
    result = lax.psum_scatter(result, "y", scatter_dimension=0)
    grad_in = jnp.einsum("erd,erf->edf", rows_all, d_raised, preferred_element_type=F32)
    d_returned = (dy_all.astype(F32) * gate_all[:, :, :1]).astype(BF)
    grad_out = jnp.einsum("erf,erd->efd", active, d_returned, preferred_element_type=F32)
    back, grad_in, grad_out = lax.optimization_barrier((back, grad_in, grad_out))
    d_middle, d_branch, wr_grad, gain_two_grad = return_step(
        scalars, back, info, gates, entering, middle, gain_rows, router, dy_own
    )
    d_pieces = gather_four(d_branch, "y")
    back_result = mm_tn(compact[:384], result).astype(BF)
    back_result, *d_pieces = lax.optimization_barrier((back_result, *d_pieces))
    returned = to_experts(back_result)
    mixture = sum(gates[:, k : k + 1] * mm(pick[k], returned) for k in range(2))
    output = (middle + mixture).astype(BF)
    ended = attention_backward(
        scalars, d_pieces, saved, wr_grad, gain_two_grad
    )
    pieces = vmem_call(
        normed_kernel,
        [((128, WIDTH), BF)] * 4,
        [((MB * SPAN, WIDTH), F32)],
        *(scalars, ended[1], weights),
    )
    terms = lax.all_to_all(ended[0].reshape(NEX, 24, 896), EX, 0, 0)
    d_normed = sum(piece.astype(F32) for piece in exchange_y(pieces))
    x = x_own.astype(F32)
    scale = lax.rsqrt(jnp.mean(x * x, axis=1, keepdims=True) + 1e-06)
    scaled = d_normed * gain_rows[0:1]
    inner = jnp.mean(scaled * x, axis=1, keepdims=True)
    input_grad = d_middle + scale * scaled - x * scale**3 * inner
    shape = (6, 704)
    wo_out, *sums = vmem_call(
        sum_kernel, [((6, WIDTH), F32)] + [(shape, F32)] * 4, [], here, terms
    )
    wqkv_out, wr_out, one_out, two_out, bias_out = vmem_call(
        finish_kernel,
        [((6, 2304), F32), ((6, 64), F32), ((1, 6), F32), ((1, 6), F32), ((1, 3), F32)],
        [],
        here,
        *exchange_y(sums),
    )
    return (
        output.reshape(MB, 1, TOK, WIDTH),
        input_grad.reshape(MB, 1, TOK, WIDTH),
        wqkv_out,
        wo_out,
        wr_out,
        one_out[0],
        two_out[0],
        bias_out[0],
        grad_in,
        grad_out,
    )


def solution(mesh):
    grid = Mesh(mesh.devices.reshape(NY, 4, 4, 2), ("y", "z", "x", "c"))
    every = ("y",) + EX
    in_specs = (
        P(None, EX, "y", None),
        P(every, None),
        P(every, None),
        P(every, None),
        P(every),
        P(every),
        P(every),
        P(EX, None, "y"),
        P(EX, "y", None),
        P(None, EX, "y", None),
        P(None, EX, None),
        P(None, EX, "y", None),
    )
    out_specs = (
        P(None, EX, "y", None),
        P(None, EX, "y", None),
        P(every, None),
        P(every, None),
        P(every, None),
        P(every),
        P(every),
        P(every),
        P(EX, None, "y"),
        P(EX, "y", None),
    )
    return jax.shard_map(body, mesh=grid, in_specs=in_specs, out_specs=out_specs, check_vma=False)
```

```python
import functools
import math

import jax
import jax.numpy as jnp
from jax import lax
from jax.experimental import pallas as pl
from jax.experimental.pallas import tpu as pltpu
from jax.sharding import Mesh
from jax.sharding import PartitionSpec as P

HEADS = 12
HEAD_DIM = 64
BUCKETS = 32
CAP = 3
FAR_STEP = 6
WIDTH = 768
TOK = 64
MB = 2
NY = 4
NEX = 32
HG = HEADS // NY
SPAN = TOK * NY
SCORE_SCALE = 1.0 / math.sqrt(HEAD_DIM)
EX = ("z", "x", "c")
F32 = jnp.float32
BF = jnp.bfloat16
GELU_IN = math.sqrt(2.0 / math.pi)
GELU_CUBE = 0.044715

UP = [(i, (i + 1) % NY) for i in range(NY)]
DOWN = [(i, (i - 1) % NY) for i in range(NY)]
ACROSS = [(i, (i + 2) % NY) for i in range(NY)]


def dot(a, b, dims):
    return lax.dot_general(a, b, ((dims[:1], dims[1:]), ((), ())), preferred_element_type=F32)


def iota(shape, dim):
    return lax.broadcasted_iota(jnp.int32, shape, dim)


def bucket_of(gap):
    far = 16 + (jnp.maximum(gap - 16, 0) * 171) // 1024
    return jnp.where(gap < 16, gap, jnp.minimum(BUCKETS - 1, far))


def table_marks(place, head):
    shape = (WIDTH, SPAN)
    row = iota(shape, 0)
    owner = row // 6
    entry = 3 * (owner - NEX * place) + row - 6 * owner
    wanted = head * BUCKETS + bucket_of(iota(shape, 1))
    return jnp.where((row - 6 * owner < 3) & (entry == wanted), 1.0, 0.0).astype(BF)


def place_rows(pieces, place, target):
    for step, piece in zip((0, 3, 1, 2), pieces):
        start = lax.rem(place + step, NY) * TOK
        for m in range(MB):
            target[pl.ds(pl.multiple_of(m * SPAN + start, TOK), TOK), :] = piece[
                m * TOK : (m + 1) * TOK, :
            ]


def take_rows(pieces, place, source):
    for step, piece in zip((0, 3, 1, 2), pieces):
        start = lax.rem(place + step, NY) * TOK
        for m in range(MB):
            piece[m * TOK : (m + 1) * TOK, :] = source[
                pl.ds(pl.multiple_of(m * SPAN + start, TOK), TOK), :
            ].astype(piece.dtype)


def forward_kernel(
    scalars, nat_row, wo_row, x0, x1, x2, x3, q0, q1, q2, q3, q4, q5, q6, q7,
    b0, b1, b2, b3, qkv, probs, mixed, weights, wo_heads, normed, router, rows,
    x_all, bias, branch, packed,
):
    place = scalars[0]
    place_rows((x0, x1, x2, x3), place, x_all)
    for spot, piece in enumerate((q0, q1, q2, q3, q4, q5, q6, q7)):
        packed[spot * 96 : spot * 96 + 96, :] = piece[...]
    row = iota((WIDTH, WIDTH), 0)
    perm = jnp.where(row == nat_row[0:1, :], 1.0, 0.0).astype(BF)
    weights[...] = dot(perm, packed[:, :704], (1, 0)).astype(BF)
    router[...] = weights[:, 576:704]
    for part in range(4):
        choose = jnp.where(iota((192, WIDTH), 0) * 4 + part == wo_row[0:1, :], 1.0, 0.0).astype(BF)
        wo_heads[:, part * 192 : part * 192 + 192] = dot(
            choose, packed[:, 704:896], (1, 0)
        ).astype(BF)
    lane_of = jnp.where(iota((8, 128), 1) == iota((8, 128), 0) + 64, 1.0, 0.0).astype(BF)
    rows[...] = dot(lane_of, weights[:, 576:704], (1, 1))
    values = x_all[...].astype(F32)
    scale = lax.rsqrt(jnp.mean(values * values, axis=1, keepdims=True) + 1e-06)
    normed[...] = (values * scale * rows[0:1, :]).astype(BF)
    qkv[...] = dot(normed[...], weights[:, :576], (1, 0)).astype(BF)
    table = rows[...].astype(BF)
    for head in range(HG):
        mirrored = dot(table, table_marks(place, head), (1, 0))[2:3, :]
        flip = jnp.where(iota((SPAN, SPAN), 0) + iota((SPAN, SPAN), 1) == SPAN - 1, 1.0, 0.0)
        mirrored = dot(jnp.broadcast_to(mirrored, (8, SPAN)).astype(BF), flip.astype(BF), (1, 0))
        spread = jnp.broadcast_to(mirrored[0:1, :], (SPAN, SPAN))
        bias[head] = pltpu.roll(spread, 1, 1, stride=1, stride_axis=0)
    query = iota((SPAN, SPAN), 0)
    key = iota((SPAN, SPAN), 1)
    for m in range(MB):
        first = scalars[1 + 2 * m]
        second = scalars[2 + 2 * m]
        of_query = jnp.where(query >= first, 1, 0) + jnp.where(query >= second, 1, 0)
        of_key = jnp.where(key >= first, 1, 0) + jnp.where(key >= second, 1, 0)
        seen = (of_query == of_key) & (query >= key)
        part = slice(m * SPAN, (m + 1) * SPAN)
        for head in range(HG):
            at = head * HEAD_DIM
            raw = dot(
                qkv[part, at : at + HEAD_DIM], qkv[part, 192 + at : 192 + at + HEAD_DIM], (1, 1)
            )
            scores = jnp.where(seen, raw * SCORE_SCALE + bias[head], -1000000000.0)
            peak = jnp.max(scores, axis=1, keepdims=True)
            powers = jnp.exp(scores - peak)
            share = powers / jnp.sum(powers, axis=1, keepdims=True)
            probs[m * HG + head] = share
            mixed[part, at : at + HEAD_DIM] = dot(
                share.astype(BF), qkv[part, 384 + at : 384 + at + HEAD_DIM], (1, 0)
            ).astype(BF)
    branch[...] = dot(mixed[...], wo_heads[...], (1, 0))
    take_rows((b0, b1, b2, b3), place, branch)


def backward_kernel(
    scalars, d0, d1, d2, d3, qkv, probs, mixed, weights, wo_heads, normed, wr_grad, gain_two,
    grads, d_qkv, d_branch, d_mixed, d_bias,
):
    place = scalars[0]
    place_rows((d0, d1, d2, d3), place, d_branch)
    grad_wo = dot(mixed[...], d_branch[...], (0, 0)).astype(BF)
    packed_wo = jnp.zeros((WIDTH, 192), F32)
    for part in range(4):
        choose = jnp.where(iota((WIDTH, 192), 1) * 4 + part == iota((WIDTH, 192), 0), 1.0, 0.0)
        packed_wo = packed_wo + dot(
            choose.astype(BF), grad_wo[:, part * 192 : part * 192 + 192], (1, 0)
        )
    grads[:, 704:896] = packed_wo.astype(BF)
    d_mixed[...] = dot(d_branch[...], wo_heads[...], (1, 1)).astype(BF)
    for m in range(MB):
        part = slice(m * SPAN, (m + 1) * SPAN)
        for head in range(HG):
            at = head * HEAD_DIM
            lanes = slice(at, at + HEAD_DIM)
            share = probs[m * HG + head]
            d_mixed_head = d_mixed[part, lanes]
            d_probs = dot(d_mixed_head, qkv[part, 384 + at : 384 + at + HEAD_DIM], (1, 1))
            d_qkv[part, 384 + at : 384 + at + HEAD_DIM] = dot(
                share.astype(BF), d_mixed_head, (0, 0)
            ).astype(BF)
            inner = jnp.sum(share * d_probs, axis=1, keepdims=True)
            d_scores = share * (d_probs - inner)
            if m == 0:
                d_bias[head] = d_scores
            else:
                d_bias[head] = d_bias[head] + d_scores
            d_raw = (d_scores * SCORE_SCALE).astype(BF)
            d_qkv[part, lanes] = dot(
                d_raw, qkv[part, 192 + at : 192 + at + HEAD_DIM], (1, 0)
            ).astype(BF)
            d_qkv[part, 192 + at : 192 + at + HEAD_DIM] = dot(
                d_raw, qkv[part, lanes], (0, 0)
            ).astype(BF)
    flip = jnp.where(iota((SPAN, SPAN), 0) + iota((SPAN, SPAN), 1) == SPAN - 1, 1.0, 0.0).astype(BF)
    table = jnp.zeros((8, WIDTH), F32)
    for head in range(HG):
        total = d_bias[head]
        high = total.astype(BF)
        low = (total - high.astype(F32)).astype(BF)
        turned = dot(flip, high, (1, 0)) + dot(flip, low, (1, 0))
        skewed = pltpu.roll(turned, 0, 1, stride=1, stride_axis=0)
        diagonal = jnp.broadcast_to(jnp.sum(skewed, axis=0, keepdims=True), (8, SPAN))
        high = diagonal.astype(BF)
        low = (diagonal - high.astype(F32)).astype(BF)
        by_gap = dot(high, flip, (1, 0)) + dot(low, flip, (1, 0))
        marks = table_marks(place, head)
        high = by_gap.astype(BF)
        low = (by_gap - high.astype(F32)).astype(BF)
        table = table + dot(high, marks, (1, 1)) + dot(low, marks, (1, 1))
    which = iota((8, WIDTH), 0)
    rows = jnp.where(which == 1, gain_two[0:1, :], jnp.where(which == 2, table, 0.0))
    lane_of = jnp.where(iota((8, 128), 1) == iota((8, 128), 0) + 64, 1.0, 0.0).astype(BF)
    grad_heads = dot(normed[...], d_qkv[...], (0, 0))
    gain_one = jnp.sum(grad_heads * weights[:, :576].astype(F32), axis=1, keepdims=True)
    gain_one = gain_one / weights[:, 640:641].astype(F32)
    small = wr_grad[...] + dot(rows.astype(BF), lane_of, (0, 0))
    small = small + jnp.where(iota((WIDTH, 128), 1) == 64, gain_one, 0.0)
    row = iota((WIDTH, WIDTH), 0)
    col = iota((WIDTH, WIDTH), 1)
    chunk = row // 24
    rest = row - 24 * chunk
    group = rest // 6
    wanted = (group * NEX + chunk) * 6 + rest - 6 * group
    perm = jnp.where(col == wanted, 1.0, 0.0).astype(BF)
    grads[:, :576] = dot(perm, grad_heads.astype(BF), (1, 0)).astype(BF)
    grads[:, 576:704] = dot(perm, small.astype(BF), (1, 0)).astype(BF)


def normed_kernel(scalars, d_qkv, weights, n0, n1, n2, n3, d_normed):
    d_normed[...] = dot(d_qkv[...], weights[:, :576], (1, 1))
    take_rows((n0, n1, n2, n3), scalars[0], d_normed)


def vmem_call(kernel, outs, scratch, *args):
    full = pl.BlockSpec()
    return pl.pallas_call(
        kernel,
        out_shape=[jax.ShapeDtypeStruct(shape, kind) for shape, kind in outs],
        in_specs=[pl.BlockSpec(memory_space=pltpu.SMEM)] + [full] * (len(args) - 1),
        out_specs=[full] * len(outs),
        scratch_shapes=[pltpu.VMEM(shape, kind) for shape, kind in scratch],
        compiler_params=pltpu.CompilerParams(vmem_limit_bytes=60 * 1024 * 1024),
    )(*args)


def attention_forward(scalars, nat_row, wo_row, x_pieces, packed):
    rows = MB * SPAN
    outs = [((128, WIDTH), BF)] * 4 + [
        ((rows, 576), BF),
        ((MB * HG, SPAN, SPAN), F32),
        ((rows, 192), BF),
        ((WIDTH, 704), BF),
        ((192, WIDTH), BF),
        ((rows, WIDTH), BF),
        ((WIDTH, 128), BF),
        ((8, WIDTH), F32),
    ]
    scratch = [((rows, WIDTH), BF), ((HG, SPAN, SPAN), F32), ((rows, WIDTH), F32), ((WIDTH, 896), BF)]
    return vmem_call(forward_kernel, outs, scratch, scalars, nat_row, wo_row, *x_pieces, *packed)


def attention_backward(scalars, d_pieces, kept, wr_grad, gain_two):
    rows = MB * SPAN
    outs = [((WIDTH, 896), BF), ((rows, 576), BF)]
    scratch = [((rows, WIDTH), BF), ((rows, 192), BF), ((HG, SPAN, SPAN), F32)]
    return vmem_call(backward_kernel, outs, scratch, scalars, *d_pieces, *kept, wr_grad, gain_two)


def middle_kernel(
    scalars, b0, b1, b2, b3, x_own, rows, router, info, middle, entering, gates, buffer
):
    values = x_own[...].astype(F32) + (
        (b0[...].astype(F32) + b1[...].astype(F32)) + (b2[...].astype(F32) + b3[...].astype(F32))
    )
    middle[...] = values
    scale = lax.rsqrt(jnp.mean(values * values, axis=1, keepdims=True) + 1e-06)
    low = (values * scale * rows[1:2, :]).astype(BF)
    entering[...] = low
    logits = dot(low, router[...], (1, 0))
    lane = iota((128, 128), 1)
    chosen = [
        jnp.sum(jnp.where(lane == info[:, 6 + k : 7 + k], logits, 0.0), axis=1, keepdims=True)
        for k in range(2)
    ]
    peak = jnp.maximum(chosen[0], chosen[1])
    powers = [jnp.exp(value - peak) for value in chosen]
    total = powers[0] + powers[1]
    share = [power / total for power in powers]
    gates[...] = jnp.where(lane == 0, share[0], jnp.where(lane == 1, share[1], 0.0))
    place = iota((128, 512), 1)
    wide = iota((128, WIDTH), 1)
    pick = jnp.where(
        (place == info[:, 0:1]) | (place == info[:, 1:2]), 1.0, 0.0
    ).astype(BF)
    sent = dot(pick, low, (0, 0))
    for k in range(2):
        mark = wide == info[:, 4 + k : 5 + k]
        high = share[k].astype(BF).astype(F32)
        rest = share[k] - high
        for at, value in ((0, high), (1, rest)):
            spot = jnp.where(place == info[:, 2 + k : 3 + k] + at, 1.0, 0.0).astype(BF)
            sent = sent + dot(spot, jnp.where(mark, value, 0.0).astype(BF), (0, 0))
    buffer[...] = sent.astype(BF)


def return_kernel(
    scalars, back, info, gates, entering, middle, rows, router, dy_own,
    d_middle, d_branch, wr_grad, gain_two,
):
    place = iota((128, 512), 1)
    wide = iota((128, WIDTH), 1)
    lane = iota((128, 128), 1)
    share = [gates[:, k : k + 1] for k in range(2)]
    d_entering = jnp.zeros((128, WIDTH), F32)
    d_gates = []
    for k in range(2):
        pick = jnp.where(place == info[:, k : k + 1], 1.0, 0.0).astype(BF)
        d_entering = d_entering + share[k] * dot(pick, back[...], (1, 0))
        at = info[:, 2 + k : 3 + k]
        spot = jnp.where((place == at) | (place == at + 1), 1.0, 0.0).astype(BF)
        d_gates.append(
            jnp.sum(
                jnp.where(wide == info[:, 4 + k : 5 + k], dot(spot, back[...], (1, 0)), 0.0),
                axis=1,
                keepdims=True,
            )
        )
    inner = share[0] * d_gates[0] + share[1] * d_gates[1]
    d_logits = jnp.zeros((128, 128), F32)
    for k in range(2):
        d_logits = d_logits + jnp.where(
            lane == info[:, 6 + k : 7 + k], share[k] * (d_gates[k] - inner), 0.0
        )
    d_logits = d_logits.astype(BF)
    d_entering = d_entering + dot(d_logits, router[...], (1, 1))
    wr_grad[...] = dot(entering[...], d_logits, (0, 0))
    values = middle[...]
    scale = lax.rsqrt(jnp.mean(values * values, axis=1, keepdims=True) + 1e-06)
    gain_two[...] = jnp.broadcast_to(
        jnp.sum(d_entering * values * scale, axis=0, keepdims=True), (8, WIDTH)
    )
    scaled = d_entering * rows[1:2, :]
    mean = jnp.mean(scaled * values, axis=1, keepdims=True)
    total = dy_own[...].astype(F32) + scale * scaled - values * scale * scale * scale * mean
    d_middle[...] = total
    d_branch[...] = total.astype(BF)


def gelu_parts(value):
    square = value * value
    bend = jnp.tanh(value * (GELU_IN + (GELU_IN * GELU_CUBE) * square))
    half = 0.5 + 0.5 * bend
    rise = value * (0.5 * GELU_IN + (1.5 * GELU_IN * GELU_CUBE) * square)
    return value * half, half + rise * (1.0 - bend * bend)


def pull_kernel(scalars, dy_rows, w_out, pulled, dy_all):
    tall = NEX * 6
    for n in range(2):
        for owner in range(NY):
            dy_all[n, owner * tall : owner * tall + tall, :] = dy_rows[
                owner, n * tall : n * tall + tall, :
            ]
        pulled[n] = dot(dy_all[n], w_out[n], (1, 1))


def expert_kernel(
    scalars, p0, p1, p2, p3a, p3b, pulled, w_in,
    o0, o1, o2, o3a, o3b, rows_all, active_all, d_raised_all, gate_all,
    rows, raised, d_raised,
):
    place = scalars[0]
    tall = NEX * 6
    wide_ones = jnp.ones((tall, 128), BF)
    extra_row = iota((16, tall), 0)
    eye = iota((tall, tall), 0) == iota((tall, tall), 1)
    starts = [
        pl.multiple_of(lax.rem(place + step, NY) * tall, tall) for step in (0, 3, 1, 2)
    ]

    def expert(n):
        part = slice(n * tall, n * tall + tall)
        for spot in range(4):
            here = slice(spot * tall, spot * tall + tall)
            if spot < 3:
                rows[here, :] = (p0, p1, p2)[spot][part, :]
            elif n == 0:
                rows[here, :] = p3a[0:tall, :]
            else:
                rows[spot * tall : spot * tall + 16, :] = p3a[tall : tall + 16, :]
                rows[spot * tall + 16 : spot * tall + tall, :] = p3b[0 : tall - 16, :]
            rows_all[0, pl.ds(starts[spot], tall), :] = rows[here, :]
        raised[...] = dot(rows[...], w_in[0], (1, 0))
        for spot in range(4):
            here = slice(spot * tall, spot * tall + tall)
            there = pl.ds(starts[spot], tall)
            gate = p3b[tall - 16 : tall, part] if spot == 3 else (p0, p1, p2)[spot][384:400, part]
            gate = gate.astype(F32)
            gate_col = dot(jnp.where(eye, gate[0:1, :], 0.0).astype(BF), wide_ones, (1, 0))
            gate_col = gate_col + dot(
                jnp.where(eye, gate[1:2, :], 0.0).astype(BF), wide_ones, (1, 0)
            )
            gate_all[0, there, :] = gate_col
            active, slope = gelu_parts(raised[here, :])
            active = active.astype(BF)
            active_all[0, there, :] = active
            pull = pulled[0, there, :]
            product = active.astype(F32) * pull
            change = slope * pull
            d_raised[here, :] = change.astype(BF)
            d_raised_all[0, there, :] = (change * gate_col[:, 0:1]).astype(BF)
            d_gate = jnp.sum(product, axis=1, keepdims=True)
            d_gate = jnp.sum(jnp.where(eye, d_gate, 0.0), axis=0, keepdims=True)
            tail = (o0, o1, o2, o3b)[spot]
            last = tail.shape[0] - 16
            if n == 0:
                tail[last:, 384:WIDTH] = jnp.zeros((16, WIDTH - 384), BF)
            tail[last:, part] = jnp.where(extra_row == 0, d_gate, 0.0).astype(BF)
        raised[...] = dot(d_raised[...], w_in[0], (1, 1))
        for spot in range(3):
            (o0, o1, o2)[spot][part, :] = raised[spot * tall : spot * tall + tall, :].astype(BF)
        final = raised[3 * tall : 4 * tall, :].astype(BF)
        if n == 0:
            o3a[0:tall, :] = final
        else:
            o3a[tall : tall + 16, :] = final[0:16, :]
            o3b[0 : tall - 16, :] = final[16:tall, :]

    for n in range(2):
        pl.when(pl.program_id(0) == n)(functools.partial(expert, n))


def expert_rows(scalars, pieces, pulled, w_in):
    square = ((2, WIDTH, WIDTH), BF)
    outs = [((400, WIDTH), BF)] * 3 + [((208, WIDTH), BF), ((192, WIDTH), BF)]
    outs = outs + [square] * 3 + [((2, WIDTH, 128), F32)]
    whole = (WIDTH, WIDTH)

    def spec(shape):
        if len(shape) == 3:
            return pl.BlockSpec((1,) + shape[1:], lambda n: (n, 0, 0))
        return pl.BlockSpec(shape, lambda n: (0, 0))

    args = (*pieces, pulled, w_in)
    return pl.pallas_call(
        expert_kernel,
        grid=(2,),
        out_shape=[jax.ShapeDtypeStruct(shape, kind) for shape, kind in outs],
        in_specs=[pl.BlockSpec(memory_space=pltpu.SMEM)] + [spec(arg.shape) for arg in args],
        out_specs=[spec(shape) for shape, _ in outs],
        scratch_shapes=[pltpu.VMEM(whole, BF), pltpu.VMEM(whole, F32), pltpu.VMEM(whole, BF)],
        compiler_params=pltpu.CompilerParams(vmem_limit_bytes=60 * 1024 * 1024),
    )(scalars, *args)


def prepare_kernel(scalars, wqkv, wr, gain_one, gain_two, rel_bias, o0, o1, o2, o3):
    place = scalars[0]
    lane = iota((6, 128), 1)
    own = iota((6, 6), 0) == iota((6, 6), 1)
    one = jnp.sum(jnp.where(own, gain_one[...].astype(F32), 0.0), axis=1, keepdims=True)
    two = jnp.sum(jnp.where(own, gain_two[...].astype(F32), 0.0), axis=1, keepdims=True)
    bias = jnp.sum(jnp.where(own, rel_bias[...].astype(F32), 0.0), axis=1, keepdims=True)
    small = jnp.concatenate([wr[...].astype(F32), jnp.zeros((6, 64), F32)], axis=1)
    small = jnp.where(
        lane == 64, one, jnp.where(lane == 65, two, jnp.where(lane == 66, bias, small))
    ).astype(BF)
    values = wqkv[...].astype(F32)
    for step, out in zip((0, 3, 1, 2), (o0, o1, o2, o3)):
        owner = lax.rem(place + step, NY)
        out[:, 576:704] = small
        for part in range(3):
            taken = jnp.zeros((6, 192), F32)
            for group in range(NY):
                at = part * WIDTH + group * 192
                taken = taken + jnp.where(owner == group, 1.0, 0.0) * values[:, at : at + 192]
            out[:, part * 192 : part * 192 + 192] = taken.astype(BF)


def pack_kernel(scalars, p0, p1, p2, p3, wo, out):
    row = iota((24, 6), 0)
    col = iota((24, 6), 1)
    total = jnp.zeros((24, 704), F32)
    for spot, piece in enumerate((p0, p1, p2, p3)):
        total = total + dot(jnp.where(row == spot * 6 + col, 1.0, 0.0).astype(BF), piece[...], (1, 0))
    out[:, :704] = total.astype(BF)
    total = jnp.zeros((24, 192), F32)
    for part in range(4):
        spot = jnp.where(row == col * 4 + part, 1.0, 0.0).astype(BF)
        total = total + dot(spot, wo[:, part * 192 : part * 192 + 192], (1, 0))
    out[:, 704:896] = total.astype(BF)


def sum_kernel(scalars, terms, wo_out, o0, o1, o2, o3):
    place = scalars[0]
    total = jnp.sum(terms[...].astype(F32), axis=0)
    for part in range(4):
        spot = jnp.where(iota((6, 24), 1) == iota((6, 24), 0) * 4 + part, 1.0, 0.0)
        wo_out[:, part * 192 : part * 192 + 192] = lax.dot_general(
            spot,
            total[:, 704:896],
            (((1,), (0,)), ((), ())),
            precision=lax.Precision.HIGHEST,
            preferred_element_type=F32,
        )
    for step, out in zip((0, 3, 1, 2), (o0, o1, o2, o3)):
        owner = lax.rem(place + step, NY)
        taken = jnp.zeros((6, 704), F32)
        for group in range(NY):
            taken = taken + jnp.where(owner == group, 1.0, 0.0) * total[
                group * 6 : group * 6 + 6, :704
            ]
        out[...] = taken


def finish_kernel(scalars, p0, p1, p2, p3, wqkv_out, wr_out, one_out, two_out, bias_out):
    place = scalars[0]
    pieces = (p0, p1, p2, p3)
    for part in range(3):
        for group in range(NY):
            taken = jnp.zeros((6, 192), F32)
            for step, piece in zip((0, 1, 3, 2), pieces):
                owner = lax.rem(place + step, NY)
                taken = taken + jnp.where(owner == group, 1.0, 0.0) * piece[
                    :, part * 192 : part * 192 + 192
                ]
            at = part * WIDTH + group * 192
            wqkv_out[:, at : at + 192] = taken
    small = p0[:, 576:704] + p1[:, 576:704] + p2[:, 576:704] + p3[:, 576:704]
    wr_out[...] = small[:, :64]
    for lane, out in ((64, one_out), (65, two_out), (66, bias_out)):
        shape = (6, out.shape[1])
        mark = iota(shape, 0) == iota(shape, 1)
        out[...] = jnp.sum(
            jnp.where(mark, small[:, lane : lane + 1], 0.0), axis=0, keepdims=True
        )


def middle_step(scalars, pieces, x_own, rows, weights, info):
    outs = [((128, WIDTH), F32), ((128, WIDTH), BF), ((128, 128), F32), ((512, WIDTH), BF)]
    return vmem_call(middle_kernel, outs, [], scalars, *pieces, x_own, rows, weights, info)


def return_step(scalars, back, info, gates, entering, middle, rows, weights, dy_own):
    outs = [((128, WIDTH), F32), ((128, WIDTH), BF), ((WIDTH, 128), F32), ((8, WIDTH), F32)]
    return vmem_call(
        return_kernel, outs, [], scalars, back, info, gates, entering, middle, rows, weights, dy_own
    )


def gather_four(piece, axis):
    return [piece] + [lax.ppermute(piece, axis, way) for way in (UP, DOWN, ACROSS)]


def owner_at(step, axis):
    shift = jnp.where(step == 1, 3, jnp.where(step == 2, 1, jnp.where(step == 3, 2, 0)))
    return (lax.axis_index(axis) + shift) % 4


def exchange_y(pieces):
    ways = (DOWN, UP, ACROSS)
    return [pieces[0]] + [lax.ppermute(piece, "y", way) for piece, way in zip(pieces[1:], ways)]


def ring_gather(piece, cut):
    below = lax.ppermute(piece, "y", UP)
    above = lax.ppermute(piece, "y", DOWN)
    first = lax.ppermute(below[:cut], "y", UP)
    second = lax.ppermute(above[cut:], "y", DOWN)
    return piece, below, above, first, second


def ring_scatter(pieces, cut):
    own, below, above, across_first, across_second = pieces
    first = lax.ppermute(across_first, "y", UP)
    second = lax.ppermute(across_second, "y", DOWN)
    up = jnp.concatenate(
        [(above[:cut].astype(F32) + first.astype(F32)).astype(BF), above[cut:]], axis=0
    )
    down = jnp.concatenate(
        [below[:cut], (below[cut:].astype(F32) + second.astype(F32)).astype(BF)], axis=0
    )
    from_below = lax.ppermute(up, "y", UP)
    from_above = lax.ppermute(down, "y", DOWN)
    total = own.astype(F32) + from_below.astype(F32) + from_above.astype(F32)
    return total, up


def mm(a, b):
    return lax.dot_general(a, b, (((1,), (0,)), ((), ())), preferred_element_type=F32)


def mm_tn(a, b):
    return lax.dot_general(a, b, (((0,), (0,)), ((), ())), preferred_element_type=F32)


def body(
    inputs, wqkv, wo, wr, gain_one, gain_two, rel_bias, w_in, w_out, routes, lengths, cotangent
):
    place = lax.axis_index("y")
    tokens = MB * TOK
    x_own = inputs.reshape(tokens, WIDTH)
    dy_own = cotangent.reshape(tokens, WIDTH)
    here = place[None].astype(jnp.int32)
    bounds = jnp.cumsum(lengths.reshape(MB, 3), axis=1)[:, :2].reshape(4)
    scalars = jnp.concatenate([here, bounds])
    x_pieces = gather_four(x_own, "y")
    bias_row = jnp.pad(rel_bias, (0, 3))[None]
    sides = vmem_call(
        prepare_kernel,
        [((6, 704), BF)] * 4,
        [],
        *(here, wqkv, wr, gain_one[None], gain_two[None], bias_row),
    )
    (pack,) = vmem_call(pack_kernel, [((24, 896), BF)], [], here, *exchange_y(sides), wo)
    packed = gather_four(jnp.concatenate(gather_four(pack, "x"), axis=0), "z")
    rows = jnp.arange(WIDTH, dtype=jnp.int32)
    step = rows // 24
    owner = owner_at(step // 4 % 4, "z") * 8 + owner_at(step % 4, "x") * 2
    owner = owner + (lax.axis_index("c") + step // 16) % 2
    in_chunk = rows % 24
    source = in_chunk // 6
    source = (place + jnp.where(source == 2, 3, jnp.where(source == 3, 2, source))) % NY
    nat_row = jnp.broadcast_to(((source * NEX + owner) * 6 + in_chunk % 6)[None], (8, WIDTH))
    wo_row = jnp.broadcast_to((owner * 24 + in_chunk)[None], (8, WIDTH))
    route = routes.reshape(MB, 2 * TOK)
    flat = jnp.arange(2 * TOK, dtype=jnp.int32)
    same = (route[:, :, None] == route[:, None, :]) & (flat[:, None] > flat[None, :])[None]
    slot = jnp.sum(same.astype(jnp.int32), axis=2)
    slot = (slot + jnp.arange(MB, dtype=jnp.int32)[:, None] * CAP).reshape(tokens, 2)
    route = route.reshape(tokens, 2)
    side = route % 2
    dest = (route // 2) * 16
    me = lax.axis_index(EX)
    info = jnp.concatenate(
        [dest + side * 6 + slot, dest + 12, side * 192 + me * 6 + slot, route], axis=1
    )
    buffer_rows = jnp.arange(512, dtype=jnp.int32)
    pick = [(buffer_rows[None, :] == info[:, k : k + 1]).astype(BF) for k in range(2)]
    slots = jnp.arange(400, dtype=jnp.int32)
    buffer_of = (slots // 6 % NEX) * 16 + (slots // 192) * 6 + slots % 6
    compact = jnp.where(
        slots[:, None] < 384,
        buffer_of[:, None] == buffer_rows[None, :],
        (buffer_rows % 16)[None, :] == 12 + slots[:, None] - 384,
    )
    compact = (compact & (slots < 386)[:, None]).astype(BF)

    def to_experts(buffer):
        return lax.all_to_all(buffer.reshape(NEX, 16, WIDTH), EX, 0, 0).reshape(512, WIDTH)

    dy_buffer = mm_tn(pick[0] + pick[1], dy_own).astype(BF)
    packed[3], nat_row, wo_row, info, scalars, dy_buffer, *x_pieces = lax.optimization_barrier(
        (packed[3], nat_row, wo_row, info, scalars, dy_buffer, *x_pieces)
    )
    packed = packed + [lax.ppermute(piece, "c", [(0, 1), (1, 0)]) for piece in packed]
    dy_buffer, *packed = lax.optimization_barrier((dy_buffer, *packed))
    dy_rows = mm(compact[:384], to_experts(dy_buffer))
    kept = attention_forward(scalars, nat_row, wo_row, x_pieces, packed)
    branch, saved, router, gain_rows = kept[:4], kept[4:10], kept[10], kept[11]
    weights = saved[3]
    branch = exchange_y(branch)
    dy_rows, *branch = lax.optimization_barrier((dy_rows.astype(BF), *branch))
    dy_rows = lax.all_gather(dy_rows, "y")
    middle, entering, gates, buffer = middle_step(
        scalars, branch, x_own, gain_rows, router, info
    )
    arrived = mm(compact, to_experts(buffer)).astype(BF)
    pulled, dy_all = vmem_call(
        pull_kernel, [((2, WIDTH, WIDTH), F32), ((2, WIDTH, WIDTH), BF)], [], here, dy_rows, w_out
    )
    results = expert_rows(scalars, ring_gather(arrived, 208), pulled, w_in)
    d_arrived, (rows_all, active, d_raised, gate_all) = results[:5], results[5:]
    d_home, in_flight = ring_scatter(d_arrived, 208)
    d_home_high = d_home.astype(BF)
    d_home_low = (d_home[384:385] - d_home_high[384:385].astype(F32)).astype(BF)
    d_home = jnp.where(
        (slots == 385)[:, None], d_home_low, d_home_high
    )
    back = to_experts(mm_tn(compact, d_home).astype(BF))
    active, _ = lax.optimization_barrier((active, in_flight))
    result = jnp.einsum("erf,efd->erd", active, w_out, preferred_element_type=F32).astype(BF)
    result = result.reshape(2, NY, 192, WIDTH).transpose(1, 0, 2, 3).reshape(NY, 384, WIDTH)
    result, _ = lax.optimization_barrier((result, d_home))
    result = lax.psum_scatter(result, "y", scatter_dimension=0)
    grad_in = jnp.einsum("erd,erf->edf", rows_all, d_raised, preferred_element_type=F32)
    back, grad_in = lax.optimization_barrier((back, grad_in))
    d_middle, d_branch, wr_grad, gain_two_grad = return_step(
        scalars, back, info, gates, entering, middle, gain_rows, router, dy_own
    )
    d_pieces = gather_four(d_branch, "y")
    back_result = mm_tn(compact[:384], result).astype(BF)
    back_result, *d_pieces = lax.optimization_barrier((back_result, *d_pieces))
    returned = to_experts(back_result)
    mixture = sum(gates[:, k : k + 1] * mm(pick[k], returned) for k in range(2))
    output = (middle + mixture).astype(BF)
    ended = attention_backward(
        scalars, d_pieces, saved, wr_grad, gain_two_grad
    )
    pieces = vmem_call(
        normed_kernel,
        [((128, WIDTH), BF)] * 4,
        [((MB * SPAN, WIDTH), F32)],
        *(scalars, ended[1], weights),
    )
    dy_all, _ = lax.optimization_barrier((dy_all, pieces[0]))
    d_returned = (dy_all.astype(F32) * gate_all[:, :, :1]).astype(BF)
    grad_out = jnp.einsum("erf,erd->efd", active, d_returned, preferred_element_type=F32)
    terms = lax.all_to_all(ended[0].reshape(NEX, 24, 896), EX, 0, 0)
    d_normed_pieces = exchange_y(pieces)
    shape = (6, 704)
    wo_out, *sums = vmem_call(
        sum_kernel, [((6, WIDTH), F32)] + [(shape, F32)] * 4, [], here, terms
    )
    d_normed_pieces[1], _ = lax.optimization_barrier((d_normed_pieces[1], sums[0]))
    d_normed = sum(piece.astype(F32) for piece in d_normed_pieces)
    x = x_own.astype(F32)
    scale = lax.rsqrt(jnp.mean(x * x, axis=1, keepdims=True) + 1e-06)
    scaled = d_normed * gain_rows[0:1]
    inner = jnp.mean(scaled * x, axis=1, keepdims=True)
    input_grad = d_middle + scale * scaled - x * scale**3 * inner
    wqkv_out, wr_out, one_out, two_out, bias_out = vmem_call(
        finish_kernel,
        [((6, 2304), F32), ((6, 64), F32), ((1, 6), F32), ((1, 6), F32), ((1, 3), F32)],
        [],
        here,
        *exchange_y(sums),
    )
    return (
        output.reshape(MB, 1, TOK, WIDTH),
        input_grad.reshape(MB, 1, TOK, WIDTH),
        wqkv_out,
        wo_out,
        wr_out,
        one_out[0],
        two_out[0],
        bias_out[0],
        grad_in,
        grad_out,
    )


def solution(mesh):
    grid = Mesh(mesh.devices.reshape(NY, 4, 4, 2), ("y", "z", "x", "c"))
    every = ("y",) + EX
    in_specs = (
        P(None, EX, "y", None),
        P(every, None),
        P(every, None),
        P(every, None),
        P(every),
        P(every),
        P(every),
        P(EX, None, "y"),
        P(EX, "y", None),
        P(None, EX, "y", None),
        P(None, EX, None),
        P(None, EX, "y", None),
    )
    out_specs = (
        P(None, EX, "y", None),
        P(None, EX, "y", None),
        P(every, None),
        P(every, None),
        P(every, None),
        P(every),
        P(every),
        P(every),
        P(EX, None, "y"),
        P(EX, "y", None),
    )
    return jax.shard_map(body, mesh=grid, in_specs=in_specs, out_specs=out_specs, check_vma=False)
```

```python
import functools
import math

import jax
import jax.numpy as jnp
from jax import lax
from jax.experimental import pallas as pl
from jax.experimental.pallas import tpu as pltpu
from jax.sharding import Mesh
from jax.sharding import PartitionSpec as P

HEADS = 12
HEAD_DIM = 64
BUCKETS = 32
CAP = 3
FAR_STEP = 6
WIDTH = 768
TOK = 64
MB = 2
NY = 4
NEX = 32
HG = HEADS // NY
SPAN = TOK * NY
SCORE_SCALE = 1.0 / math.sqrt(HEAD_DIM)
EX = ("z", "x", "c")
F32 = jnp.float32
BF = jnp.bfloat16
GELU_IN = math.sqrt(2.0 / math.pi)
GELU_CUBE = 0.044715

UP = [(i, (i + 1) % NY) for i in range(NY)]
DOWN = [(i, (i - 1) % NY) for i in range(NY)]
ACROSS = [(i, (i + 2) % NY) for i in range(NY)]


def dot(a, b, dims):
    return lax.dot_general(a, b, ((dims[:1], dims[1:]), ((), ())), preferred_element_type=F32)


def iota(shape, dim):
    return lax.broadcasted_iota(jnp.int32, shape, dim)


def bucket_of(gap):
    far = 16 + (jnp.maximum(gap - 16, 0) * 171) // 1024
    return jnp.where(gap < 16, gap, jnp.minimum(BUCKETS - 1, far))


def table_marks(place, head):
    shape = (WIDTH, SPAN)
    row = iota(shape, 0)
    owner = row // 6
    entry = 3 * (owner - NEX * place) + row - 6 * owner
    wanted = head * BUCKETS + bucket_of(iota(shape, 1))
    return jnp.where((row - 6 * owner < 3) & (entry == wanted), 1.0, 0.0).astype(BF)


def place_rows(pieces, place, target):
    for step, piece in zip((0, 3, 1, 2), pieces):
        start = lax.rem(place + step, NY) * TOK
        for m in range(MB):
            target[pl.ds(pl.multiple_of(m * SPAN + start, TOK), TOK), :] = piece[
                m * TOK : (m + 1) * TOK, :
            ]


def take_rows(pieces, place, source):
    for step, piece in zip((0, 3, 1, 2), pieces):
        start = lax.rem(place + step, NY) * TOK
        for m in range(MB):
            piece[m * TOK : (m + 1) * TOK, :] = source[
                pl.ds(pl.multiple_of(m * SPAN + start, TOK), TOK), :
            ].astype(piece.dtype)


def forward_kernel(
    scalars, nat_row, wo_row, x0, x1, x2, x3, q0, q1, q2, q3, q4, q5, q6, q7,
    b0, b1, b2, b3, qkv, probs, mixed, weights, wo_heads, normed, router, rows,
    x_all, bias, branch, packed,
):
    place = scalars[0]
    place_rows((x0, x1, x2, x3), place, x_all)
    for spot, piece in enumerate((q0, q1, q2, q3, q4, q5, q6, q7)):
        packed[spot * 96 : spot * 96 + 96, :] = piece[...]
    row = iota((WIDTH, WIDTH), 0)
    perm = jnp.where(row == nat_row[0:1, :], 1.0, 0.0).astype(BF)
    weights[...] = dot(perm, packed[:, :704], (1, 0)).astype(BF)
    router[...] = weights[:, 576:704]
    for part in range(4):
        choose = jnp.where(iota((192, WIDTH), 0) * 4 + part == wo_row[0:1, :], 1.0, 0.0).astype(BF)
        wo_heads[:, part * 192 : part * 192 + 192] = dot(
            choose, packed[:, 704:896], (1, 0)
        ).astype(BF)
    lane_of = jnp.where(iota((8, 128), 1) == iota((8, 128), 0) + 64, 1.0, 0.0).astype(BF)
    rows[...] = dot(lane_of, weights[:, 576:704], (1, 1))
    values = x_all[...].astype(F32)
    scale = lax.rsqrt(jnp.mean(values * values, axis=1, keepdims=True) + 1e-06)
    normed[...] = (values * scale * rows[0:1, :]).astype(BF)
    qkv[...] = dot(normed[...], weights[:, :576], (1, 0)).astype(BF)
    table = rows[...].astype(BF)
    for head in range(HG):
        mirrored = dot(table, table_marks(place, head), (1, 0))[2:3, :]
        flip = jnp.where(iota((SPAN, SPAN), 0) + iota((SPAN, SPAN), 1) == SPAN - 1, 1.0, 0.0)
        mirrored = dot(jnp.broadcast_to(mirrored, (8, SPAN)).astype(BF), flip.astype(BF), (1, 0))
        spread = jnp.broadcast_to(mirrored[0:1, :], (SPAN, SPAN))
        bias[head] = pltpu.roll(spread, 1, 1, stride=1, stride_axis=0)
    query = iota((SPAN, SPAN), 0)
    key = iota((SPAN, SPAN), 1)
    for m in range(MB):
        first = scalars[1 + 2 * m]
        second = scalars[2 + 2 * m]
        of_query = jnp.where(query >= first, 1, 0) + jnp.where(query >= second, 1, 0)
        of_key = jnp.where(key >= first, 1, 0) + jnp.where(key >= second, 1, 0)
        seen = (of_query == of_key) & (query >= key)
        part = slice(m * SPAN, (m + 1) * SPAN)
        for head in range(HG):
            at = head * HEAD_DIM
            raw = dot(
                qkv[part, at : at + HEAD_DIM], qkv[part, 192 + at : 192 + at + HEAD_DIM], (1, 1)
            )
            scores = jnp.where(seen, raw * SCORE_SCALE + bias[head], -1000000000.0)
            peak = jnp.max(scores, axis=1, keepdims=True)
            powers = jnp.exp(scores - peak)
            share = powers / jnp.sum(powers, axis=1, keepdims=True)
            probs[m * HG + head] = share
            mixed[part, at : at + HEAD_DIM] = dot(
                share.astype(BF), qkv[part, 384 + at : 384 + at + HEAD_DIM], (1, 0)
            ).astype(BF)
    branch[...] = dot(mixed[...], wo_heads[...], (1, 0))
    take_rows((b0, b1, b2, b3), place, branch)


def backward_kernel(
    scalars, d0, d1, d2, d3, qkv, probs, mixed, weights, wo_heads, normed, wr_grad, gain_two,
    grads, d_qkv, d_branch, d_mixed, d_bias,
):
    place = scalars[0]
    place_rows((d0, d1, d2, d3), place, d_branch)
    grad_wo = dot(mixed[...], d_branch[...], (0, 0)).astype(BF)
    packed_wo = jnp.zeros((WIDTH, 192), F32)
    for part in range(4):
        choose = jnp.where(iota((WIDTH, 192), 1) * 4 + part == iota((WIDTH, 192), 0), 1.0, 0.0)
        packed_wo = packed_wo + dot(
            choose.astype(BF), grad_wo[:, part * 192 : part * 192 + 192], (1, 0)
        )
    grads[:, 704:896] = packed_wo.astype(BF)
    d_mixed[...] = dot(d_branch[...], wo_heads[...], (1, 1)).astype(BF)
    for m in range(MB):
        part = slice(m * SPAN, (m + 1) * SPAN)
        for head in range(HG):
            at = head * HEAD_DIM
            lanes = slice(at, at + HEAD_DIM)
            share = probs[m * HG + head]
            d_mixed_head = d_mixed[part, lanes]
            d_probs = dot(d_mixed_head, qkv[part, 384 + at : 384 + at + HEAD_DIM], (1, 1))
            d_qkv[part, 384 + at : 384 + at + HEAD_DIM] = dot(
                share.astype(BF), d_mixed_head, (0, 0)
            ).astype(BF)
            inner = jnp.sum(share * d_probs, axis=1, keepdims=True)
            d_scores = share * (d_probs - inner)
            if m == 0:
                d_bias[head] = d_scores
            else:
                d_bias[head] = d_bias[head] + d_scores
            d_raw = (d_scores * SCORE_SCALE).astype(BF)
            d_qkv[part, lanes] = dot(
                d_raw, qkv[part, 192 + at : 192 + at + HEAD_DIM], (1, 0)
            ).astype(BF)
            d_qkv[part, 192 + at : 192 + at + HEAD_DIM] = dot(
                d_raw, qkv[part, lanes], (0, 0)
            ).astype(BF)
    flip = jnp.where(iota((SPAN, SPAN), 0) + iota((SPAN, SPAN), 1) == SPAN - 1, 1.0, 0.0).astype(BF)
    table = jnp.zeros((8, WIDTH), F32)
    for head in range(HG):
        total = d_bias[head]
        high = total.astype(BF)
        low = (total - high.astype(F32)).astype(BF)
        turned = dot(flip, high, (1, 0)) + dot(flip, low, (1, 0))
        skewed = pltpu.roll(turned, 0, 1, stride=1, stride_axis=0)
        diagonal = jnp.broadcast_to(jnp.sum(skewed, axis=0, keepdims=True), (8, SPAN))
        high = diagonal.astype(BF)
        low = (diagonal - high.astype(F32)).astype(BF)
        by_gap = dot(high, flip, (1, 0)) + dot(low, flip, (1, 0))
        marks = table_marks(place, head)
        high = by_gap.astype(BF)
        low = (by_gap - high.astype(F32)).astype(BF)
        table = table + dot(high, marks, (1, 1)) + dot(low, marks, (1, 1))
    which = iota((8, WIDTH), 0)
    rows = jnp.where(which == 1, gain_two[0:1, :], jnp.where(which == 2, table, 0.0))
    lane_of = jnp.where(iota((8, 128), 1) == iota((8, 128), 0) + 64, 1.0, 0.0).astype(BF)
    grad_heads = dot(normed[...], d_qkv[...], (0, 0))
    gain_one = jnp.sum(grad_heads * weights[:, :576].astype(F32), axis=1, keepdims=True)
    gain_one = gain_one / weights[:, 640:641].astype(F32)
    small = wr_grad[...] + dot(rows.astype(BF), lane_of, (0, 0))
    small = small + jnp.where(iota((WIDTH, 128), 1) == 64, gain_one, 0.0)
    row = iota((WIDTH, WIDTH), 0)
    col = iota((WIDTH, WIDTH), 1)
    chunk = row // 24
    rest = row - 24 * chunk
    group = rest // 6
    wanted = (group * NEX + chunk) * 6 + rest - 6 * group
    perm = jnp.where(col == wanted, 1.0, 0.0).astype(BF)
    grads[:, :576] = dot(perm, grad_heads.astype(BF), (1, 0)).astype(BF)
    grads[:, 576:704] = dot(perm, small.astype(BF), (1, 0)).astype(BF)


def normed_kernel(scalars, d_qkv, weights, n0, n1, n2, n3, d_normed):
    d_normed[...] = dot(d_qkv[...], weights[:, :576], (1, 1))
    take_rows((n0, n1, n2, n3), scalars[0], d_normed)


def vmem_call(kernel, outs, scratch, *args, grant=60):
    full = pl.BlockSpec()
    return pl.pallas_call(
        kernel,
        out_shape=[jax.ShapeDtypeStruct(shape, kind) for shape, kind in outs],
        in_specs=[pl.BlockSpec(memory_space=pltpu.SMEM)] + [full] * (len(args) - 1),
        out_specs=[full] * len(outs),
        scratch_shapes=[pltpu.VMEM(shape, kind) for shape, kind in scratch],
        compiler_params=pltpu.CompilerParams(vmem_limit_bytes=grant * 1024 * 1024),
    )(*args)


def attention_forward(scalars, nat_row, wo_row, x_pieces, packed):
    rows = MB * SPAN
    outs = [((128, WIDTH), BF)] * 4 + [
        ((rows, 576), BF),
        ((MB * HG, SPAN, SPAN), F32),
        ((rows, 192), BF),
        ((WIDTH, 704), BF),
        ((192, WIDTH), BF),
        ((rows, WIDTH), BF),
        ((WIDTH, 128), BF),
        ((8, WIDTH), F32),
    ]
    scratch = [((rows, WIDTH), BF), ((HG, SPAN, SPAN), F32), ((rows, WIDTH), F32), ((WIDTH, 896), BF)]
    return vmem_call(forward_kernel, outs, scratch, scalars, nat_row, wo_row, *x_pieces, *packed)


def attention_backward(scalars, d_pieces, kept, wr_grad, gain_two):
    rows = MB * SPAN
    outs = [((WIDTH, 896), BF), ((rows, 576), BF)]
    scratch = [((rows, WIDTH), BF), ((rows, 192), BF), ((HG, SPAN, SPAN), F32)]
    return vmem_call(backward_kernel, outs, scratch, scalars, *d_pieces, *kept, wr_grad, gain_two)


def middle_kernel(
    scalars, b0, b1, b2, b3, x_own, rows, router, info, middle, entering, gates, buffer
):
    values = x_own[...].astype(F32) + (
        (b0[...].astype(F32) + b1[...].astype(F32)) + (b2[...].astype(F32) + b3[...].astype(F32))
    )
    middle[...] = values
    scale = lax.rsqrt(jnp.mean(values * values, axis=1, keepdims=True) + 1e-06)
    low = (values * scale * rows[1:2, :]).astype(BF)
    entering[...] = low
    logits = dot(low, router[...], (1, 0))
    lane = iota((128, 128), 1)
    chosen = [
        jnp.sum(jnp.where(lane == info[:, 6 + k : 7 + k], logits, 0.0), axis=1, keepdims=True)
        for k in range(2)
    ]
    peak = jnp.maximum(chosen[0], chosen[1])
    powers = [jnp.exp(value - peak) for value in chosen]
    total = powers[0] + powers[1]
    share = [power / total for power in powers]
    gates[...] = jnp.where(lane == 0, share[0], jnp.where(lane == 1, share[1], 0.0))
    place = iota((128, 512), 1)
    wide = iota((128, WIDTH), 1)
    pick = jnp.where(
        (place == info[:, 0:1]) | (place == info[:, 1:2]), 1.0, 0.0
    ).astype(BF)
    sent = dot(pick, low, (0, 0))
    for k in range(2):
        mark = wide == info[:, 4 + k : 5 + k]
        high = share[k].astype(BF).astype(F32)
        rest = share[k] - high
        for at, value in ((0, high), (1, rest)):
            spot = jnp.where(place == info[:, 2 + k : 3 + k] + at, 1.0, 0.0).astype(BF)
            sent = sent + dot(spot, jnp.where(mark, value, 0.0).astype(BF), (0, 0))
    buffer[...] = sent.astype(BF)


def return_kernel(
    scalars, back, info, gates, entering, middle, rows, router, dy_own,
    d_middle, d_branch, wr_grad, gain_two,
):
    place = iota((128, 512), 1)
    wide = iota((128, WIDTH), 1)
    lane = iota((128, 128), 1)
    share = [gates[:, k : k + 1] for k in range(2)]
    d_entering = jnp.zeros((128, WIDTH), F32)
    d_gates = []
    for k in range(2):
        pick = jnp.where(place == info[:, k : k + 1], 1.0, 0.0).astype(BF)
        d_entering = d_entering + share[k] * dot(pick, back[...], (1, 0))
        at = info[:, 2 + k : 3 + k]
        spot = jnp.where((place == at) | (place == at + 1), 1.0, 0.0).astype(BF)
        d_gates.append(
            jnp.sum(
                jnp.where(wide == info[:, 4 + k : 5 + k], dot(spot, back[...], (1, 0)), 0.0),
                axis=1,
                keepdims=True,
            )
        )
    inner = share[0] * d_gates[0] + share[1] * d_gates[1]
    d_logits = jnp.zeros((128, 128), F32)
    for k in range(2):
        d_logits = d_logits + jnp.where(
            lane == info[:, 6 + k : 7 + k], share[k] * (d_gates[k] - inner), 0.0
        )
    d_logits = d_logits.astype(BF)
    d_entering = d_entering + dot(d_logits, router[...], (1, 1))
    wr_grad[...] = dot(entering[...], d_logits, (0, 0))
    values = middle[...]
    scale = lax.rsqrt(jnp.mean(values * values, axis=1, keepdims=True) + 1e-06)
    gain_two[...] = jnp.broadcast_to(
        jnp.sum(d_entering * values * scale, axis=0, keepdims=True), (8, WIDTH)
    )
    scaled = d_entering * rows[1:2, :]
    mean = jnp.mean(scaled * values, axis=1, keepdims=True)
    total = dy_own[...].astype(F32) + scale * scaled - values * scale * scale * scale * mean
    d_middle[...] = total
    d_branch[...] = total.astype(BF)


def gelu_parts(value):
    square = value * value
    bend = jnp.tanh(value * (GELU_IN + (GELU_IN * GELU_CUBE) * square))
    half = 0.5 + 0.5 * bend
    rise = value * (0.5 * GELU_IN + (1.5 * GELU_IN * GELU_CUBE) * square)
    return value * half, half + rise * (1.0 - bend * bend)


def pull_kernel(scalars, dy_rows, w_out, pulled, dy_all):
    tall = NEX * 6
    for n in range(2):
        for owner in range(NY):
            dy_all[n, owner * tall : owner * tall + tall, :] = dy_rows[
                owner, n * tall : n * tall + tall, :
            ]
        pulled[n] = dot(dy_all[n], w_out[n], (1, 1))


def expert_kernel(
    scalars, p0, p1, p2, p3a, p3b, pulled, w_in,
    o0, o1, o2, o3a, o3b, rows_all, active_all, d_raised_all, gate_all,
    rows, raised, d_raised,
):
    place = scalars[0]
    tall = NEX * 6
    wide_ones = jnp.ones((tall, 128), BF)
    extra_row = iota((16, tall), 0)
    eye = iota((tall, tall), 0) == iota((tall, tall), 1)
    starts = [
        pl.multiple_of(lax.rem(place + step, NY) * tall, tall) for step in (0, 3, 1, 2)
    ]

    def expert(n):
        part = slice(n * tall, n * tall + tall)
        for spot in range(4):
            here = slice(spot * tall, spot * tall + tall)
            if spot < 3:
                rows[here, :] = (p0, p1, p2)[spot][part, :]
            elif n == 0:
                rows[here, :] = p3a[0:tall, :]
            else:
                rows[spot * tall : spot * tall + 16, :] = p3a[tall : tall + 16, :]
                rows[spot * tall + 16 : spot * tall + tall, :] = p3b[0 : tall - 16, :]
            rows_all[0, pl.ds(starts[spot], tall), :] = rows[here, :]
        raised[...] = dot(rows[...], w_in[0], (1, 0))
        for spot in range(4):
            here = slice(spot * tall, spot * tall + tall)
            there = pl.ds(starts[spot], tall)
            gate = p3b[tall - 16 : tall, part] if spot == 3 else (p0, p1, p2)[spot][384:400, part]
            gate = gate.astype(F32)
            gate_col = dot(jnp.where(eye, gate[0:1, :], 0.0).astype(BF), wide_ones, (1, 0))
            gate_col = gate_col + dot(
                jnp.where(eye, gate[1:2, :], 0.0).astype(BF), wide_ones, (1, 0)
            )
            gate_all[0, there, :] = gate_col
            active, slope = gelu_parts(raised[here, :])
            active = active.astype(BF)
            active_all[0, there, :] = active
            pull = pulled[0, there, :]
            product = active.astype(F32) * pull
            change = slope * pull
            d_raised[here, :] = change.astype(BF)
            d_raised_all[0, there, :] = (change * gate_col[:, 0:1]).astype(BF)
            d_gate = jnp.sum(product, axis=1, keepdims=True)
            d_gate = jnp.sum(jnp.where(eye, d_gate, 0.0), axis=0, keepdims=True)
            tail = (o0, o1, o2, o3b)[spot]
            last = tail.shape[0] - 16
            if n == 0:
                tail[last:, 384:WIDTH] = jnp.zeros((16, WIDTH - 384), BF)
            tail[last:, part] = jnp.where(extra_row == 0, d_gate, 0.0).astype(BF)
        raised[...] = dot(d_raised[...], w_in[0], (1, 1))
        for spot in range(3):
            (o0, o1, o2)[spot][part, :] = raised[spot * tall : spot * tall + tall, :].astype(BF)
        final = raised[3 * tall : 4 * tall, :].astype(BF)
        if n == 0:
            o3a[0:tall, :] = final
        else:
            o3a[tall : tall + 16, :] = final[0:16, :]
            o3b[0 : tall - 16, :] = final[16:tall, :]

    for n in range(2):
        pl.when(pl.program_id(0) == n)(functools.partial(expert, n))


def expert_rows(scalars, pieces, pulled, w_in):
    square = ((2, WIDTH, WIDTH), BF)
    outs = [((400, WIDTH), BF)] * 3 + [((208, WIDTH), BF), ((192, WIDTH), BF)]
    outs = outs + [square] * 3 + [((2, WIDTH, 128), F32)]
    whole = (WIDTH, WIDTH)

    def spec(shape):
        if len(shape) == 3:
            return pl.BlockSpec((1,) + shape[1:], lambda n: (n, 0, 0))
        return pl.BlockSpec(shape, lambda n: (0, 0))

    args = (*pieces, pulled, w_in)
    return pl.pallas_call(
        expert_kernel,
        grid=(2,),
        out_shape=[jax.ShapeDtypeStruct(shape, kind) for shape, kind in outs],
        in_specs=[pl.BlockSpec(memory_space=pltpu.SMEM)] + [spec(arg.shape) for arg in args],
        out_specs=[spec(shape) for shape, _ in outs],
        scratch_shapes=[pltpu.VMEM(whole, BF), pltpu.VMEM(whole, F32), pltpu.VMEM(whole, BF)],
        compiler_params=pltpu.CompilerParams(vmem_limit_bytes=60 * 1024 * 1024),
    )(scalars, *args)


def prepare_kernel(scalars, wqkv, wr, gain_one, gain_two, rel_bias, o0, o1, o2, o3):
    place = scalars[0]
    lane = iota((6, 128), 1)
    own = iota((6, 6), 0) == iota((6, 6), 1)
    one = jnp.sum(jnp.where(own, gain_one[...].astype(F32), 0.0), axis=1, keepdims=True)
    two = jnp.sum(jnp.where(own, gain_two[...].astype(F32), 0.0), axis=1, keepdims=True)
    bias = jnp.sum(jnp.where(own, rel_bias[...].astype(F32), 0.0), axis=1, keepdims=True)
    small = jnp.concatenate([wr[...].astype(F32), jnp.zeros((6, 64), F32)], axis=1)
    small = jnp.where(
        lane == 64, one, jnp.where(lane == 65, two, jnp.where(lane == 66, bias, small))
    ).astype(BF)
    values = wqkv[...].astype(F32)
    for step, out in zip((0, 3, 1, 2), (o0, o1, o2, o3)):
        owner = lax.rem(place + step, NY)
        out[:, 576:704] = small
        for part in range(3):
            taken = jnp.zeros((6, 192), F32)
            for group in range(NY):
                at = part * WIDTH + group * 192
                taken = taken + jnp.where(owner == group, 1.0, 0.0) * values[:, at : at + 192]
            out[:, part * 192 : part * 192 + 192] = taken.astype(BF)


def pack_kernel(scalars, p0, p1, p2, p3, wo, out):
    row = iota((24, 6), 0)
    col = iota((24, 6), 1)
    total = jnp.zeros((24, 704), F32)
    for spot, piece in enumerate((p0, p1, p2, p3)):
        total = total + dot(jnp.where(row == spot * 6 + col, 1.0, 0.0).astype(BF), piece[...], (1, 0))
    out[:, :704] = total.astype(BF)
    total = jnp.zeros((24, 192), F32)
    for part in range(4):
        spot = jnp.where(row == col * 4 + part, 1.0, 0.0).astype(BF)
        total = total + dot(spot, wo[:, part * 192 : part * 192 + 192], (1, 0))
    out[:, 704:896] = total.astype(BF)


def sum_kernel(scalars, terms, wo_out, o0, o1, o2, o3):
    place = scalars[0]
    total = jnp.sum(terms[...].astype(F32), axis=0)
    for part in range(4):
        spot = jnp.where(iota((6, 24), 1) == iota((6, 24), 0) * 4 + part, 1.0, 0.0)
        wo_out[:, part * 192 : part * 192 + 192] = lax.dot_general(
            spot,
            total[:, 704:896],
            (((1,), (0,)), ((), ())),
            precision=lax.Precision.HIGHEST,
            preferred_element_type=F32,
        )
    for step, out in zip((0, 3, 1, 2), (o0, o1, o2, o3)):
        owner = lax.rem(place + step, NY)
        taken = jnp.zeros((6, 704), F32)
        for group in range(NY):
            taken = taken + jnp.where(owner == group, 1.0, 0.0) * total[
                group * 6 : group * 6 + 6, :704
            ]
        out[...] = taken


def finish_kernel(scalars, p0, p1, p2, p3, wqkv_out, wr_out, one_out, two_out, bias_out):
    place = scalars[0]
    pieces = (p0, p1, p2, p3)
    for part in range(3):
        for group in range(NY):
            taken = jnp.zeros((6, 192), F32)
            for step, piece in zip((0, 1, 3, 2), pieces):
                owner = lax.rem(place + step, NY)
                taken = taken + jnp.where(owner == group, 1.0, 0.0) * piece[
                    :, part * 192 : part * 192 + 192
                ]
            at = part * WIDTH + group * 192
            wqkv_out[:, at : at + 192] = taken
    small = p0[:, 576:704] + p1[:, 576:704] + p2[:, 576:704] + p3[:, 576:704]
    wr_out[...] = small[:, :64]
    for lane, out in ((64, one_out), (65, two_out), (66, bias_out)):
        shape = (6, out.shape[1])
        mark = iota(shape, 0) == iota(shape, 1)
        out[...] = jnp.sum(
            jnp.where(mark, small[:, lane : lane + 1], 0.0), axis=0, keepdims=True
        )


def middle_step(scalars, pieces, x_own, rows, weights, info):
    outs = [((128, WIDTH), F32), ((128, WIDTH), BF), ((128, 128), F32), ((512, WIDTH), BF)]
    return vmem_call(middle_kernel, outs, [], scalars, *pieces, x_own, rows, weights, info, grant=20)


def return_step(scalars, back, info, gates, entering, middle, rows, weights, dy_own):
    outs = [((128, WIDTH), F32), ((128, WIDTH), BF), ((WIDTH, 128), F32), ((8, WIDTH), F32)]
    return vmem_call(
        return_kernel, outs, [], scalars, back, info, gates, entering, middle, rows, weights, dy_own,
        grant=20,
    )


def gather_four(piece, axis):
    return [piece] + [lax.ppermute(piece, axis, way) for way in (UP, DOWN, ACROSS)]


def owner_at(step, axis):
    shift = jnp.where(step == 1, 3, jnp.where(step == 2, 1, jnp.where(step == 3, 2, 0)))
    return (lax.axis_index(axis) + shift) % 4


def exchange_y(pieces):
    ways = (DOWN, UP, ACROSS)
    return [pieces[0]] + [lax.ppermute(piece, "y", way) for piece, way in zip(pieces[1:], ways)]


def ring_gather(piece, cut, ready):
    below = lax.ppermute(piece, "y", UP)
    above = lax.ppermute(piece, "y", DOWN)
    below, above, ready = lax.optimization_barrier((below, above, ready))
    first = lax.ppermute(below[:cut], "y", UP)
    second = lax.ppermute(above[cut:], "y", DOWN)
    return (piece, below, above, first, second), ready


def ring_scatter(pieces, cut):
    own, below, above, across_first, across_second = pieces
    first = lax.ppermute(across_first, "y", UP)
    second = lax.ppermute(across_second, "y", DOWN)
    up = jnp.concatenate(
        [(above[:cut].astype(F32) + first.astype(F32)).astype(BF), above[cut:]], axis=0
    )
    down = jnp.concatenate(
        [below[:cut], (below[cut:].astype(F32) + second.astype(F32)).astype(BF)], axis=0
    )
    from_below = lax.ppermute(up, "y", UP)
    from_above = lax.ppermute(down, "y", DOWN)
    total = own.astype(F32) + from_below.astype(F32) + from_above.astype(F32)
    return total, up


def mm(a, b):
    return lax.dot_general(a, b, (((1,), (0,)), ((), ())), preferred_element_type=F32)


def mm_tn(a, b):
    return lax.dot_general(a, b, (((0,), (0,)), ((), ())), preferred_element_type=F32)


def body(
    inputs, wqkv, wo, wr, gain_one, gain_two, rel_bias, w_in, w_out, routes, lengths, cotangent
):
    place = lax.axis_index("y")
    tokens = MB * TOK
    x_own = inputs.reshape(tokens, WIDTH)
    dy_own = cotangent.reshape(tokens, WIDTH)
    here = place[None].astype(jnp.int32)
    bounds = jnp.cumsum(lengths.reshape(MB, 3), axis=1)[:, :2].reshape(4)
    scalars = jnp.concatenate([here, bounds])
    x_pieces = gather_four(x_own, "y")
    bias_row = jnp.pad(rel_bias, (0, 3))[None]
    sides = vmem_call(
        prepare_kernel,
        [((6, 704), BF)] * 4,
        [],
        *(here, wqkv, wr, gain_one[None], gain_two[None], bias_row),
    )
    (pack,) = vmem_call(pack_kernel, [((24, 896), BF)], [], here, *exchange_y(sides), wo)
    packed = gather_four(jnp.concatenate(gather_four(pack, "x"), axis=0), "z")
    rows = jnp.arange(WIDTH, dtype=jnp.int32)
    step = rows // 24
    owner = owner_at(step // 4 % 4, "z") * 8 + owner_at(step % 4, "x") * 2
    owner = owner + (lax.axis_index("c") + step // 16) % 2
    in_chunk = rows % 24
    source = in_chunk // 6
    source = (place + jnp.where(source == 2, 3, jnp.where(source == 3, 2, source))) % NY
    nat_row = jnp.broadcast_to(((source * NEX + owner) * 6 + in_chunk % 6)[None], (8, WIDTH))
    wo_row = jnp.broadcast_to((owner * 24 + in_chunk)[None], (8, WIDTH))
    route = routes.reshape(MB, 2 * TOK)
    flat = jnp.arange(2 * TOK, dtype=jnp.int32)
    same = (route[:, :, None] == route[:, None, :]) & (flat[:, None] > flat[None, :])[None]
    slot = jnp.sum(same.astype(jnp.int32), axis=2)
    slot = (slot + jnp.arange(MB, dtype=jnp.int32)[:, None] * CAP).reshape(tokens, 2)
    route = route.reshape(tokens, 2)
    side = route % 2
    dest = (route // 2) * 16
    me = lax.axis_index(EX)
    info = jnp.concatenate(
        [dest + side * 6 + slot, dest + 12, side * 192 + me * 6 + slot, route], axis=1
    )
    buffer_rows = jnp.arange(512, dtype=jnp.int32)
    pick = [(buffer_rows[None, :] == info[:, k : k + 1]).astype(BF) for k in range(2)]
    slots = jnp.arange(400, dtype=jnp.int32)
    buffer_of = (slots // 6 % NEX) * 16 + (slots // 192) * 6 + slots % 6
    compact = jnp.where(
        slots[:, None] < 384,
        buffer_of[:, None] == buffer_rows[None, :],
        (buffer_rows % 16)[None, :] == 12 + slots[:, None] - 384,
    )
    compact = (compact & (slots < 386)[:, None]).astype(BF)

    def to_experts(buffer):
        return lax.all_to_all(buffer.reshape(NEX, 16, WIDTH), EX, 0, 0).reshape(512, WIDTH)

    dy_buffer = mm_tn(pick[0] + pick[1], dy_own).astype(BF)
    packed[3], nat_row, wo_row, info, scalars, dy_buffer, *x_pieces = lax.optimization_barrier(
        (packed[3], nat_row, wo_row, info, scalars, dy_buffer, *x_pieces)
    )
    packed = packed + [lax.ppermute(piece, "c", [(0, 1), (1, 0)]) for piece in packed]
    dy_buffer, *packed = lax.optimization_barrier((dy_buffer, *packed))
    dy_rows = mm(compact[:384], to_experts(dy_buffer))
    kept = attention_forward(scalars, nat_row, wo_row, x_pieces, packed)
    branch, saved, router, gain_rows = kept[:4], kept[4:10], kept[10], kept[11]
    weights = saved[3]
    branch = exchange_y(branch)
    dy_rows, *branch = lax.optimization_barrier((dy_rows.astype(BF), *branch))
    dy_rows = lax.all_gather(dy_rows, "y")
    middle, entering, gates, buffer = middle_step(
        scalars, branch, x_own, gain_rows, router, info
    )
    arrived = mm(compact, to_experts(buffer)).astype(BF)
    pulled, dy_all = vmem_call(
        pull_kernel, [((2, WIDTH, WIDTH), F32), ((2, WIDTH, WIDTH), BF)], [], here, dy_rows, w_out
    )
    arrived, pulled = ring_gather(arrived, 208, pulled)
    results = expert_rows(scalars, arrived, pulled, w_in)
    d_arrived, (rows_all, active, d_raised, gate_all) = results[:5], results[5:]
    d_home, in_flight = ring_scatter(d_arrived, 208)
    d_home_high = d_home.astype(BF)
    d_home_low = (d_home[384:385] - d_home_high[384:385].astype(F32)).astype(BF)
    d_home = jnp.where(
        (slots == 385)[:, None], d_home_low, d_home_high
    )
    back = to_experts(mm_tn(compact, d_home).astype(BF))
    active, _ = lax.optimization_barrier((active, in_flight))
    result = jnp.einsum("erf,efd->erd", active, w_out, preferred_element_type=F32).astype(BF)
    result = result.reshape(2, NY, 192, WIDTH).transpose(1, 0, 2, 3).reshape(NY, 384, WIDTH)
    result, _ = lax.optimization_barrier((result, d_home))
    result = lax.psum_scatter(result, "y", scatter_dimension=0)
    grad_in = jnp.einsum("erd,erf->edf", rows_all, d_raised, preferred_element_type=F32)
    back, grad_in = lax.optimization_barrier((back, grad_in))
    d_middle, d_branch, wr_grad, gain_two_grad = return_step(
        scalars, back, info, gates, entering, middle, gain_rows, router, dy_own
    )
    d_pieces = gather_four(d_branch, "y")
    back_result = mm_tn(compact[:384], result).astype(BF)
    back_result, *d_pieces = lax.optimization_barrier((back_result, *d_pieces))
    returned = to_experts(back_result)
    mixture = sum(gates[:, k : k + 1] * mm(pick[k], returned) for k in range(2))
    output = (middle + mixture).astype(BF)
    ended = attention_backward(
        scalars, d_pieces, saved, wr_grad, gain_two_grad
    )
    pieces = vmem_call(
        normed_kernel,
        [((128, WIDTH), BF)] * 4,
        [((MB * SPAN, WIDTH), F32)],
        *(scalars, ended[1], weights),
    )
    dy_all, _ = lax.optimization_barrier((dy_all, pieces[0]))
    d_returned = (dy_all.astype(F32) * gate_all[:, :, :1]).astype(BF)
    grad_out = jnp.einsum("erf,erd->efd", active, d_returned, preferred_element_type=F32)
    terms = lax.all_to_all(ended[0].reshape(NEX, 24, 896), EX, 0, 0)
    d_normed_pieces = exchange_y(pieces)
    shape = (6, 704)
    wo_out, *sums = vmem_call(
        sum_kernel, [((6, WIDTH), F32)] + [(shape, F32)] * 4, [], here, terms
    )
    d_normed_pieces[1], _ = lax.optimization_barrier((d_normed_pieces[1], sums[0]))
    d_normed = sum(piece.astype(F32) for piece in d_normed_pieces)
    x = x_own.astype(F32)
    scale = lax.rsqrt(jnp.mean(x * x, axis=1, keepdims=True) + 1e-06)
    scaled = d_normed * gain_rows[0:1]
    inner = jnp.mean(scaled * x, axis=1, keepdims=True)
    input_grad = d_middle + scale * scaled - x * scale**3 * inner
    wqkv_out, wr_out, one_out, two_out, bias_out = vmem_call(
        finish_kernel,
        [((6, 2304), F32), ((6, 64), F32), ((1, 6), F32), ((1, 6), F32), ((1, 3), F32)],
        [],
        here,
        *exchange_y(sums),
    )
    return (
        output.reshape(MB, 1, TOK, WIDTH),
        input_grad.reshape(MB, 1, TOK, WIDTH),
        wqkv_out,
        wo_out,
        wr_out,
        one_out[0],
        two_out[0],
        bias_out[0],
        grad_in,
        grad_out,
    )


def solution(mesh):
    grid = Mesh(mesh.devices.reshape(NY, 4, 4, 2), ("y", "z", "x", "c"))
    every = ("y",) + EX
    in_specs = (
        P(None, EX, "y", None),
        P(every, None),
        P(every, None),
        P(every, None),
        P(every),
        P(every),
        P(every),
        P(EX, None, "y"),
        P(EX, "y", None),
        P(None, EX, "y", None),
        P(None, EX, None),
        P(None, EX, "y", None),
    )
    out_specs = (
        P(None, EX, "y", None),
        P(None, EX, "y", None),
        P(every, None),
        P(every, None),
        P(every, None),
        P(every),
        P(every),
        P(every),
        P(EX, None, "y"),
        P(EX, "y", None),
    )
    return jax.shard_map(body, mesh=grid, in_specs=in_specs, out_specs=out_specs, check_vma=False)
```
